32 devices in a mesh: grp: 8 (over z, y), sub: 4 (over x, core).
Axes of the slice: x: 2, y: 2, z: 4, core: 2. Of those that a mesh axis runs over, the one named last changes fastest.
Arguments:
- adj_next: float32 [8, 128, 128, 128], P('grp', 'sub'), may hold values from -4.5 to 4.5
- adj_later: float32 [8, 128, 128, 128], P('grp', 'sub'), may hold values from -2.25 to 2.25
- box_sizes: int32 [8, 2], replicated, may hold values from 64 to 128, as said below
- holder: int32 [8], replicated, may hold values from 0 to 7, as said below
- partner: int32 [8, 2, 4], replicated, may hold values from -1 to 31, as said below
Outputs:
- adj_now: float32 [8, 128, 128, 128], P('grp', 'sub')
- adj_earlier: float32 [8, 128, 128, 128], P('grp', 'sub')
The draws below stay inside these ranges and needn't reach their ends.
Inputs may be any that keep to these rules, and one draw needn't show every extreme that they name: box_sizes[p] = (Lx, Ly) with 64 <= Lx <= 128 and 64 <= Ly <= 128; some partition has Lx = 128 and Ly = 128, some has Lx = 64, some has Ly = 64. holder names every slot exactly once. The joining is mutual: if partner[p, f, s] = q * 4 + t then partner[q, 1 - f, t] = p * 4 + s, and q differs from p. A face may be joined in part and walled in part; some faces are wholly walls. Over both faces, a partition has at most 3 segments joined to any one other partition, and some pair of partitions has exactly 3.
All inputs are finite; a program needn't handle non-finite values.
Results may differ from the reference program's by a relative error of at most 0.0003.
Values sent between devices are 32-bit elements; how exact they have to be, the bound alone decides.
No kernel may reach another device: no remote copies, remote signals or barrier semaphores. Data moves between devices by JAX's collectives and lax.ppermute only.
A program may use at most 128 MiB of HBM per device.

```python
import jax
import jax.numpy as jnp
from jax import lax

PX = 128
Y = 128
Z = 128
SEGS = 4
PARTS_SIZE = 8


def layout(key):
    box_key = jax.random.fold_in(key, 7001)
    key_x, key_y, key_pick = jax.random.split(box_key, 3)
    part_ids = jnp.arange(PARTS_SIZE, dtype=jnp.int32)
    len_x = jax.random.randint(key_x, (PARTS_SIZE,), PX // 2, PX + 1, dtype=jnp.int32)
    len_y = jax.random.randint(key_y, (PARTS_SIZE,), Y // 2, Y + 1, dtype=jnp.int32)
    chosen = jax.random.permutation(key_pick, PARTS_SIZE)
    len_x = jnp.where(part_ids == chosen[0], PX, len_x)
    len_x = jnp.where(part_ids == chosen[1], PX // 2, len_x)
    len_y = jnp.where(part_ids == chosen[0], Y, len_y)
    len_y = jnp.where(part_ids == chosen[2], Y // 2, len_y)
    holder = jax.random.permutation(jax.random.fold_in(key, 7002), PARTS_SIZE).astype(jnp.int32)
    return (len_x.astype(jnp.int32), len_y.astype(jnp.int32), holder)


def draw_box_sizes(key, part):
    len_x, len_y, holder = layout(key)
    return jnp.stack([len_x, len_y], axis=1).astype(jnp.int32)


def draw_holder(key, part):
    len_x, len_y, holder = layout(key)
    return holder


def face_weight(key):
    len_x, len_y, holder = layout(key)
    slot_part = jnp.zeros((PARTS_SIZE,), jnp.int32).at[holder].set(jnp.arange(PARTS_SIZE, dtype=jnp.int32))
    slot_len = len_y[slot_part]
    rows = jnp.arange(Y, dtype=jnp.int32)
    near = (rows[None, :] == 1) | (rows[None, :] == slot_len[:, None] - 2)
    weight = jnp.where(near, jnp.float32(1.0), jnp.float32(0.03))
    return weight[:, None, :, None]


def draw_field(key, salt, amplitude):
    weight = face_weight(key)
    value_key = jax.random.fold_in(key, salt)
    values = jax.random.normal(value_key, (PARTS_SIZE, PX, Y, Z), jnp.float32)
    values = jnp.clip(values, -4.5, 4.5)
    return (amplitude * weight * values).astype(jnp.float32)


def draw_adj_next(key, part):
    return draw_field(key, 7101, 1.0)


def draw_adj_later(key, part):
    return draw_field(key, 7102, 0.5)


def draw_partner(key, part):
    key_order, key_shift, key_wall = jax.random.split(key, 3)
    chain_order = jax.random.permutation(key_order, PARTS_SIZE).astype(jnp.int32)
    seg_shift = jnp.where(jax.random.randint(key_shift, (), 0, 2) == 0, 1, SEGS - 1)
    places = jnp.arange(PARTS_SIZE, dtype=jnp.int32)
    walled = jax.random.randint(key_wall, (PARTS_SIZE,), 0, 4) == 0
    walled = (walled | (places == PARTS_SIZE - 1)) & (places != 0)
    segment = jnp.arange(SEGS, dtype=jnp.int32)
    up_step = 1 + (segment[None, :] >= SEGS - seg_shift).astype(jnp.int32)
    up_part = chain_order[(places[:, None] + up_step) % PARTS_SIZE]
    up_seg = (segment[None, :] + seg_shift) % SEGS
    up_link = jnp.where(walled[:, None], -1, up_part * SEGS + up_seg)
    down_step = 1 + (segment[None, :] < seg_shift).astype(jnp.int32)
    down_place = (places[:, None] - down_step) % PARTS_SIZE
    down_part = chain_order[down_place]
    down_seg = (segment[None, :] - seg_shift) % SEGS
    down_link = jnp.where(walled[down_place], -1, down_part * SEGS + down_seg)
    face_rows = jnp.stack([down_link, up_link], axis=1).astype(jnp.int32)
    return jnp.zeros((PARTS_SIZE, 2, SEGS), jnp.int32).at[chain_order].set(face_rows)


def setup_inputs(seed: int = 0) -> dict:
    splits = jax.random.split(jax.random.key(seed), 6)
    adj_next = draw_adj_next(jax.random.fold_in(splits[5], 71), 0)
    adj_later = draw_adj_later(jax.random.fold_in(splits[5], 71), 0)
    box_sizes = draw_box_sizes(jax.random.fold_in(splits[5], 71), 0)
    holder = draw_holder(jax.random.fold_in(splits[5], 71), 0)
    partner = draw_partner(jax.random.fold_in(splits[5], 71), 0)
    return {"adj_next": adj_next, "adj_later": adj_later, "box_sizes": box_sizes, "holder": holder, "partner": partner}


time_step = 0.5
precise = lax.Precision.HIGHEST
stencil_rows = ((0, 0, -2, 2, 0, 0), (0, 2, -27, 27, -2, 0), (-2, 27, -270, 270, -27, 2), (2, -27, 270, -270, 27, -2), (0, -2, 27, -27, 2, 0), (0, 0, 2, -2, 0, 0))

def cosine_table(size_cells, length):
    mode_index = jnp.arange(size_cells, dtype=jnp.int32)[:, None]
    cell_index = jnp.arange(size_cells, dtype=jnp.int32)[None, :]
    extent = length.astype(jnp.float32)
    angles = jnp.pi * mode_index.astype(jnp.float32) * (cell_index.astype(jnp.float32) + 0.5) / extent
    scaling = jnp.sqrt(jnp.where(mode_index == 0, 1.0, 2.0).astype(jnp.float32) / extent)
    inside = (mode_index < length) & (cell_index < length)
    return jnp.where(inside, scaling * jnp.cos(angles), jnp.float32(0.0)).astype(jnp.float32)

def update_factors(len_x, len_y, first_y, count_y, total_x, total_z):
    wave_x = jnp.arange(total_x, dtype=jnp.int32).astype(jnp.float32) / len_x.astype(jnp.float32)
    wave_y = (first_y + jnp.arange(count_y, dtype=jnp.int32)).astype(jnp.float32) / len_y.astype(jnp.float32)
    wave_z = jnp.arange(total_z, dtype=jnp.int32).astype(jnp.float32) / jnp.float32(total_z)
    angular = jnp.pi * jnp.sqrt(wave_x[:, None, None] ** 2 + wave_y[None, :, None] ** 2 + wave_z[None, None, :] ** 2)
    two_cos = 2.0 * jnp.cos(angular * time_step)
    source = time_step ** 2 * jnp.sinc(angular * (time_step / (2.0 * jnp.pi))) ** 2
    return (two_cos.astype(jnp.float32), source.astype(jnp.float32))

def forward_cosine(physical, table_x, table_y, table_z):
    spectral = jnp.einsum('kx,xyz->kyz', table_x, physical, precision=precise)
    spectral = jnp.einsum('ly,kyz->klz', table_y, spectral, precision=precise)
    return jnp.einsum('mz,klz->klm', table_z, spectral, precision=precise)

def inverse_cosine(spectral, table_x, table_y, table_z):
    physical = jnp.einsum('kx,klm->xlm', table_x, spectral, precision=precise)
    physical = jnp.einsum('ly,xlm->xym', table_y, physical, precision=precise)
    return jnp.einsum('mz,xym->xyz', table_z, physical, precision=precise)

def coupling_terms(own_strips, other_strips):
    weights = jnp.transpose(jnp.asarray(stencil_rows, dtype=jnp.float32)) / 180.0
    low_terms = jnp.einsum('ij,...jw->...iw', weights[3:6, 0:3], other_strips[..., 0, :, :, :], precision=precise) + jnp.einsum('ij,...jw->...iw', weights[3:6, 3:6], own_strips[..., 0, :, :, :], precision=precise)
    high_terms = jnp.einsum('ij,...jw->...iw', weights[0:3, 0:3], own_strips[..., 1, :, :, :], precision=precise) + jnp.einsum('ij,...jw->...iw', weights[0:3, 3:6], other_strips[..., 1, :, :, :], precision=precise)
    return jnp.stack([low_terms, high_terms], axis=-4)

def place_terms(result, low_terms, high_terms, len_y):
    result = result.at[:, 0:3, :].add(low_terms)
    window = lax.dynamic_slice_in_dim(result, len_y - 3, 3, 1)
    return lax.dynamic_update_slice_in_dim(result, window + high_terms, len_y - 3, 1)

def reverse_step(current, earlier, box_sizes, holder, partner, slot_part):
    part_count, x_cells, y_cells, z_cells = current.shape
    seg_count = partner.shape[2]
    seg_cells = z_cells // seg_count

    def per_slot(slot_index):
        owner_part = slot_part[slot_index]
        len_x = box_sizes[owner_part, 0]
        len_y = box_sizes[owner_part, 1]
        table_x = cosine_table(x_cells, len_x)
        table_y = cosine_table(y_cells, len_y)
        table_z = cosine_table(z_cells, jnp.int32(z_cells))
        two_cos, source = update_factors(len_x, len_y, 0, y_cells, x_cells, z_cells)
        spectral = forward_cosine(current[slot_index], table_x, table_y, table_z)
        wave_part = inverse_cosine(two_cos * spectral, table_x, table_y, table_z)
        force_part = inverse_cosine(source * spectral, table_x, table_y, table_z)
        low_rows = force_part[:, 0:3, :]
        high_rows = lax.dynamic_slice_in_dim(force_part, len_y - 3, 3, 1)
        return (wave_part, jnp.stack([low_rows, high_rows]))
    wave_all, strip_all = lax.map(per_slot, jnp.arange(part_count, dtype=jnp.int32))
    own_all = strip_all.reshape(part_count, 2, x_cells, 3, seg_count, seg_cells)
    own_all = jnp.transpose(own_all, (0, 1, 4, 3, 2, 5)).reshape(part_count, 2, seg_count, 3, x_cells * seg_cells)
    link_ids = partner[slot_part]
    is_wall = link_ids < 0
    safe_links = jnp.maximum(link_ids, 0)
    peer_part = safe_links // seg_count
    peer_seg = safe_links % seg_count
    peer_slot = holder[peer_part]
    peer_face = jnp.broadcast_to(1 - jnp.arange(2, dtype=jnp.int32)[None, :, None], link_ids.shape)
    other_all = own_all[peer_slot, peer_face, peer_seg]
    coupled = coupling_terms(own_all, other_all)
    len_x_all = box_sizes[slot_part, 0]
    len_y_all = box_sizes[slot_part, 1]
    x_limit = jnp.minimum(len_x_all[:, None, None], box_sizes[peer_part, 0])
    column_x = jnp.arange(x_cells * seg_cells, dtype=jnp.int32) // seg_cells
    joined = ((column_x < x_limit[..., None]) & jnp.logical_not(is_wall)[..., None]).astype(jnp.float32)
    coupled = coupled * joined[:, :, :, None, :]
    coupled = coupled.reshape(part_count, 2, seg_count, 3, x_cells, seg_cells)
    coupled = jnp.transpose(coupled, (0, 1, 4, 3, 2, 5)).reshape(part_count, 2, x_cells, 3, z_cells)
    x_index = jnp.arange(x_cells, dtype=jnp.int32)
    y_index = jnp.arange(y_cells, dtype=jnp.int32)
    inside = ((x_index[None, :, None, None] < len_x_all[:, None, None, None]) & (y_index[None, None, :, None] < len_y_all[:, None, None, None])).astype(jnp.float32)
    result = wave_all - inside * earlier
    return jax.vmap(place_terms)(result, coupled[:, 0], coupled[:, 1], len_y_all)

def reference(adj_next, adj_later, box_sizes, holder, partner):
    part_count = holder.shape[0]
    slot_part = jnp.zeros((part_count,), jnp.int32).at[holder].set(jnp.arange(part_count, dtype=jnp.int32))
    adj_now = reverse_step(adj_next, adj_later, box_sizes, holder, partner, slot_part)
    adj_earlier = reverse_step(adj_now, adj_next, box_sizes, holder, partner, slot_part)
    return (adj_now, adj_earlier)
```

```python
import functools

import jax
import jax.numpy as jnp
import numpy as np
from jax import lax
from jax.experimental import pallas as pl
from jax.experimental.pallas import tpu as pltpu
from jax.sharding import PartitionSpec as P

f32 = jnp.float32
bf16 = jnp.bfloat16
time_step = 0.5
pair_limit = 3
face_rows = 6
padded_rows = 8
plane_block = 8
stencil = np.array(
    (
        (0, 0, -2, 2, 0, 0),
        (0, 2, -27, 27, -2, 0),
        (-2, 27, -270, 270, -27, 2),
        (2, -27, 270, -270, 27, -2),
        (0, -2, 27, -27, 2, 0),
        (0, 0, 2, -2, 0, 0),
    ),
    np.float32,
)
weights = np.transpose(stencil) / np.float32(180.0)
params = pltpu.CompilerParams(vmem_limit_bytes=40 * 2**20)


def cost(flops, data):
    return pl.CostEstimate(flops=int(flops), bytes_accessed=int(data), transcendentals=0)


def cosine_entries(modes, cells, length):
    turns = jnp.remainder(modes * (2 * cells + 1), 4 * length)
    extent = length.astype(f32)
    angles = turns.astype(f32) * (f32(jnp.pi) / (2.0 * extent))
    scaling = jnp.sqrt(jnp.where(modes == 0, 1.0, 2.0).astype(f32) / extent)
    inside = (modes < length) & (cells < length) & (cells >= 0)
    return jnp.where(inside, scaling * jnp.cos(angles), f32(0.0))


def halves(table):
    high = lax.reduce_precision(table, 8, 7)
    return high, table - high


def stacked(table):
    high, low = halves(table)
    row = jnp.concatenate([high, low], axis=1)
    return jnp.concatenate([row, row], axis=0).astype(bf16)


def stacked_constant(table):
    high = table.astype(np.float32).astype(jnp.bfloat16)
    low = (table - high.astype(np.float64)).astype(np.float32).astype(jnp.bfloat16)
    row = np.concatenate([high, low], axis=1)
    return np.concatenate([row, row], axis=0)


def z_tables(z_cells, count):
    modes = np.arange(z_cells)[:, None]
    cells = np.arange(z_cells)[None, :]
    table = np.sqrt(np.where(modes == 0, 1.0, 2.0) / z_cells) * np.cos(
        np.pi * modes * (cells + 0.5) / z_cells
    )
    width = z_cells // count
    forward, inverse = [], []
    for me in range(count):
        order = np.concatenate([np.arange(width) + (me ^ k) * width for k in range(count)])
        mine = table[order]
        forward.append(stacked_constant(mine.T))
        inverse.append(stacked_constant(mine))
    return np.stack(forward), np.stack(inverse)


def update_factors(len_x, len_y, first_z, count_z, total_x, total_y, total_z):
    wave_x = jnp.arange(total_x, dtype=jnp.int32).astype(f32) / len_x.astype(f32)
    wave_y = jnp.arange(total_y, dtype=jnp.int32).astype(f32) / len_y.astype(f32)
    wave_z = (first_z + jnp.arange(count_z, dtype=jnp.int32)).astype(f32) / f32(total_z)
    angular = jnp.pi * jnp.sqrt(
        wave_x[None, None, :] ** 2 + wave_y[None, :, None] ** 2 + wave_z[:, None, None] ** 2
    )
    two_cos = 2.0 * jnp.cos(angular * time_step)
    source = time_step**2 * jnp.sinc(angular * (time_step / (2.0 * jnp.pi))) ** 2
    return two_cos, source.astype(f32)


def split(value):
    high = value.astype(bf16)
    low = (value - high.astype(f32)).astype(bf16)
    return high, low


def times(value, table):
    product = jnp.dot(
        jnp.concatenate(split(value), axis=1), table, preferred_element_type=f32
    )
    width = product.shape[1] // 2
    return product[:, :width] + product[:, width:]


def flip(value, count):
    rows = value.shape[0] // count
    return jnp.concatenate([value[i * rows : (i + 1) * rows].T for i in range(count)], axis=0)


def lanes_of(refs, row, width):
    return jnp.concatenate([ref[:, row * width : (row + 1) * width] for ref in refs], axis=1)


def z_forward_kernel(count, me_ref, field_ref, table_ref, *out_refs):
    block, y_cells, z_cells = field_ref.shape
    width = z_cells // count
    modes = times(field_ref[...].reshape(block * y_cells, z_cells), table_ref[0])
    for x in range(block):
        turned = modes[x * y_cells : (x + 1) * y_cells].T
        for k in range(count):
            out_refs[k][x] = turned[k * width : (k + 1) * width]


def z_forward(field, me, tables, count):
    x_local, y_cells, z_cells = field.shape
    width = z_cells // count
    block = min(8, x_local)
    return pl.pallas_call(
        functools.partial(z_forward_kernel, count),
        grid_spec=pltpu.PrefetchScalarGridSpec(
            num_scalar_prefetch=1,
            grid=(x_local // block,),
            in_specs=[
                pl.BlockSpec((block, y_cells, z_cells), lambda i, me: (i, 0, 0)),
                pl.BlockSpec((1,) + tables.shape[1:], lambda i, me: (me[0], 0, 0)),
            ],
            out_specs=[
                pl.BlockSpec((block, width, y_cells), lambda i, me: (i, 0, 0))
                for _ in range(count)
            ],
        ),
        out_shape=[jax.ShapeDtypeStruct((x_local, width, y_cells), f32)] * count,
        compiler_params=params,
        cost_estimate=cost(8 * field.size * z_cells, 8 * field.size),
        name="z_forward",
    )(me, field, tables)


def plane_forward(block_refs, y_table, x_table):
    planes = block_refs[0].shape[1]
    value = jnp.concatenate([ref[...] for ref in block_refs], axis=0)
    x_cells, _, y_cells = value.shape
    value = jnp.swapaxes(value, 0, 1).reshape(planes * x_cells, y_cells)
    value = flip(times(value, y_table), planes)
    return times(value, x_table)


def plane_inverse(spectral, planes, x_table, y_table):
    value = flip(times(spectral, x_table), planes)
    value = times(value, y_table)
    value = value.reshape(planes, value.shape[0] // planes, value.shape[1])
    return jnp.swapaxes(value, 0, 1)


def store_faces(step, planes, total, spectral, face_table, rows_ref):
    y_modes = spectral.shape[0] // planes
    for j in range(planes):
        high, low = split(spectral[j * y_modes : (j + 1) * y_modes])
        both = jnp.dot(
            face_table, jnp.concatenate([high, low], axis=0), preferred_element_type=f32
        )
        rows = both[:padded_rows] + both[padded_rows:]
        rows_ref[pl.ds(step * planes + j, padded_rows, stride=total), :] = rows


def send_faces(rows_ref, x_table, face_refs):
    value = times(rows_ref[...], x_table).T
    x_local = face_refs[0].shape[0]
    for k, ref in enumerate(face_refs):
        ref[...] = value[k * x_local : (k + 1) * x_local]


def first_kernel(count, *refs):
    blocks, refs = refs[:count], refs[count:]
    wave_ref, source_ref, y_ref, x_ref, x_back_ref, face_ref = refs[:6]
    out_ref, face_refs, rows_ref = refs[6], refs[7 : 7 + count], refs[7 + count]
    step = pl.program_id(0)
    planes = wave_ref.shape[0]
    spectral = plane_forward(blocks, y_ref[...], x_ref[...])
    shape = wave_ref.shape
    out_ref[...] = wave_ref[...] * spectral.reshape(shape)
    forced = source_ref[...].reshape(spectral.shape) * spectral
    total = rows_ref.shape[0] // padded_rows
    store_faces(step, planes, total, forced, face_ref[...], rows_ref)

    @pl.when(step == pl.num_programs(0) - 1)
    def _():
        send_faces(rows_ref, x_back_ref[...], face_refs)


def difference_kernel(count, *refs):
    blocks = refs[:count]
    waved_ref, y_ref, x_ref, out_ref = refs[count:]
    spectral = plane_forward(blocks, y_ref[...], x_ref[...])
    out_ref[...] = waved_ref[...] - spectral.reshape(waved_ref.shape)


def second_kernel(count, *refs):
    sums, refs = refs[:count], refs[count:]
    partial_ref, wave_ref, source_ref, x_ref, x_back_ref, face_ref, place_ref = refs[:7]
    out_ref, face_refs = refs[7], refs[8 : 8 + count]
    rows_ref, terms_ref = refs[8 + count :]
    step = pl.program_id(0)
    planes, y_modes, x_modes = wave_ref.shape
    total = rows_ref.shape[0] // padded_rows

    @pl.when(step == 0)
    def _():
        width = sums[0].shape[1] // padded_rows
        value = jnp.concatenate([lanes_of(sums, r, width) for r in range(padded_rows)], axis=0)
        terms_ref[...] = times(value, x_ref[...])

    pieces = []
    for j in range(planes):
        rows = terms_ref[pl.ds(step * planes + j, padded_rows, stride=total), :]
        high = rows.astype(bf16).astype(f32)
        low = rows - high
        stack = jnp.concatenate([high, low, high, jnp.zeros_like(rows)], axis=0).astype(bf16)
        added = jnp.dot(place_ref[...], stack, preferred_element_type=f32)
        pieces.append(partial_ref[j] + added)
    spectral = jnp.concatenate(pieces, axis=0)
    out_ref[...] = wave_ref[...] * spectral.reshape(wave_ref.shape)
    forced = source_ref[...].reshape(spectral.shape) * spectral
    store_faces(step, planes, total, forced, face_ref[...], rows_ref)

    @pl.when(step == pl.num_programs(0) - 1)
    def _():
        send_faces(rows_ref, x_back_ref[...], face_refs)


def inverse_kernel(count, *refs):
    waved_ref, x_ref, y_ref = refs[:3]
    out_refs = refs[3:]
    planes, y_modes, x_modes = waved_ref.shape
    value = plane_inverse(
        waved_ref[...].reshape(planes * y_modes, x_modes), planes, x_ref[...], y_ref[...]
    )
    parts = len(out_refs) // count
    x_part = out_refs[0].shape[0]
    for i, ref in enumerate(out_refs):
        ref[...] = value[i * x_part : (i + 1) * x_part]


def whole(shape):
    zeros = (0,) * len(shape)
    return pl.BlockSpec(shape, lambda i: zeros)


def plane_specs(blocks):
    return [
        pl.BlockSpec((b.shape[0], plane_block, b.shape[2]), lambda i: (0, i, 0)) for b in blocks
    ]


def mode_spec(shape):
    return pl.BlockSpec((plane_block,) + shape[1:], lambda i: (i, 0, 0))


def first_part(blocks, wave, source, tabs):
    count = len(blocks)
    planes, y_modes, x_modes = wave.shape
    x_local = x_modes // count
    face_shape = (x_local, padded_rows * planes)
    small = [tabs["y"], tabs["x"], tabs["x_back"], tabs["face"]]
    out = pl.pallas_call(
        functools.partial(first_kernel, count),
        grid=(planes // plane_block,),
        in_specs=plane_specs(blocks)
        + [mode_spec(wave.shape)] * 2
        + [whole(t.shape) for t in small],
        out_specs=[mode_spec(wave.shape)] + [whole(face_shape)] * count,
        out_shape=[jax.ShapeDtypeStruct(wave.shape, f32)]
        + [jax.ShapeDtypeStruct(face_shape, f32)] * count,
        scratch_shapes=[pltpu.VMEM((padded_rows * planes, x_modes), f32)],
        compiler_params=params,
        cost_estimate=cost(24 * wave.size * x_modes, 16 * wave.size),
        name="first_modes",
    )(*blocks, wave, source, *small)
    return out[0], out[1:]


def difference_part(blocks, waved, tabs):
    count = len(blocks)
    small = [tabs["y"], tabs["x"]]
    return pl.pallas_call(
        functools.partial(difference_kernel, count),
        grid=(waved.shape[0] // plane_block,),
        in_specs=plane_specs(blocks) + [mode_spec(waved.shape)] + [whole(t.shape) for t in small],
        out_specs=mode_spec(waved.shape),
        out_shape=jax.ShapeDtypeStruct(waved.shape, f32),
        compiler_params=params,
        cost_estimate=cost(16 * waved.size * waved.shape[2], 12 * waved.size),
        name="later_modes",
    )(*blocks, waved, *small)


def second_part(sums, partial, wave, source, tabs):
    count = len(sums)
    planes, y_modes, x_modes = wave.shape
    x_local = x_modes // count
    face_shape = (x_local, padded_rows * planes)
    small = [tabs["x"], tabs["x_back"], tabs["face"], tabs["place"]]
    out = pl.pallas_call(
        functools.partial(second_kernel, count),
        grid=(planes // plane_block,),
        in_specs=[whole(s.shape) for s in sums]
        + [mode_spec(wave.shape)] * 3
        + [whole(t.shape) for t in small],
        out_specs=[mode_spec(wave.shape)] + [whole(face_shape)] * count,
        out_shape=[jax.ShapeDtypeStruct(wave.shape, f32)]
        + [jax.ShapeDtypeStruct(face_shape, f32)] * count,
        scratch_shapes=[
            pltpu.VMEM((padded_rows * planes, x_modes), f32),
            pltpu.VMEM((padded_rows * planes, x_modes), f32),
        ],
        compiler_params=params,
        cost_estimate=cost(8 * wave.size * x_modes, 16 * wave.size),
        name="second_modes",
    )(*sums, partial, wave, source, *small)
    return out[0], out[1:]


def inverse_part(waved, tabs, count, parts):
    planes, y_modes, x_modes = waved.shape
    y_cells = tabs["y_back"].shape[1] // 2
    x_part = x_modes // (count * parts)
    small = [tabs["x_back"], tabs["y_back"]]
    out = pl.pallas_call(
        functools.partial(inverse_kernel, count),
        grid=(planes // plane_block,),
        in_specs=[mode_spec(waved.shape)] + [whole(t.shape) for t in small],
        out_specs=[
            pl.BlockSpec((x_part, plane_block, y_cells), lambda i: (0, i, 0))
            for _ in range(count * parts)
        ],
        out_shape=[jax.ShapeDtypeStruct((x_part, planes, y_cells), f32)] * (count * parts),
        compiler_params=params,
        cost_estimate=cost(16 * waved.size * x_modes, 8 * waved.size),
        name="modes_to_cells",
    )(waved, *small)
    return [[out[k * parts + c] for k in range(count)] for c in range(parts)]


def strips_kernel(count, seg_count, scalars_ref, *refs):
    faces, (table_ref, own_ref, send_ref) = refs[:count], refs[count:]
    rows, x_local, z_cells = own_ref.shape
    width = faces[0].shape[1] // padded_rows
    value = jnp.concatenate([lanes_of(faces, r, width) for r in range(rows)], axis=0)
    value = times(value, table_ref[0]).reshape(rows, x_local, z_cells)
    own_ref[...] = value
    seg_cells = z_cells // seg_count
    groups = z_cells // seg_cells
    lane = lax.broadcasted_iota(jnp.int32, (8, z_cells), 1) // seg_cells
    for item in range(2 * seg_count):
        face, seg = item // seg_count, item % seg_count
        dest, slot, wall = scalars_ref[1, item], scalars_ref[2, item], scalars_ref[5, item]

        @pl.when(wall == 0)
        def _():
            for j in range(3):
                packed = jnp.zeros((8, z_cells), f32)
                for c in range(groups):
                    piece = value[face * 3 + j, 8 * c : 8 * (c + 1)]
                    shift = (c - seg) * seg_cells % z_cells
                    if shift:
                        piece = pltpu.roll(piece, shift, 1)
                    packed = jnp.where(lane == c, piece, packed)
                send_ref[dest, slot, j] = packed


def strips_part(faces, scalars, tables, seg_count, part_count):
    count = len(faces)
    x_local = faces[0].shape[0]
    z_cells = tables.shape[2] // 2
    own_shape = (face_rows, x_local, z_cells)
    send_shape = (part_count, pair_limit, 3, 8, z_cells)
    return pl.pallas_call(
        functools.partial(strips_kernel, count, seg_count),
        grid_spec=pltpu.PrefetchScalarGridSpec(
            num_scalar_prefetch=1,
            grid=(1,),
            in_specs=[pl.BlockSpec(f.shape, lambda i, s: (0, 0)) for f in faces]
            + [pl.BlockSpec((1,) + tables.shape[1:], lambda i, s: (s[0, 0], 0, 0))],
            out_specs=[
                pl.BlockSpec(own_shape, lambda i, s: (0, 0, 0)),
                pl.BlockSpec(send_shape, lambda i, s: (0, 0, 0, 0, 0)),
            ],
        ),
        out_shape=[jax.ShapeDtypeStruct(own_shape, f32), jax.ShapeDtypeStruct(send_shape, f32)],
        compiler_params=params,
        cost_estimate=cost(1e6, 2e6),
        name="strips",
    )(scalars, *faces, tables)


def couple_kernel(count, seg_count, send, scalars_ref, own_ref, got_ref, table_ref, *out_refs):
    rows, x_local, z_cells = own_ref.shape
    seg_cells = z_cells // seg_count
    groups = z_cells // seg_cells
    lane = lax.broadcasted_iota(jnp.int32, (8, z_cells), 1) // seg_cells
    first_x = scalars_ref[0, 0] * x_local
    row_x = first_x + lax.broadcasted_iota(jnp.int32, (x_local, z_cells), 0)
    lane_all = lax.broadcasted_iota(jnp.int32, (x_local, z_cells), 1) // seg_cells
    terms = []
    for face in range(2):
        limit = jnp.zeros((x_local, z_cells), jnp.int32)
        other = [[jnp.zeros((8, z_cells), f32)] * groups for _ in range(3)]
        for seg in range(seg_count):
            item = face * seg_count + seg
            source, slot = scalars_ref[1, item], scalars_ref[3, item]
            limit = jnp.where(lane_all == seg, scalars_ref[4, item], limit)
            for j in range(3):
                packed = got_ref[source, slot, j]
                for c in range(groups):
                    shift = (seg - c) * seg_cells % z_cells
                    piece = pltpu.roll(packed, shift, 1) if shift else packed
                    other[j][c] = jnp.where(lane == seg, piece, other[j][c])
        other = [jnp.concatenate(o, axis=0) for o in other]
        own = [own_ref[face * 3 + j] for j in range(3)]
        low, high = (other, own) if face == 0 else (own, other)
        keep = row_x < limit
        for i in range(3):
            row = weights[3 + i] if face == 0 else weights[i]
            total = jnp.zeros((x_local, z_cells), f32)
            for j in range(6):
                if row[j] != 0:
                    total = total + float(row[j]) * (low + high)[j]
            terms.append(jnp.where(keep, total, 0.0))
    for r in range(rows):
        out_refs[0][r] = terms[r]
    if send:
        blank = [jnp.zeros((x_local, z_cells), f32)] * (padded_rows - rows)
        value = times(jnp.concatenate(terms + blank, axis=0), table_ref[0]).T
        width = z_cells // count
        for k in range(count):
            out_refs[1 + k][...] = value[k * width : (k + 1) * width]


def couple_part(own, got, scalars, tables, seg_count, count, send):
    rows, x_local, z_cells = own.shape
    sum_shape = (z_cells // count, padded_rows * x_local)
    extra = count if send else 0
    out = pl.pallas_call(
        functools.partial(couple_kernel, count, seg_count, send),
        grid_spec=pltpu.PrefetchScalarGridSpec(
            num_scalar_prefetch=1,
            grid=(1,),
            in_specs=[
                pl.BlockSpec(own.shape, lambda i, s: (0, 0, 0)),
                pl.BlockSpec(got.shape, lambda i, s: (0, 0, 0, 0, 0)),
                pl.BlockSpec((1,) + tables.shape[1:], lambda i, s: (s[0, 0], 0, 0)),
            ],
            out_specs=[pl.BlockSpec(own.shape, lambda i, s: (0, 0, 0))]
            + [pl.BlockSpec(sum_shape, lambda i, s: (0, 0))] * extra,
        ),
        out_shape=[jax.ShapeDtypeStruct(own.shape, f32)]
        + [jax.ShapeDtypeStruct(sum_shape, f32)] * extra,
        compiler_params=params,
        cost_estimate=cost(1e6, 2e6),
        name="couple",
    )(scalars, own, got, tables)
    return out[0], out[1:]


def z_inverse_kernel(count, scalars_ref, *refs):
    blocks, (earlier_ref, terms_ref, table_ref, out_ref) = refs[:count], refs[count:]
    block, y_cells, z_cells = earlier_ref.shape
    me, len_x, len_y = scalars_ref[0, 0], scalars_ref[0, 1], scalars_ref[0, 2]
    first = scalars_ref[0, 3] + pl.program_id(0) * block
    row = lax.broadcasted_iota(jnp.int32, (y_cells, z_cells), 0)
    pieces = []
    for x in range(block):
        modes = jnp.concatenate([ref[x] for ref in blocks], axis=0)
        pieces.append(modes.T)
    value = times(jnp.concatenate(pieces, axis=0), table_ref[0])
    start = pl.multiple_of(jnp.minimum((len_y - 3) // 8 * 8, y_cells - 16), 8)
    window = start + lax.broadcasted_iota(jnp.int32, (16, z_cells), 0)
    low_row = lax.broadcasted_iota(jnp.int32, (8, z_cells), 0)
    for x in range(block):
        limit = jnp.where(first + x < len_x, len_y, 0)
        out_ref[x] = value[x * y_cells : (x + 1) * y_cells] - jnp.where(
            row < limit, earlier_ref[x], 0.0
        )
        low = out_ref[x, 0:8]
        for r in range(3):
            low = low + jnp.where(low_row == r, terms_ref[r, x : x + 1], 0.0)
        out_ref[x, 0:8] = low
        high = out_ref[x, pl.ds(start, 16)]
        for r in range(3):
            high = high + jnp.where(window == len_y - 3 + r, terms_ref[3 + r, x : x + 1], 0.0)
        out_ref[x, pl.ds(start, 16)] = high


def z_inverse(blocks, earlier, terms, scalars, tables):
    count = len(blocks)
    x_local, y_cells, z_cells = earlier.shape
    width = z_cells // count
    block = min(8, x_local)
    return pl.pallas_call(
        functools.partial(z_inverse_kernel, count),
        grid_spec=pltpu.PrefetchScalarGridSpec(
            num_scalar_prefetch=1,
            grid=(x_local // block,),
            in_specs=[pl.BlockSpec((block, width, y_cells), lambda i, s: (i, 0, 0))] * count
            + [
                pl.BlockSpec((block, y_cells, z_cells), lambda i, s: (i, 0, 0)),
                pl.BlockSpec((face_rows, block, z_cells), lambda i, s: (0, i, 0)),
                pl.BlockSpec((1,) + tables.shape[1:], lambda i, s: (s[0, 0], 0, 0)),
            ],
            out_specs=pl.BlockSpec((block, y_cells, z_cells), lambda i, s: (i, 0, 0)),
        ),
        out_shape=jax.ShapeDtypeStruct(earlier.shape, f32),
        compiler_params=params,
        cost_estimate=cost(8 * earlier.size * z_cells, 12 * earlier.size),
        name="z_inverse",
    )(scalars, *blocks, earlier, terms, tables)


def exchange(blocks):
    count = len(blocks)
    return [blocks[0]] + [
        lax.ppermute(blocks[k], "sub", [(i, i ^ k) for i in range(count)])
        for k in range(1, count)
    ]


def local(adj_next, adj_later, box_sizes, holder, partner):
    part_count = holder.shape[0]
    seg_count = partner.shape[2]
    item_count = 2 * seg_count
    my_group = lax.axis_index("grp")
    me = lax.axis_index("sub").astype(jnp.int32)
    count = lax.axis_size("sub")
    _, x_local, y_cells, z_cells = adj_next.shape
    x_total = x_local * count
    z_local = z_cells // count
    z_fwd, z_inv = (jnp.asarray(t) for t in z_tables(z_cells, count))
    place = me.reshape(1)

    next_blocks = exchange(z_forward(adj_next[0], place, z_fwd, count))
    later_blocks = exchange(z_forward(adj_later[0], place, z_fwd, count))

    part_ids = jnp.arange(part_count, dtype=jnp.int32)
    my_part = jnp.sum(jnp.where(holder == my_group, part_ids, 0))
    len_x = box_sizes[my_part, 0]
    len_y = box_sizes[my_part, 1]
    modes = jnp.arange(x_total, dtype=jnp.int32)
    cells = (modes // x_local ^ me) * x_local + modes % x_local
    table_x = cosine_entries(modes[:, None], cells[None, :], len_x)
    table_x_t = cosine_entries(modes[None, :], cells[:, None], len_x)
    modes_y = jnp.arange(y_cells, dtype=jnp.int32)
    table_y = cosine_entries(modes_y[:, None], modes_y[None, :], len_y)
    table_y_t = cosine_entries(modes_y[None, :], modes_y[:, None], len_y)
    rows = jnp.arange(padded_rows, dtype=jnp.int32)
    cell_rows = jnp.where(rows < 3, rows, jnp.where(rows < 6, len_y - 6 + rows, -1))
    face_high, face_low = halves(cosine_entries(modes_y[None, :], cell_rows[:, None], len_y))
    turn_high, turn_low = halves(cosine_entries(modes_y[:, None], cell_rows[None, :], len_y))
    tabs = {
        "x": stacked(table_x_t),
        "x_back": stacked(table_x),
        "y": stacked(table_y_t),
        "y_back": stacked(table_y),
        "face": jnp.concatenate(
            [
                jnp.concatenate([face_high, face_high], axis=1),
                jnp.concatenate([face_low, face_low], axis=1),
            ],
            axis=0,
        ).astype(bf16),
        "place": jnp.concatenate(
            [turn_high, turn_high, turn_low, jnp.zeros_like(turn_low)], axis=1
        ).astype(bf16),
    }
    wave, source = update_factors(
        len_x, len_y, me * z_local, z_local, x_total, y_cells, z_cells
    )

    link_ids = partner[my_part].reshape(item_count)
    is_wall = link_ids < 0
    safe_links = jnp.maximum(link_ids, 0)
    peer_part = safe_links // seg_count
    peer_seg = safe_links % seg_count
    item_ids = jnp.arange(item_count, dtype=jnp.int32)
    peer_item = (1 - item_ids // seg_count) * seg_count + peer_seg
    to_part = jnp.where(is_wall, -1, peer_part)
    same = (to_part[None, :] == to_part[:, None]) & (item_ids[None, :] < item_ids[:, None])
    send_slot = jnp.sum(same.astype(jnp.int32), axis=1)
    peer_links = partner.reshape(part_count, item_count)[peer_part]
    to_me = (peer_links >= 0) & (peer_links // seg_count == my_part)
    before = item_ids[None, :] < peer_item[:, None]
    get_slot = jnp.sum((to_me & before).astype(jnp.int32), axis=1)
    x_limit = jnp.where(is_wall, 0, jnp.minimum(len_x, box_sizes[peer_part, 0]))
    head = jnp.zeros((item_count,), jnp.int32)
    head = head.at[0].set(me).at[1].set(len_x).at[2].set(len_y).at[3].set(me * x_local)
    scalars = jnp.stack(
        [
            head,
            jnp.where(is_wall, 0, holder[peer_part]),
            jnp.minimum(send_slot, pair_limit - 1),
            jnp.where(is_wall, 0, jnp.minimum(get_slot, pair_limit - 1)),
            x_limit,
            is_wall.astype(jnp.int32),
        ]
    )

    def coupled(faces, send):
        own, outgoing = strips_part(exchange(faces), scalars, z_inv, seg_count, part_count)
        got = lax.all_to_all(outgoing, "grp", 0, 0, tiled=True)
        return couple_part(own, got, scalars, z_fwd, seg_count, count, send)

    waved, faces = first_part(next_blocks, wave, source, tabs)
    (back,) = inverse_part(waved, tabs, count, 1)
    terms_now, sums = coupled(faces, True)
    adj_now = z_inverse(exchange(back), adj_later[0], terms_now, scalars, z_inv)
    partial = difference_part(later_blocks, waved, tabs)
    waved, faces = second_part(exchange(sums), partial, wave, source, tabs)
    (back,) = inverse_part(waved, tabs, count, 1)
    terms_earlier, _ = coupled(faces, False)
    adj_earlier = z_inverse(exchange(back), adj_next[0], terms_earlier, scalars, z_inv)
    return (adj_now[None], adj_earlier[None])


def solution(mesh):
    return jax.shard_map(
        local,
        mesh=mesh,
        in_specs=(P("grp", "sub", None, None), P("grp", "sub", None, None), P(), P(), P()),
        out_specs=(P("grp", "sub", None, None), P("grp", "sub", None, None)),
        check_vma=False,
    )
```

```python
import functools
import math

import jax
import jax.numpy as jnp
import numpy as np
from jax import lax
from jax.experimental import pallas as pl
from jax.experimental.pallas import tpu as pltpu
from jax.sharding import PartitionSpec as P

f32 = jnp.float32
bf16 = jnp.bfloat16
time_step = 0.5
half_phase = (math.pi * time_step / 2.0) ** 2
pair_limit = 3
face_rows = 6
padded_rows = 8
plane_block = 8
costs = {"forward_next": 2, "tables": 0, "forward_later": 8, "first_a": 8, "first_b": 32, "back": 10, "strips_now": 8, "later": 0, "couple_now": 8, "second": 16, "strips_earlier": 8, "now": 64, "end": 0, "gate": 0.0}
stencil = np.array(
    (
        (0, 0, -2, 2, 0, 0),
        (0, 2, -27, 27, -2, 0),
        (-2, 27, -270, 270, -27, 2),
        (2, -27, 270, -270, 27, -2),
        (0, -2, 27, -27, 2, 0),
        (0, 0, 2, -2, 0, 0),
    ),
    np.float32,
)
weights = np.transpose(stencil) / np.float32(180.0)
params = pltpu.CompilerParams(vmem_limit_bytes=60 * 2**20)


anywhere = pl.BlockSpec(memory_space=pl.ANY)


def array_of(shape, dtype=f32):
    return jax.ShapeDtypeStruct(shape, dtype)


def cost(work):
    return pl.CostEstimate(flops=int(work * 1e9), bytes_accessed=1024, transcendentals=0)


def stacked_constant(table):
    high = table.astype(np.float32).astype(jnp.bfloat16)
    low = (table - high.astype(np.float64)).astype(np.float32).astype(jnp.bfloat16)
    row = np.concatenate([high, low], axis=1)
    return np.concatenate([row, row], axis=0)


def z_tables(z_cells, count):
    modes = np.arange(z_cells)[:, None]
    cells = np.arange(z_cells)[None, :]
    table = np.sqrt(np.where(modes == 0, 1.0, 2.0) / z_cells) * np.cos(
        np.pi * modes * (cells + 0.5) / z_cells
    )
    width = z_cells // count
    forward, inverse = [], []
    for me in range(count):
        order = np.concatenate([np.arange(width) + (me ^ k) * width for k in range(count)])
        mine = table[order]
        forward.append(stacked_constant(mine.T))
        inverse.append(stacked_constant(mine))
    return np.stack(forward), np.stack(inverse)


def split(value):
    high = value.astype(bf16)
    low = (value - high.astype(f32)).astype(bf16)
    return high, low


def times(value, table):
    product = jnp.dot(
        jnp.concatenate(split(value), axis=1), table, preferred_element_type=f32
    )
    width = product.shape[1] // 2
    return product[:, :width] + product[:, width:]


def flip(value, count):
    rows = value.shape[0] // count
    return jnp.concatenate([value[i * rows : (i + 1) * rows].T for i in range(count)], axis=0)


def lanes_of(refs, row, parts):
    pieces = []
    for ref in refs:
        width = ref.shape[1] // (parts * padded_rows)
        for c in range(parts):
            first = (c * padded_rows + row) * width
            pieces.append(ref[:, first : first + width])
    return jnp.concatenate(pieces, axis=1)


def sine_ratio(square, terms):
    total = jnp.full_like(square, (-1.0) ** (terms - 1) / math.factorial(2 * terms - 1))
    for n in reversed(range(terms - 1)):
        total = total * square + (-1.0) ** n / math.factorial(2 * n + 1)
    return total


def cosine_entries(modes, cells, length):
    extent = jnp.full(modes.shape, length).astype(f32)
    steps = (modes * (2 * cells + 1)).astype(f32)
    period = 4.0 * extent
    turns = steps - period * jnp.floor(steps / period)
    turns = jnp.where(turns < 0.0, turns + period, turns)
    turns = jnp.where(turns >= period, turns - period, turns)
    turns = jnp.minimum(turns, period - turns)
    angle = (extent - turns) * (f32(math.pi / 2) / extent)
    scaling = jnp.sqrt(jnp.where(modes == 0, 1.0, 2.0) / extent)
    inside = (modes < length) & (cells < length) & (cells >= 0)
    return jnp.where(inside, scaling * angle * sine_ratio(angle * angle, 9), 0.0)


def stacked(table):
    row = jnp.concatenate(split(table), axis=1)
    return jnp.concatenate([row, row], axis=0)


def links(seg_count, ids_ref, box_ref, holder_ref, partner_ref, scalars_ref):
    item_count = 2 * seg_count
    part_count = holder_ref.shape[0]
    me, group, x_local = ids_ref[0], ids_ref[1], ids_ref[2]

    def find(p, found):
        return jnp.where(holder_ref[p] == group, p, found)

    part = lax.fori_loop(0, part_count, find, jnp.int32(0))
    len_x, len_y = box_ref[part, 0], box_ref[part, 1]
    head = [me, len_x, len_y, me * x_local]
    mine = [partner_ref[part, i] for i in range(item_count)]
    peers = [jnp.where(m < 0, -1, lax.div(jnp.maximum(m, 0), seg_count)) for m in mine]
    for item in range(item_count):
        wall = mine[item] < 0
        peer = jnp.maximum(peers[item], 0)
        seg = lax.rem(jnp.maximum(mine[item], 0), seg_count)
        peer_item = (1 - item // seg_count) * seg_count + seg
        send_slot, get_slot = jnp.int32(0), jnp.int32(0)
        for i in range(item_count):
            if i < item:
                send_slot += jnp.where(peers[i] == peer, 1, 0)
            link = partner_ref[peer, i]
            back = jnp.where(link < 0, -1, lax.div(jnp.maximum(link, 0), seg_count))
            get_slot += jnp.where((back == part) & (i < peer_item), 1, 0)
        scalars_ref[0, item] = head[item] if item < len(head) else jnp.int32(0)
        scalars_ref[1, item] = jnp.where(wall, 0, holder_ref[peer])
        scalars_ref[2, item] = jnp.minimum(send_slot, pair_limit - 1)
        scalars_ref[3, item] = jnp.where(wall, 0, jnp.minimum(get_slot, pair_limit - 1))
        scalars_ref[4, item] = jnp.where(wall, 0, jnp.minimum(len_x, box_ref[peer, 0]))
        scalars_ref[5, item] = jnp.where(wall, 1, 0)
    return me, len_x, len_y


def tables_kernel(seg_count, ids_ref, box_ref, holder_ref, partner_ref, *refs):
    z_ref, z_back_ref = refs[:2]
    refs = refs[-10:]
    scalars_ref, x_ref, x_back_ref, y_ref, y_back_ref, face_ref, place_ref = refs[:7]
    squares_ref, my_z_ref, my_z_back_ref = refs[7:]
    my_z_ref[...] = z_ref[ids_ref[0]]
    my_z_back_ref[...] = z_back_ref[ids_ref[0]]
    y_cells, x_cells = squares_ref.shape
    me, len_x, len_y = links(seg_count, ids_ref, box_ref, holder_ref, partner_ref, scalars_ref)
    x_local = ids_ref[2]

    def index(shape, axis):
        return lax.broadcasted_iota(jnp.int32, shape, axis)

    def cells_x(axis):
        cell = index((x_cells, x_cells), axis)
        return (lax.div(cell, x_local) ^ me) * x_local + lax.rem(cell, x_local)

    square = (x_cells, x_cells)
    x_ref[...] = stacked(cosine_entries(index(square, 1), cells_x(0), len_x))
    x_back_ref[...] = stacked(cosine_entries(index(square, 0), cells_x(1), len_x))
    square = (y_cells, y_cells)
    y_ref[...] = stacked(cosine_entries(index(square, 1), index(square, 0), len_y))
    y_back_ref[...] = stacked(cosine_entries(index(square, 0), index(square, 1), len_y))

    def cell_rows(rows):
        return jnp.where(rows < 3, rows, jnp.where(rows < face_rows, len_y - face_rows + rows, -1))

    shape = (padded_rows, y_cells)
    face = cosine_entries(index(shape, 1), cell_rows(index(shape, 0)), len_y)
    high = face.astype(bf16).astype(f32)
    both = jnp.concatenate([high, face - high], axis=0)
    face_ref[...] = jnp.concatenate([both, both], axis=1).astype(bf16)
    shape = (y_cells, 4 * padded_rows)
    column = index(shape, 1)
    turned = cosine_entries(index(shape, 0), cell_rows(lax.rem(column, padded_rows)), len_y)
    high = turned.astype(bf16).astype(f32)
    part = jnp.where(column < 2 * padded_rows, high, turned - high)
    place_ref[...] = jnp.where(column < 3 * padded_rows, part, 0.0).astype(bf16)

    shape = (y_cells, x_cells)
    ratio_x = index(shape, 1).astype(f32) / jnp.full(shape, len_x).astype(f32)
    ratio_y = index(shape, 0).astype(f32) / jnp.full(shape, len_y).astype(f32)
    squares_ref[...] = (ratio_x * ratio_x + ratio_y * ratio_y) * half_phase


def make_tables(ids, box_sizes, holder, partner, shape, z_fwd, z_inv, after):
    y_cells, x_cells = shape
    part_count, _, seg_count = partner.shape
    item_count = 2 * seg_count
    out_shapes = [
        (6, item_count),
        (2 * x_cells, 2 * x_cells),
        (2 * x_cells, 2 * x_cells),
        (2 * y_cells, 2 * y_cells),
        (2 * y_cells, 2 * y_cells),
        (2 * padded_rows, 2 * y_cells),
        (y_cells, 4 * padded_rows),
        shape,
        z_fwd.shape[1:],
        z_inv.shape[1:],
    ]
    types = [bf16] * 6 + [f32] + [bf16] * 2
    smem = pl.BlockSpec(memory_space=pltpu.SMEM)
    vmem = pl.BlockSpec(memory_space=pltpu.VMEM)
    out = pl.pallas_call(
        functools.partial(tables_kernel, seg_count),
        in_specs=[smem] * 4 + [vmem] * 2 + [anywhere] * len(after),
        out_specs=[smem] + [vmem] * 9,
        out_shape=[jax.ShapeDtypeStruct(out_shapes[0], jnp.int32)]
        + [array_of(s, t) for s, t in zip(out_shapes[1:], types)],
        compiler_params=params,
        cost_estimate=cost(costs["tables"]),
        name="tables",
    )(ids, box_sizes, holder, partner.reshape(part_count, item_count), z_fwd, z_inv, *after)
    names = ("x", "x_back", "y", "y_back", "face", "place", "squares", "z", "z_back")
    return out[0], dict(zip(names, out[1:]))


def factors(squares, plane, z_total):
    ratio_z = jnp.full(squares.shape, plane).astype(f32) * (1.0 / z_total)
    halved = squares + ratio_z * ratio_z * half_phase
    ratio = sine_ratio(halved, 8)
    source = (time_step**2 * ratio) * ratio
    return 2.0 - (4.0 / time_step**2) * (halved * source), source


def parcel_shapes(whole_shape, part_shape, count, parts, paired):
    near = array_of((2,) + whole_shape if paired else whole_shape)
    return [array_of(whole_shape), near] + [array_of(part_shape)] * (
        (count - 2) * parts
    )


def near_spec(shape, which, index):
    if which is None:
        return pl.BlockSpec(shape, index)
    return pl.BlockSpec((None,) + shape, lambda *a: (which,) + index(*a))


def parcel_of(out, parts):
    return [out[0], out[1]] + [out[i : i + parts] for i in range(2, len(out), parts)]


def array_in(block):
    return block[0] if isinstance(block, tuple) else block


def block_spec(block, shape, index):
    if isinstance(block, tuple):
        return pl.BlockSpec((None,) + shape, lambda *a: (block[1],) + index(*a))
    return pl.BlockSpec(shape, index)


def z_forward_kernel(count, parts, after, me_ref, field_ref, table_ref, *refs):
    out_refs = refs[after:]
    block, y_cells, z_cells = field_ref.shape
    width = z_cells // count
    part = width // parts
    modes = times(field_ref[...].reshape(block * y_cells, z_cells), table_ref[0])
    for x in range(block):
        turned = modes[x * y_cells : (x + 1) * y_cells].T
        out_refs[0][x] = turned[:width]
        out_refs[1][x] = turned[width : 2 * width]
        for i, ref in enumerate(out_refs[2:]):
            start = 2 * width + i * part
            ref[x] = turned[start : start + part]


def z_forward(field, me, tables, count, parts, after, key, which=None):
    size, y_cells, z_cells = field.shape
    width = z_cells // count
    part = width // parts
    rest = (count - 2) * parts
    block = min(8, size)
    out = pl.pallas_call(
        functools.partial(z_forward_kernel, count, parts, len(after)),
        grid_spec=pltpu.PrefetchScalarGridSpec(
            num_scalar_prefetch=1,
            grid=(size // block,),
            in_specs=[
                pl.BlockSpec((block, y_cells, z_cells), lambda i, me: (i, 0, 0)),
                pl.BlockSpec((1,) + tables.shape[1:], lambda i, me: (me[0], 0, 0)),
            ]
            + [anywhere] * len(after),
            out_specs=[
                pl.BlockSpec((block, width, y_cells), lambda i, me: (i, 0, 0)),
                near_spec((block, width, y_cells), which, lambda i, me: (i, 0, 0)),
            ]
            + [pl.BlockSpec((block, part, y_cells), lambda i, me: (i, 0, 0))] * rest,
        ),
        out_shape=parcel_shapes(
            (size, width, y_cells), (size, part, y_cells), count, parts, which is not None
        ),
        compiler_params=params,
        cost_estimate=cost(costs[key]),
        name="z_forward",
    )(me, field, tables, *after)
    return parcel_of(out, parts)


def plane_forward(block_refs, y_table, x_table):
    planes = block_refs[0].shape[1]
    value = jnp.concatenate([ref[...] for ref in block_refs], axis=0)
    x_cells, _, y_cells = value.shape
    value = jnp.swapaxes(value, 0, 1).reshape(planes * x_cells, y_cells)
    value = flip(times(value, y_table), planes)
    return times(value, x_table)


def store_faces(step, total, forced, face_table, rows_ref):
    planes = len(forced)
    for j, value in enumerate(forced):
        both = jnp.dot(
            face_table, jnp.concatenate(split(value), axis=0), preferred_element_type=f32
        )
        rows = both[:padded_rows] + both[padded_rows:]
        rows_ref[pl.ds(step * planes + j, padded_rows, stride=total), :] = rows


def send_faces(rows, x_table, face_refs):
    value = times(rows, x_table).T
    x_local = face_refs[0].shape[0]
    for k, ref in enumerate(face_refs):
        ref[...] = value[k * x_local : (k + 1) * x_local]


def first_kernel(count, last, offset, z_total, me_ref, *refs):
    blocks, refs = refs[:count], refs[count:]
    squares_ref, y_ref, x_ref, face_ref = refs[:4]
    spectral = plane_forward(blocks, y_ref[...], x_ref[...])
    if not last:
        out_ref, rows_ref = refs[-2:]
    else:
        x_back_ref, before_ref = refs[4:6]
        out_ref, face_refs, rows_ref = refs[-2 - count], refs[-1 - count : -1], refs[-1]
    planes, y_modes, x_modes = out_ref.shape
    total = rows_ref.shape[0] // padded_rows
    first = me_ref[1] + offset + pl.program_id(0) * planes
    forced = []
    for j in range(planes):
        mine = spectral[j * y_modes : (j + 1) * y_modes]
        wave, source = factors(squares_ref[...], first + j, z_total)
        out_ref[j] = wave * mine
        forced.append(source * mine)
    store_faces(pl.program_id(0), total, forced, face_ref[...], rows_ref)
    if last:

        @pl.when(pl.program_id(0) == pl.num_programs(0) - 1)
        def _():
            rows = jnp.concatenate([before_ref[...], rows_ref[...]], axis=0)
            send_faces(rows, x_back_ref[...], face_refs)


def difference_kernel(count, *refs):
    blocks = refs[:count]
    waved_ref, y_ref, x_ref, out_ref = refs[count : count + 3] + refs[-1:]
    spectral = plane_forward(blocks, y_ref[...], x_ref[...])
    out_ref[...] = waved_ref[...] - spectral.reshape(waved_ref.shape)


def second_kernel(count, z_total, me_ref, *refs):
    sums, refs = refs[:count], refs[count:]
    partial_ref, squares_ref, x_ref, x_back_ref, y_back_ref, face_ref, place_ref = refs[:7]
    out_refs, face_refs = refs[7 : 7 + count], refs[7 + count : 7 + 2 * count]
    rows_ref, terms_ref = refs[7 + 2 * count :]
    step = pl.program_id(0)
    planes = partial_ref.shape[0]
    total = rows_ref.shape[0] // padded_rows

    @pl.when(step == 0)
    def _():
        value = jnp.concatenate([lanes_of(sums, r, 1) for r in range(padded_rows)], axis=0)
        terms_ref[...] = times(value, x_ref[...])

    waved, forced = [], []
    for j in range(planes):
        rows = terms_ref[pl.ds(step * planes + j, padded_rows, stride=total), :]
        high = rows.astype(bf16).astype(f32)
        low = rows - high
        stack = jnp.concatenate([high, low, high, jnp.zeros_like(rows)], axis=0).astype(bf16)
        added = jnp.dot(place_ref[...], stack, preferred_element_type=f32)
        mine = partial_ref[j] + added
        wave, source = factors(squares_ref[...], me_ref[1] + step * planes + j, z_total)
        waved.append(wave * mine)
        forced.append(source * mine)
    store_faces(step, total, forced, face_ref[...], rows_ref)
    store_cells(waved, x_back_ref[...], y_back_ref[...], out_refs)

    @pl.when(step == pl.num_programs(0) - 1)
    def _():
        send_faces(rows_ref[...], x_back_ref[...], face_refs)


def store_cells(waved, x_table, y_table, out_refs):
    planes = len(waved)
    value = times(jnp.concatenate(waved, axis=0), x_table)
    value = times(flip(value, planes), y_table)
    value = value.reshape(planes, value.shape[0] // planes, value.shape[1])
    value = jnp.swapaxes(value, 0, 1)
    x_local = out_refs[0].shape[0]
    for k, ref in enumerate(out_refs):
        ref[...] = value[k * x_local : (k + 1) * x_local]


def inverse_kernel(count, waved_ref, x_ref, y_ref, pair_ref, *out_refs):
    waved = [waved_ref[j] for j in range(waved_ref.shape[0])]
    store_cells(waved, x_ref[...], y_ref[...], out_refs)


def whole(shape):
    zeros = (0,) * len(shape)
    return pl.BlockSpec(shape, lambda i, *s: zeros)


def plane_specs(blocks, planes=None, first=0):
    specs = []
    for b in blocks:
        x_cells, held, y_cells = array_in(b).shape[-3:]
        start = first if held == planes else 0
        specs.append(
            block_spec(
                b, (x_cells, plane_block, y_cells), lambda i, *s, start=start: (0, start + i, 0)
            )
        )
    return specs


def mode_spec(shape, first=0):
    return pl.BlockSpec((plane_block,) + shape[1:], lambda i, *s: (first + i, 0, 0))


def first_part(blocks, place, tabs, before, after, key):
    count = len(blocks)
    x_local, own, _ = array_in(blocks[-1]).shape
    planes = array_in(blocks[0]).shape[1]
    y_modes, x_modes = tabs["squares"].shape
    small = [tabs["squares"], tabs["y"], tabs["x"], tabs["face"]]
    last = before is not None
    offset = planes - own if last else 0
    shape = (planes, y_modes, x_modes)
    operands = [place, *map(array_in, blocks), *small]
    in_specs = plane_specs(blocks, planes, offset // plane_block) + [whole(t.shape) for t in small]
    rows_shape = (padded_rows * own, x_modes)
    out_specs = [mode_spec(shape, offset // plane_block)]
    out_shape = [array_of(shape)]
    scratch, aliases = [], {}
    if last:
        waved, rows = before
        operands += [tabs["x_back"], rows, waved]
        in_specs += [whole(tabs["x_back"].shape), whole(rows.shape), anywhere]
        aliases = {len(operands) - 1: 0}
        face_shape = (x_local, padded_rows * planes)
        out_specs += [whole(face_shape)] * count
        out_shape += [array_of(face_shape)] * count
        scratch = [pltpu.VMEM(rows_shape, f32)]
    else:
        out_specs += [whole(rows_shape)]
        out_shape += [array_of(rows_shape)]
    operands += after
    in_specs += [anywhere] * len(after)
    out = pl.pallas_call(
        functools.partial(first_kernel, count, last, offset, planes * count),
        grid_spec=pltpu.PrefetchScalarGridSpec(
            num_scalar_prefetch=1,
            grid=(own // plane_block,),
            in_specs=in_specs,
            out_specs=out_specs,
            scratch_shapes=scratch,
        ),
        out_shape=out_shape,
        input_output_aliases=aliases,
        compiler_params=params,
        cost_estimate=cost(costs[key]),
        name="first_modes",
    )(*operands)
    return out[0], out[1:] if last else out[1]


def difference_part(blocks, waved, tabs, after):
    count = len(blocks)
    small = [tabs["y"], tabs["x"]]
    return pl.pallas_call(
        functools.partial(difference_kernel, count),
        grid=(waved.shape[0] // plane_block,),
        in_specs=plane_specs(blocks)
        + [mode_spec(waved.shape)]
        + [whole(t.shape) for t in small]
        + [anywhere] * len(after),
        out_specs=mode_spec(waved.shape),
        out_shape=array_of(waved.shape),
        compiler_params=params,
        cost_estimate=cost(costs["later"]),
        name="later_modes",
    )(*map(array_in, blocks), waved, *small, *after)


def second_part(sums, partial, place, tabs):
    count = len(sums)
    planes, y_modes, x_modes = partial.shape
    y_cells = tabs["y_back"].shape[1] // 2
    x_local = x_modes // count
    face_shape = (x_local, padded_rows * planes)
    shape = (x_local, planes, y_cells)
    small = [tabs[n] for n in ("squares", "x", "x_back", "y_back", "face", "place")]
    out = pl.pallas_call(
        functools.partial(second_kernel, count, planes * count),
        grid_spec=pltpu.PrefetchScalarGridSpec(
            num_scalar_prefetch=1,
            grid=(planes // plane_block,),
            in_specs=[whole(s.shape) for s in sums]
            + [mode_spec(partial.shape)]
            + [whole(t.shape) for t in small],
            out_specs=[pl.BlockSpec((x_local, plane_block, y_cells), lambda i, *s: (0, i, 0))]
            * count
            + [whole(face_shape)] * count,
            scratch_shapes=[
                pltpu.VMEM((padded_rows * planes, x_modes), f32),
                pltpu.VMEM((padded_rows * planes, x_modes), f32),
            ],
        ),
        out_shape=[array_of(shape)] * count + [array_of(face_shape)] * count,
        compiler_params=params,
        cost_estimate=cost(costs["second"]),
        name="second_modes",
    )(place, *sums, partial, *small)
    return out[:count], out[count:]


def inverse_part(waved, tabs, count, key, pair):
    planes, y_modes, x_modes = waved.shape
    y_cells = tabs["y_back"].shape[1] // 2
    x_local = x_modes // count
    small = [tabs["x_back"], tabs["y_back"]]
    shape = (x_local, plane_block, y_cells)
    out = pl.pallas_call(
        functools.partial(inverse_kernel, count),
        grid=(planes // plane_block,),
        in_specs=[mode_spec(waved.shape)] + [whole(t.shape) for t in small] + [anywhere],
        out_specs=[pl.BlockSpec(shape, lambda i: (0, i, 0))]
        + [near_spec(shape, 1, lambda i: (0, i, 0))]
        + [pl.BlockSpec(shape, lambda i: (0, i, 0))] * (count - 2),
        out_shape=parcel_shapes(
            (x_local, planes, y_cells), (x_local, planes, y_cells), count, 1, True
        ),
        input_output_aliases={3: 1},
        compiler_params=params,
        cost_estimate=cost(costs[key]),
        name="modes_to_cells",
    )(waved, *small, pair)
    return list(out)


def strips_kernel(count, seg_count, parts, scalars_ref, *refs):
    faces, table_ref, (own_ref, send_ref) = refs[:count], refs[count], refs[-2:]
    rows, x_local, z_cells = own_ref.shape
    value = jnp.concatenate([lanes_of(faces, r, parts) for r in range(rows)], axis=0)
    value = times(value, table_ref[...]).reshape(rows, x_local, z_cells)
    own_ref[...] = value
    seg_cells = z_cells // seg_count
    groups = z_cells // seg_cells
    lane = lax.broadcasted_iota(jnp.int32, (8, z_cells), 1) // seg_cells
    for item in range(2 * seg_count):
        face, seg = item // seg_count, item % seg_count
        dest, slot, wall = scalars_ref[1, item], scalars_ref[2, item], scalars_ref[5, item]

        @pl.when(wall == 0)
        def _():
            for j in range(3):
                packed = jnp.zeros((8, z_cells), f32)
                for c in range(groups):
                    piece = value[face * 3 + j, 8 * c : 8 * (c + 1)]
                    shift = (c - seg) * seg_cells % z_cells
                    if shift:
                        piece = pltpu.roll(piece, shift, 1)
                    packed = jnp.where(lane == c, piece, packed)
                send_ref[dest, slot, j] = packed


def strips_part(faces, scalars, tables, seg_count, part_count, parts, after, key):
    count = len(faces)
    x_local = faces[0].shape[0]
    z_cells = tables.shape[1] // 2
    own_shape = (face_rows, x_local, z_cells)
    send_shape = (part_count, pair_limit, 3, 8, z_cells)
    return pl.pallas_call(
        functools.partial(strips_kernel, count, seg_count, parts),
        grid_spec=pltpu.PrefetchScalarGridSpec(
            num_scalar_prefetch=1,
            grid=(1,),
            in_specs=[pl.BlockSpec(f.shape, lambda i, s: (0, 0)) for f in faces]
            + [pl.BlockSpec(tables.shape, lambda i, s: (0, 0))]
            + [anywhere] * len(after),
            out_specs=[
                pl.BlockSpec(own_shape, lambda i, s: (0, 0, 0)),
                pl.BlockSpec(send_shape, lambda i, s: (0, 0, 0, 0, 0)),
            ],
        ),
        out_shape=[array_of(own_shape), array_of(send_shape)],
        compiler_params=params,
        cost_estimate=cost(costs[key]),
        name="strips",
    )(scalars, *faces, tables, *after)


def coupled_terms(seg_count, scalars_ref, own_ref, got_ref):
    _, x_local, z_cells = own_ref.shape
    seg_cells = z_cells // seg_count
    groups = z_cells // seg_cells
    lane = lax.broadcasted_iota(jnp.int32, (8, z_cells), 1) // seg_cells
    row_x = scalars_ref[0, 3] + lax.broadcasted_iota(jnp.int32, (x_local, z_cells), 0)
    lane_all = lax.broadcasted_iota(jnp.int32, (x_local, z_cells), 1) // seg_cells
    terms = []
    for face in range(2):
        limit = jnp.zeros((x_local, z_cells), jnp.int32)
        other = [[jnp.zeros((8, z_cells), f32)] * groups for _ in range(3)]
        for seg in range(seg_count):
            item = face * seg_count + seg
            source, slot = scalars_ref[1, item], scalars_ref[3, item]
            limit = jnp.where(lane_all == seg, scalars_ref[4, item], limit)
            for j in range(3):
                packed = got_ref[source, slot, j]
                for c in range(groups):
                    shift = (seg - c) * seg_cells % z_cells
                    piece = pltpu.roll(packed, shift, 1) if shift else packed
                    other[j][c] = jnp.where(lane == seg, piece, other[j][c])
        other = [jnp.concatenate(o, axis=0) for o in other]
        own = [own_ref[face * 3 + j] for j in range(3)]
        low, high = (other, own) if face == 0 else (own, other)
        keep = row_x < limit
        for i in range(3):
            row = weights[3 + i] if face == 0 else weights[i]
            total = jnp.zeros((x_local, z_cells), f32)
            for j in range(6):
                if row[j] != 0:
                    total = total + float(row[j]) * (low + high)[j]
            terms.append(jnp.where(keep, total, 0.0))
    return terms


def couple_kernel(count, seg_count, skip, scalars_ref, own_ref, got_ref, table_ref, *out_refs):
    out_refs = out_refs[skip:]
    terms = coupled_terms(seg_count, scalars_ref, own_ref, got_ref)
    for r, term in enumerate(terms):
        out_refs[0][r] = term
    _, x_local, z_cells = own_ref.shape
    blank = [jnp.zeros((x_local, z_cells), f32)] * (padded_rows - len(terms))
    value = times(jnp.concatenate(terms + blank, axis=0), table_ref[...]).T
    width = z_cells // count
    for k in range(count):
        out_refs[1 + k][...] = value[k * width : (k + 1) * width]


def couple_part(own, got, scalars, tables, seg_count, count, after, key):
    rows, x_local, z_cells = own.shape
    sum_shape = (z_cells // count, padded_rows * x_local)
    out = pl.pallas_call(
        functools.partial(couple_kernel, count, seg_count, len(after)),
        grid_spec=pltpu.PrefetchScalarGridSpec(
            num_scalar_prefetch=1,
            grid=(1,),
            in_specs=[
                pl.BlockSpec(own.shape, lambda i, s: (0, 0, 0)),
                pl.BlockSpec(got.shape, lambda i, s: (0, 0, 0, 0, 0)),
                pl.BlockSpec(tables.shape, lambda i, s: (0, 0)),
            ]
            + [anywhere] * len(after),
            out_specs=[pl.BlockSpec(own.shape, lambda i, s: (0, 0, 0))]
            + [pl.BlockSpec(sum_shape, lambda i, s: (0, 0))] * count,
        ),
        out_shape=[array_of(own.shape)] + [array_of(sum_shape)] * count,
        compiler_params=params,
        cost_estimate=cost(costs[key]),
        name="couple",
    )(scalars, own, got, tables, *after)
    return out[0], out[1:]


def z_inverse_kernel(count, seg_count, scalars_ref, *refs):
    blocks, (earlier_ref, table_ref) = refs[:count], refs[count : count + 2]
    block, y_cells, z_cells = earlier_ref.shape
    len_x, len_y = scalars_ref[0, 1], scalars_ref[0, 2]
    step = pl.program_id(0)
    if seg_count:
        own_ref, got_ref = refs[count + 2 : count + 4]
        out_ref, terms_ref = refs[-2:]

        @pl.when(step == 0)
        def _():
            for r, term in enumerate(coupled_terms(seg_count, scalars_ref, own_ref, got_ref)):
                terms_ref[r] = term

    else:
        terms_ref, out_ref = refs[count + 2], refs[-1]
    first = scalars_ref[0, 3] + step * block
    row = lax.broadcasted_iota(jnp.int32, (y_cells, z_cells), 0)
    pieces = []
    for x in range(block):
        modes = jnp.concatenate([ref[x] for ref in blocks], axis=0)
        pieces.append(modes.T)
    value = times(jnp.concatenate(pieces, axis=0), table_ref[...])
    for x in range(block):
        limit = jnp.where(first + x < len_x, len_y, 0)
        out_ref[x] = value[x * y_cells : (x + 1) * y_cells] - jnp.where(
            row < limit, earlier_ref[x], 0.0
        )
    start = pl.multiple_of(jnp.minimum((len_y - 3) // 8 * 8, y_cells - 16), 8)
    mine = pl.ds(pl.multiple_of(step * block, block), block)
    terms = [terms_ref[r, mine][:, None, :] for r in range(face_rows)]
    low_row = lax.broadcasted_iota(jnp.int32, (block, 8, z_cells), 1)
    high_row = start + lax.broadcasted_iota(jnp.int32, (block, 16, z_cells), 1)
    low = out_ref[:, 0:8, :]
    for r in range(3):
        low = low + jnp.where(low_row == r, terms[r], 0.0)
    out_ref[:, 0:8, :] = low
    high = out_ref[:, pl.ds(start, 16), :]
    for r in range(3):
        high = high + jnp.where(high_row == len_y - 3 + r, terms[3 + r], 0.0)
    out_ref[:, pl.ds(start, 16), :] = high


def z_inverse(blocks, earlier, terms, scalars, tables, seg_count, key, after=()):
    count = len(blocks)
    x_local, y_cells, z_cells = earlier.shape
    width = z_cells // count
    block = min(8, x_local)
    given = len(terms) == 1
    operands = [scalars, *map(array_in, blocks), earlier, tables, *terms, *after]
    return pl.pallas_call(
        functools.partial(z_inverse_kernel, count, 0 if given else seg_count),
        grid_spec=pltpu.PrefetchScalarGridSpec(
            num_scalar_prefetch=1,
            grid=(x_local // block,),
            in_specs=[
                block_spec(b, (block, width, y_cells), lambda i, s: (i, 0, 0)) for b in blocks
            ]
            + [pl.BlockSpec((block, y_cells, z_cells), lambda i, s: (i, 0, 0))]
            + [whole(t.shape) for t in (tables, *terms)]
            + [anywhere] * len(after),
            out_specs=pl.BlockSpec((block, y_cells, z_cells), lambda i, s: (i, 0, 0)),
            scratch_shapes=[] if given else [pltpu.VMEM((face_rows, x_local, z_cells), f32)],
        ),
        out_shape=array_of(earlier.shape),
        compiler_params=params,
        cost_estimate=cost(costs[key]),
        name="z_inverse",
    )(*operands)


def gate_kernel(*refs):
    pass


def gated(array, after):
    return pl.pallas_call(
        gate_kernel,
        in_specs=[anywhere] * (1 + len(after)),
        out_specs=anywhere,
        out_shape=array_of(array.shape),
        input_output_aliases={0: 0},
        compiler_params=params,
        cost_estimate=cost(costs["gate"]),
        name="gate",
    )(array, *after)


def pairs_at(count, distance):
    return [(i, i ^ distance) for i in range(count)]


def send(block, distance):
    count = lax.axis_size("sub")
    return lax.ppermute(block, "sub", pairs_at(count, distance))


def exchange(blocks):
    return [blocks[0]] + [send(blocks[k], k) for k in range(1, len(blocks))]


def local(adj_next, adj_later, box_sizes, holder, partner):
    part_count = holder.shape[0]
    seg_count = partner.shape[2]
    my_group = lax.axis_index("grp").astype(jnp.int32)
    me = lax.axis_index("sub").astype(jnp.int32)
    count = lax.axis_size("sub")
    _, x_local, y_cells, z_cells = adj_next.shape
    x_total = x_local * count
    z_local = z_cells // count
    z_fwd, z_inv = (jnp.asarray(t) for t in z_tables(z_cells, count))
    place = jnp.stack([me, me * z_local])

    middle = count // 2
    parcel = z_forward(adj_next[0], place, z_fwd, count, 2, [], "forward_next")
    near = send(parcel[1], 1)
    first_a, first_b = (
        [parcel[0], near] + [send(parcel[k][c], k) for k in range(2, count)] for c in range(2)
    )

    ids = jnp.stack([me, my_group, jnp.int32(x_local)])
    scalars, tabs = make_tables(
        ids,
        box_sizes,
        holder,
        partner,
        (y_cells, x_total),
        z_fwd,
        z_inv,
        [parcel[0]],
    )
    later = z_forward(
        adj_later[0], place, z_fwd, count, 1, [tabs["squares"]], "forward_later", 0
    )
    pair = later[1]
    later = [later[0], None] + [b[0] for b in later[2:]]
    for k in range(2, middle + 1):
        later[k] = send(later[k], k)

    before = first_part(first_a, place, tabs, None, [later[0]], "first_a")
    waved, faces = first_part(first_b, place, tabs, before, [], "first_b")
    faces = exchange(faces)
    for k in range(middle + 1, count):
        later[k] = send(gated(later[k], [faces[1]]), k)
    back = inverse_part(waved, tabs, count, "back", pair)
    near = send(back[1], 1)
    later[1] = (near, 0)
    back[1] = (near, 1)
    own, outgoing = strips_part(
        faces,
        scalars,
        tabs["z_back"],
        seg_count,
        part_count,
        2,
        [back[0], *later[2 : middle + 1]],
        "strips_now",
    )
    for k in range(2, count):
        back[k] = send(gated(back[k], [outgoing]), k)
    got = lax.all_to_all(outgoing, "grp", 0, 0, tiled=True)
    partial = difference_part(later, waved, tabs, [outgoing])
    terms_now, sums = couple_part(
        own,
        got,
        scalars,
        tabs["z"],
        seg_count,
        count,
        [partial, *back[2 : middle + 1]],
        "couple_now",
    )
    last, faces = second_part(exchange(sums), partial, place, tabs)
    faces = exchange(faces)
    last = [last[0], None] + [send(last[k], k) for k in range(2, count)] + [last[1]]
    own, outgoing = strips_part(
        faces,
        scalars,
        tabs["z_back"],
        seg_count,
        part_count,
        1,
        [last[0], back[-1]],
        "strips_earlier",
    )
    last[1] = send(gated(last.pop(), [outgoing]), 1)
    got = lax.all_to_all(outgoing, "grp", 0, 0, tiled=True)
    adj_now = z_inverse(
        back,
        adj_later[0],
        [terms_now],
        scalars,
        tabs["z_back"],
        seg_count,
        "now",
        last[2 : middle + 1],
    )
    adj_earlier = z_inverse(
        last, adj_next[0], [own, got], scalars, tabs["z_back"], seg_count, "end", [adj_now]
    )
    return (adj_now[None], adj_earlier[None])


def solution(mesh):
    return jax.shard_map(
        local,
        mesh=mesh,
        in_specs=(P("grp", "sub", None, None), P("grp", "sub", None, None), P(), P(), P()),
        out_specs=(P("grp", "sub", None, None), P("grp", "sub", None, None)),
        check_vma=False,
    )
```

```python
import functools
import math

import jax
import jax.numpy as jnp
import numpy as np
from jax import lax
from jax.experimental import pallas as pl
from jax.experimental.pallas import tpu as pltpu
from jax.sharding import PartitionSpec as P

f32 = jnp.float32
bf16 = jnp.bfloat16
time_step = 0.5
half_phase = (math.pi * time_step / 2.0) ** 2
pair_limit = 3
face_rows = 6
padded_rows = 8
plane_block = 8
costs = {"forward_next": 2, "tables": 0, "forward_later": 8, "first_a": 8, "first_b": 32, "back": 10, "strips_now": 8, "later": 0, "couple_now": 8, "second": 16, "strips_earlier": 8, "now": 64, "end": 0, "gate": 0.0}
stencil = np.array(
    (
        (0, 0, -2, 2, 0, 0),
        (0, 2, -27, 27, -2, 0),
        (-2, 27, -270, 270, -27, 2),
        (2, -27, 270, -270, 27, -2),
        (0, -2, 27, -27, 2, 0),
        (0, 0, 2, -2, 0, 0),
    ),
    np.float32,
)
weights = np.transpose(stencil) / np.float32(180.0)
params = pltpu.CompilerParams(vmem_limit_bytes=64 * 2**20 - 65536)


anywhere = pl.BlockSpec(memory_space=pl.ANY)


def array_of(shape, dtype=f32):
    return jax.ShapeDtypeStruct(shape, dtype)


def cost(work):
    return pl.CostEstimate(flops=int(work * 1e9), bytes_accessed=1024, transcendentals=0)


def stacked_constant(table):
    high = table.astype(np.float32).astype(jnp.bfloat16)
    low = (table - high.astype(np.float64)).astype(np.float32).astype(jnp.bfloat16)
    row = np.concatenate([high, low], axis=1)
    return np.concatenate([row, row], axis=0)


def z_tables(z_cells, count):
    modes = np.arange(z_cells)[:, None]
    cells = np.arange(z_cells)[None, :]
    table = np.sqrt(np.where(modes == 0, 1.0, 2.0) / z_cells) * np.cos(
        np.pi * modes * (cells + 0.5) / z_cells
    )
    width = z_cells // count
    forward, inverse = [], []
    for me in range(count):
        order = np.concatenate([np.arange(width) + (me ^ k) * width for k in range(count)])
        mine = table[order]
        forward.append(stacked_constant(mine.T))
        inverse.append(stacked_constant(mine))
    return np.stack(forward), np.stack(inverse)


def split(value):
    high = value.astype(bf16)
    low = (value - high.astype(f32)).astype(bf16)
    return high, low


def times(value, table):
    product = jnp.dot(
        jnp.concatenate(split(value), axis=1), table, preferred_element_type=f32
    )
    width = product.shape[1] // 2
    return product[:, :width] + product[:, width:]


def flip(value, count):
    rows = value.shape[0] // count
    return jnp.concatenate([value[i * rows : (i + 1) * rows].T for i in range(count)], axis=0)


def lanes_of(refs, row, parts):
    pieces = []
    for ref in refs:
        width = ref.shape[1] // (parts * padded_rows)
        for c in range(parts):
            first = (c * padded_rows + row) * width
            pieces.append(ref[:, first : first + width])
    return jnp.concatenate(pieces, axis=1)


def sine_ratio(square, terms):
    total = jnp.full_like(square, (-1.0) ** (terms - 1) / math.factorial(2 * terms - 1))
    for n in reversed(range(terms - 1)):
        total = total * square + (-1.0) ** n / math.factorial(2 * n + 1)
    return total


def cosine_entries(modes, cells, length):
    extent = jnp.full(modes.shape, length).astype(f32)
    steps = (modes * (2 * cells + 1)).astype(f32)
    period = 4.0 * extent
    turns = steps - period * jnp.floor(steps / period)
    turns = jnp.where(turns < 0.0, turns + period, turns)
    turns = jnp.where(turns >= period, turns - period, turns)
    turns = jnp.minimum(turns, period - turns)
    angle = (extent - turns) * (f32(math.pi / 2) / extent)
    scaling = jnp.sqrt(jnp.where(modes == 0, 1.0, 2.0) / extent)
    inside = (modes < length) & (cells < length) & (cells >= 0)
    return jnp.where(inside, scaling * angle * sine_ratio(angle * angle, 9), 0.0)


def stacked(table):
    row = jnp.concatenate(split(table), axis=1)
    return jnp.concatenate([row, row], axis=0)


def links(seg_count, ids_ref, box_ref, holder_ref, partner_ref, scalars_ref):
    item_count = 2 * seg_count
    part_count = holder_ref.shape[0]
    me, group, x_local = ids_ref[0], ids_ref[1], ids_ref[2]

    def find(p, found):
        return jnp.where(holder_ref[p] == group, p, found)

    part = lax.fori_loop(0, part_count, find, jnp.int32(0))
    len_x, len_y = box_ref[part, 0], box_ref[part, 1]
    head = [me, len_x, len_y, me * x_local]
    mine = [partner_ref[part, i] for i in range(item_count)]
    peers = [jnp.where(m < 0, -1, lax.div(jnp.maximum(m, 0), seg_count)) for m in mine]
    for item in range(item_count):
        wall = mine[item] < 0
        peer = jnp.maximum(peers[item], 0)
        seg = lax.rem(jnp.maximum(mine[item], 0), seg_count)
        peer_item = (1 - item // seg_count) * seg_count + seg
        send_slot, get_slot = jnp.int32(0), jnp.int32(0)
        for i in range(item_count):
            if i < item:
                send_slot += jnp.where(peers[i] == peer, 1, 0)
            link = partner_ref[peer, i]
            back = jnp.where(link < 0, -1, lax.div(jnp.maximum(link, 0), seg_count))
            get_slot += jnp.where((back == part) & (i < peer_item), 1, 0)
        scalars_ref[0, item] = head[item] if item < len(head) else jnp.int32(0)
        scalars_ref[1, item] = jnp.where(wall, 0, holder_ref[peer])
        scalars_ref[2, item] = jnp.minimum(send_slot, pair_limit - 1)
        scalars_ref[3, item] = jnp.where(wall, 0, jnp.minimum(get_slot, pair_limit - 1))
        scalars_ref[4, item] = jnp.where(wall, 0, jnp.minimum(len_x, box_ref[peer, 0]))
        scalars_ref[5, item] = jnp.where(wall, 1, 0)
    return me, len_x, len_y


def tables_kernel(seg_count, ids_ref, box_ref, holder_ref, partner_ref, *refs):
    z_ref, z_back_ref = refs[:2]
    refs = refs[-10:]
    scalars_ref, x_ref, x_back_ref, y_ref, y_back_ref, face_ref, place_ref = refs[:7]
    squares_ref, my_z_ref, my_z_back_ref = refs[7:]
    my_z_ref[...] = z_ref[ids_ref[0]]
    my_z_back_ref[...] = z_back_ref[ids_ref[0]]
    y_cells, x_cells = squares_ref.shape
    me, len_x, len_y = links(seg_count, ids_ref, box_ref, holder_ref, partner_ref, scalars_ref)
    x_local = ids_ref[2]

    def index(shape, axis):
        return lax.broadcasted_iota(jnp.int32, shape, axis)

    def cells_x(axis):
        cell = index((x_cells, x_cells), axis)
        return (lax.div(cell, x_local) ^ me) * x_local + lax.rem(cell, x_local)

    square = (x_cells, x_cells)
    x_ref[...] = stacked(cosine_entries(index(square, 1), cells_x(0), len_x))
    x_back_ref[...] = stacked(cosine_entries(index(square, 0), cells_x(1), len_x))
    square = (y_cells, y_cells)
    y_ref[...] = stacked(cosine_entries(index(square, 1), index(square, 0), len_y))
    y_back_ref[...] = stacked(cosine_entries(index(square, 0), index(square, 1), len_y))

    def cell_rows(rows):
        return jnp.where(rows < 3, rows, jnp.where(rows < face_rows, len_y - face_rows + rows, -1))

    shape = (padded_rows, y_cells)
    face = cosine_entries(index(shape, 1), cell_rows(index(shape, 0)), len_y)
    high = face.astype(bf16).astype(f32)
    both = jnp.concatenate([high, face - high], axis=0)
    face_ref[...] = jnp.concatenate([both, both], axis=1).astype(bf16)
    shape = (y_cells, 4 * padded_rows)
    column = index(shape, 1)
    turned = cosine_entries(index(shape, 0), cell_rows(lax.rem(column, padded_rows)), len_y)
    high = turned.astype(bf16).astype(f32)
    part = jnp.where(column < 2 * padded_rows, high, turned - high)
    place_ref[...] = jnp.where(column < 3 * padded_rows, part, 0.0).astype(bf16)

    shape = (y_cells, x_cells)
    ratio_x = index(shape, 1).astype(f32) / jnp.full(shape, len_x).astype(f32)
    ratio_y = index(shape, 0).astype(f32) / jnp.full(shape, len_y).astype(f32)
    squares_ref[...] = (ratio_x * ratio_x + ratio_y * ratio_y) * half_phase


def make_tables(ids, box_sizes, holder, partner, shape, z_fwd, z_inv, after):
    y_cells, x_cells = shape
    part_count, _, seg_count = partner.shape
    item_count = 2 * seg_count
    out_shapes = [
        (6, item_count),
        (2 * x_cells, 2 * x_cells),
        (2 * x_cells, 2 * x_cells),
        (2 * y_cells, 2 * y_cells),
        (2 * y_cells, 2 * y_cells),
        (2 * padded_rows, 2 * y_cells),
        (y_cells, 4 * padded_rows),
        shape,
        z_fwd.shape[1:],
        z_inv.shape[1:],
    ]
    types = [bf16] * 6 + [f32] + [bf16] * 2
    smem = pl.BlockSpec(memory_space=pltpu.SMEM)
    vmem = pl.BlockSpec(memory_space=pltpu.VMEM)
    out = pl.pallas_call(
        functools.partial(tables_kernel, seg_count),
        in_specs=[smem] * 4 + [vmem] * 2 + [anywhere] * len(after),
        out_specs=[smem] + [vmem] * 9,
        out_shape=[jax.ShapeDtypeStruct(out_shapes[0], jnp.int32)]
        + [array_of(s, t) for s, t in zip(out_shapes[1:], types)],
        compiler_params=params,
        cost_estimate=cost(costs["tables"]),
        name="tables",
    )(ids, box_sizes, holder, partner.reshape(part_count, item_count), z_fwd, z_inv, *after)
    names = ("x", "x_back", "y", "y_back", "face", "place", "squares", "z", "z_back")
    return out[0], dict(zip(names, out[1:]))


def factors(squares, plane, z_total):
    ratio_z = jnp.full(squares.shape, plane).astype(f32) * (1.0 / z_total)
    halved = squares + ratio_z * ratio_z * half_phase
    ratio = sine_ratio(halved, 8)
    source = (time_step**2 * ratio) * ratio
    return 2.0 - (4.0 / time_step**2) * (halved * source), source


def parcel_shapes(whole_shape, part_shape, count, parts, paired):
    near = array_of((2,) + whole_shape if paired else whole_shape)
    return [array_of(whole_shape), near] + [array_of(part_shape)] * (
        (count - 2) * parts
    )


def near_spec(shape, which, index):
    if which is None:
        return pl.BlockSpec(shape, index)
    return pl.BlockSpec((None,) + shape, lambda *a: (which,) + index(*a))


def parcel_of(out, parts):
    return [out[0], out[1]] + [out[i : i + parts] for i in range(2, len(out), parts)]


def array_in(block):
    return block[0] if isinstance(block, tuple) else block


def block_spec(block, shape, index):
    if isinstance(block, tuple):
        return pl.BlockSpec((None,) + shape, lambda *a: (block[1],) + index(*a))
    return pl.BlockSpec(shape, index)


def z_forward_kernel(count, parts, after, me_ref, field_ref, table_ref, *refs):
    out_refs = refs[after:]
    block, y_cells, z_cells = field_ref.shape
    width = z_cells // count
    part = width // parts
    modes = times(field_ref[...].reshape(block * y_cells, z_cells), table_ref[0])
    for x in range(block):
        turned = modes[x * y_cells : (x + 1) * y_cells].T
        out_refs[0][x] = turned[:width]
        out_refs[1][x] = turned[width : 2 * width]
        for i, ref in enumerate(out_refs[2:]):
            start = 2 * width + i * part
            ref[x] = turned[start : start + part]


def z_forward(field, me, tables, count, parts, after, key, which=None):
    size, y_cells, z_cells = field.shape
    width = z_cells // count
    part = width // parts
    rest = (count - 2) * parts
    block = min(8, size)
    out = pl.pallas_call(
        functools.partial(z_forward_kernel, count, parts, len(after)),
        grid_spec=pltpu.PrefetchScalarGridSpec(
            num_scalar_prefetch=1,
            grid=(size // block,),
            in_specs=[
                pl.BlockSpec((block, y_cells, z_cells), lambda i, me: (i, 0, 0)),
                pl.BlockSpec((1,) + tables.shape[1:], lambda i, me: (me[0], 0, 0)),
            ]
            + [anywhere] * len(after),
            out_specs=[
                pl.BlockSpec((block, width, y_cells), lambda i, me: (i, 0, 0)),
                near_spec((block, width, y_cells), which, lambda i, me: (i, 0, 0)),
            ]
            + [pl.BlockSpec((block, part, y_cells), lambda i, me: (i, 0, 0))] * rest,
        ),
        out_shape=parcel_shapes(
            (size, width, y_cells), (size, part, y_cells), count, parts, which is not None
        ),
        compiler_params=params,
        cost_estimate=cost(costs[key]),
        name="z_forward",
    )(me, field, tables, *after)
    return parcel_of(out, parts)


def plane_forward(block_refs, y_table, x_table):
    planes = block_refs[0].shape[1]
    value = jnp.concatenate([ref[...] for ref in block_refs], axis=0)
    x_cells, _, y_cells = value.shape
    value = jnp.swapaxes(value, 0, 1).reshape(planes * x_cells, y_cells)
    value = flip(times(value, y_table), planes)
    return times(value, x_table)


def store_faces(step, total, forced, face_table, rows_ref):
    planes = len(forced)
    for j, value in enumerate(forced):
        both = jnp.dot(
            face_table, jnp.concatenate(split(value), axis=0), preferred_element_type=f32
        )
        rows = both[:padded_rows] + both[padded_rows:]
        rows_ref[pl.ds(step * planes + j, padded_rows, stride=total), :] = rows


def send_faces(rows, x_table, face_refs):
    value = times(rows, x_table).T
    x_local = face_refs[0].shape[0]
    for k, ref in enumerate(face_refs):
        ref[...] = value[k * x_local : (k + 1) * x_local]


def first_kernel(count, last, offset, z_total, me_ref, *refs):
    blocks, refs = refs[:count], refs[count:]
    squares_ref, y_ref, x_ref, face_ref = refs[:4]
    spectral = plane_forward(blocks, y_ref[...], x_ref[...])
    if not last:
        out_ref, rows_ref = refs[-2:]
    else:
        x_back_ref, before_ref = refs[4:6]
        out_ref, face_refs, rows_ref = refs[-2 - count], refs[-1 - count : -1], refs[-1]
    planes, y_modes, x_modes = out_ref.shape
    total = rows_ref.shape[0] // padded_rows
    first = me_ref[0] * (z_total // count) + offset + pl.program_id(0) * planes
    forced = []
    for j in range(planes):
        mine = spectral[j * y_modes : (j + 1) * y_modes]
        wave, source = factors(squares_ref[...], first + j, z_total)
        out_ref[j] = wave * mine
        forced.append(source * mine)
    store_faces(pl.program_id(0), total, forced, face_ref[...], rows_ref)
    if last:

        @pl.when(pl.program_id(0) == pl.num_programs(0) - 1)
        def _():
            rows = jnp.concatenate([before_ref[...], rows_ref[...]], axis=0)
            send_faces(rows, x_back_ref[...], face_refs)


def difference_kernel(count, *refs):
    blocks = refs[:count]
    waved_ref, y_ref, x_ref, out_ref = refs[count : count + 3] + refs[-1:]
    spectral = plane_forward(blocks, y_ref[...], x_ref[...])
    out_ref[...] = waved_ref[...] - spectral.reshape(waved_ref.shape)


def second_kernel(count, z_total, me_ref, *refs):
    sums, refs = refs[:count], refs[count:]
    partial_ref, squares_ref, x_ref, x_back_ref, y_back_ref, face_ref, place_ref = refs[:7]
    out_refs, face_refs = refs[7 : 7 + count], refs[7 + count : 7 + 2 * count]
    rows_ref, terms_ref = refs[7 + 2 * count :]
    step = pl.program_id(0)
    planes = partial_ref.shape[0]
    total = rows_ref.shape[0] // padded_rows

    @pl.when(step == 0)
    def _():
        value = jnp.concatenate([lanes_of(sums, r, 1) for r in range(padded_rows)], axis=0)
        terms_ref[...] = times(value, x_ref[...])

    waved, forced = [], []
    for j in range(planes):
        rows = terms_ref[pl.ds(step * planes + j, padded_rows, stride=total), :]
        high = rows.astype(bf16).astype(f32)
        low = rows - high
        stack = jnp.concatenate([high, low, high, jnp.zeros_like(rows)], axis=0).astype(bf16)
        added = jnp.dot(place_ref[...], stack, preferred_element_type=f32)
        mine = partial_ref[j] + added
        wave, source = factors(squares_ref[...], me_ref[0] * total + step * planes + j, z_total)
        waved.append(wave * mine)
        forced.append(source * mine)
    store_faces(step, total, forced, face_ref[...], rows_ref)
    store_cells(waved, x_back_ref[...], y_back_ref[...], out_refs)

    @pl.when(step == pl.num_programs(0) - 1)
    def _():
        send_faces(rows_ref[...], x_back_ref[...], face_refs)


def store_cells(waved, x_table, y_table, out_refs):
    planes = len(waved)
    value = times(jnp.concatenate(waved, axis=0), x_table)
    value = times(flip(value, planes), y_table)
    value = value.reshape(planes, value.shape[0] // planes, value.shape[1])
    value = jnp.swapaxes(value, 0, 1)
    x_local = out_refs[0].shape[0]
    for k, ref in enumerate(out_refs):
        ref[...] = value[k * x_local : (k + 1) * x_local]


def inverse_kernel(count, waved_ref, x_ref, y_ref, pair_ref, *out_refs):
    waved = [waved_ref[j] for j in range(waved_ref.shape[0])]
    store_cells(waved, x_ref[...], y_ref[...], out_refs)


def whole(shape):
    zeros = (0,) * len(shape)
    return pl.BlockSpec(shape, lambda i, *s: zeros)


def plane_specs(blocks, planes=None, first=0):
    specs = []
    for b in blocks:
        x_cells, held, y_cells = array_in(b).shape[-3:]
        start = first if held == planes else 0
        specs.append(
            block_spec(
                b, (x_cells, plane_block, y_cells), lambda i, *s, start=start: (0, start + i, 0)
            )
        )
    return specs


def mode_spec(shape, first=0):
    return pl.BlockSpec((plane_block,) + shape[1:], lambda i, *s: (first + i, 0, 0))


def first_part(blocks, place, tabs, before, after, key):
    count = len(blocks)
    x_local, own, _ = array_in(blocks[-1]).shape
    planes = array_in(blocks[0]).shape[1]
    y_modes, x_modes = tabs["squares"].shape
    small = [tabs["squares"], tabs["y"], tabs["x"], tabs["face"]]
    last = before is not None
    offset = planes - own if last else 0
    shape = (planes, y_modes, x_modes)
    operands = [place, *map(array_in, blocks), *small]
    in_specs = plane_specs(blocks, planes, offset // plane_block) + [whole(t.shape) for t in small]
    rows_shape = (padded_rows * own, x_modes)
    out_specs = [mode_spec(shape, offset // plane_block)]
    out_shape = [array_of(shape)]
    scratch, aliases = [], {}
    if last:
        waved, rows = before
        operands += [tabs["x_back"], rows, waved]
        in_specs += [whole(tabs["x_back"].shape), whole(rows.shape), anywhere]
        aliases = {len(operands) - 1: 0}
        face_shape = (x_local, padded_rows * planes)
        out_specs += [whole(face_shape)] * count
        out_shape += [array_of(face_shape)] * count
        scratch = [pltpu.VMEM(rows_shape, f32)]
    else:
        out_specs += [whole(rows_shape)]
        out_shape += [array_of(rows_shape)]
    operands += after
    in_specs += [anywhere] * len(after)
    out = pl.pallas_call(
        functools.partial(first_kernel, count, last, offset, planes * count),
        grid_spec=pltpu.PrefetchScalarGridSpec(
            num_scalar_prefetch=1,
            grid=(own // plane_block,),
            in_specs=in_specs,
            out_specs=out_specs,
            scratch_shapes=scratch,
        ),
        out_shape=out_shape,
        input_output_aliases=aliases,
        compiler_params=params,
        cost_estimate=cost(costs[key]),
        name="first_modes",
    )(*operands)
    return out[0], out[1:] if last else out[1]


def difference_part(blocks, waved, tabs, after):
    count = len(blocks)
    small = [tabs["y"], tabs["x"]]
    return pl.pallas_call(
        functools.partial(difference_kernel, count),
        grid=(waved.shape[0] // plane_block,),
        in_specs=plane_specs(blocks)
        + [mode_spec(waved.shape)]
        + [whole(t.shape) for t in small]
        + [anywhere] * len(after),
        out_specs=mode_spec(waved.shape),
        out_shape=array_of(waved.shape),
        compiler_params=params,
        cost_estimate=cost(costs["later"]),
        name="later_modes",
    )(*map(array_in, blocks), waved, *small, *after)


def second_part(sums, partial, place, tabs):
    count = len(sums)
    planes, y_modes, x_modes = partial.shape
    y_cells = tabs["y_back"].shape[1] // 2
    x_local = x_modes // count
    face_shape = (x_local, padded_rows * planes)
    shape = (x_local, planes, y_cells)
    small = [tabs[n] for n in ("squares", "x", "x_back", "y_back", "face", "place")]
    out = pl.pallas_call(
        functools.partial(second_kernel, count, planes * count),
        grid_spec=pltpu.PrefetchScalarGridSpec(
            num_scalar_prefetch=1,
            grid=(planes // plane_block,),
            in_specs=[whole(s.shape) for s in sums]
            + [mode_spec(partial.shape)]
            + [whole(t.shape) for t in small],
            out_specs=[pl.BlockSpec((x_local, plane_block, y_cells), lambda i, *s: (0, i, 0))]
            * count
            + [whole(face_shape)] * count,
            scratch_shapes=[
                pltpu.VMEM((padded_rows * planes, x_modes), f32),
                pltpu.VMEM((padded_rows * planes, x_modes), f32),
            ],
        ),
        out_shape=[array_of(shape)] * count + [array_of(face_shape)] * count,
        compiler_params=params,
        cost_estimate=cost(costs["second"]),
        name="second_modes",
    )(place, *sums, partial, *small)
    return out[:count], out[count:]


def inverse_part(waved, tabs, count, key, pair):
    planes, y_modes, x_modes = waved.shape
    y_cells = tabs["y_back"].shape[1] // 2
    x_local = x_modes // count
    small = [tabs["x_back"], tabs["y_back"]]
    shape = (x_local, plane_block, y_cells)
    out = pl.pallas_call(
        functools.partial(inverse_kernel, count),
        grid=(planes // plane_block,),
        in_specs=[mode_spec(waved.shape)] + [whole(t.shape) for t in small] + [anywhere],
        out_specs=[pl.BlockSpec(shape, lambda i: (0, i, 0))]
        + [near_spec(shape, 1, lambda i: (0, i, 0))]
        + [pl.BlockSpec(shape, lambda i: (0, i, 0))] * (count - 2),
        out_shape=parcel_shapes(
            (x_local, planes, y_cells), (x_local, planes, y_cells), count, 1, True
        ),
        input_output_aliases={3: 1},
        compiler_params=params,
        cost_estimate=cost(costs[key]),
        name="modes_to_cells",
    )(waved, *small, pair)
    return list(out)


def strips_kernel(count, seg_count, parts, scalars_ref, *refs):
    faces, table_ref, (own_ref, send_ref) = refs[:count], refs[count], refs[-2:]
    rows, x_local, z_cells = own_ref.shape
    value = jnp.concatenate([lanes_of(faces, r, parts) for r in range(rows)], axis=0)
    value = times(value, table_ref[...]).reshape(rows, x_local, z_cells)
    own_ref[...] = value
    seg_cells = z_cells // seg_count
    groups = z_cells // seg_cells
    lane = lax.broadcasted_iota(jnp.int32, (8, z_cells), 1) // seg_cells
    for item in range(2 * seg_count):
        face, seg = item // seg_count, item % seg_count
        dest, slot, wall = scalars_ref[1, item], scalars_ref[2, item], scalars_ref[5, item]

        @pl.when(wall == 0)
        def _():
            for j in range(3):
                packed = jnp.zeros((8, z_cells), f32)
                for c in range(groups):
                    piece = value[face * 3 + j, 8 * c : 8 * (c + 1)]
                    shift = (c - seg) * seg_cells % z_cells
                    if shift:
                        piece = pltpu.roll(piece, shift, 1)
                    packed = jnp.where(lane == c, piece, packed)
                send_ref[dest, slot, j] = packed


def strips_part(faces, scalars, tables, seg_count, part_count, parts, after, key):
    count = len(faces)
    x_local = faces[0].shape[0]
    z_cells = tables.shape[1] // 2
    own_shape = (face_rows, x_local, z_cells)
    send_shape = (part_count, pair_limit, 3, 8, z_cells)
    return pl.pallas_call(
        functools.partial(strips_kernel, count, seg_count, parts),
        grid_spec=pltpu.PrefetchScalarGridSpec(
            num_scalar_prefetch=1,
            grid=(1,),
            in_specs=[pl.BlockSpec(f.shape, lambda i, s: (0, 0)) for f in faces]
            + [pl.BlockSpec(tables.shape, lambda i, s: (0, 0))]
            + [anywhere] * len(after),
            out_specs=[
                pl.BlockSpec(own_shape, lambda i, s: (0, 0, 0)),
                pl.BlockSpec(send_shape, lambda i, s: (0, 0, 0, 0, 0)),
            ],
        ),
        out_shape=[array_of(own_shape), array_of(send_shape)],
        compiler_params=params,
        cost_estimate=cost(costs[key]),
        name="strips",
    )(scalars, *faces, tables, *after)


def coupled_terms(seg_count, scalars_ref, own_ref, got_ref):
    _, x_local, z_cells = own_ref.shape
    seg_cells = z_cells // seg_count
    groups = z_cells // seg_cells
    lane = lax.broadcasted_iota(jnp.int32, (8, z_cells), 1) // seg_cells
    row_x = scalars_ref[0, 3] + lax.broadcasted_iota(jnp.int32, (x_local, z_cells), 0)
    lane_all = lax.broadcasted_iota(jnp.int32, (x_local, z_cells), 1) // seg_cells
    terms = []
    for face in range(2):
        limit = jnp.zeros((x_local, z_cells), jnp.int32)
        other = [[jnp.zeros((8, z_cells), f32)] * groups for _ in range(3)]
        for seg in range(seg_count):
            item = face * seg_count + seg
            source, slot = scalars_ref[1, item], scalars_ref[3, item]
            limit = jnp.where(lane_all == seg, scalars_ref[4, item], limit)
            for j in range(3):
                packed = got_ref[source, slot, j]
                for c in range(groups):
                    shift = (seg - c) * seg_cells % z_cells
                    piece = pltpu.roll(packed, shift, 1) if shift else packed
                    other[j][c] = jnp.where(lane == seg, piece, other[j][c])
        other = [jnp.concatenate(o, axis=0) for o in other]
        own = [own_ref[face * 3 + j] for j in range(3)]
        low, high = (other, own) if face == 0 else (own, other)
        keep = row_x < limit
        for i in range(3):
            row = weights[3 + i] if face == 0 else weights[i]
            total = jnp.zeros((x_local, z_cells), f32)
            for j in range(6):
                if row[j] != 0:
                    total = total + float(row[j]) * (low + high)[j]
            terms.append(jnp.where(keep, total, 0.0))
    return terms


def couple_kernel(count, seg_count, skip, scalars_ref, own_ref, got_ref, table_ref, *out_refs):
    out_refs = out_refs[skip:]
    terms = coupled_terms(seg_count, scalars_ref, own_ref, got_ref)
    for r, term in enumerate(terms):
        out_refs[0][r] = term
    _, x_local, z_cells = own_ref.shape
    blank = [jnp.zeros((x_local, z_cells), f32)] * (padded_rows - len(terms))
    value = times(jnp.concatenate(terms + blank, axis=0), table_ref[...]).T
    width = z_cells // count
    for k in range(count):
        out_refs[1 + k][...] = value[k * width : (k + 1) * width]


def couple_part(own, got, scalars, tables, seg_count, count, after, key):
    rows, x_local, z_cells = own.shape
    sum_shape = (z_cells // count, padded_rows * x_local)
    out = pl.pallas_call(
        functools.partial(couple_kernel, count, seg_count, len(after)),
        grid_spec=pltpu.PrefetchScalarGridSpec(
            num_scalar_prefetch=1,
            grid=(1,),
            in_specs=[
                pl.BlockSpec(own.shape, lambda i, s: (0, 0, 0)),
                pl.BlockSpec(got.shape, lambda i, s: (0, 0, 0, 0, 0)),
                pl.BlockSpec(tables.shape, lambda i, s: (0, 0)),
            ]
            + [anywhere] * len(after),
            out_specs=[pl.BlockSpec(own.shape, lambda i, s: (0, 0, 0))]
            + [pl.BlockSpec(sum_shape, lambda i, s: (0, 0))] * count,
        ),
        out_shape=[array_of(own.shape)] + [array_of(sum_shape)] * count,
        compiler_params=params,
        cost_estimate=cost(costs[key]),
        name="couple",
    )(scalars, own, got, tables, *after)
    return out[0], out[1:]


def z_inverse_kernel(count, seg_count, scalars_ref, *refs):
    blocks, (earlier_ref, table_ref) = refs[:count], refs[count : count + 2]
    block, y_cells, z_cells = earlier_ref.shape
    len_x, len_y = scalars_ref[0, 1], scalars_ref[0, 2]
    step = pl.program_id(0)
    if seg_count:
        own_ref, got_ref = refs[count + 2 : count + 4]
        out_ref, terms_ref = refs[-2:]

        @pl.when(step == 0)
        def _():
            for r, term in enumerate(coupled_terms(seg_count, scalars_ref, own_ref, got_ref)):
                terms_ref[r] = term

    else:
        terms_ref, out_ref = refs[count + 2], refs[-1]
    first = scalars_ref[0, 3] + step * block
    row = lax.broadcasted_iota(jnp.int32, (y_cells, z_cells), 0)
    pieces = []
    for x in range(block):
        modes = jnp.concatenate([ref[x] for ref in blocks], axis=0)
        pieces.append(modes.T)
    value = times(jnp.concatenate(pieces, axis=0), table_ref[...])
    for x in range(block):
        limit = jnp.where(first + x < len_x, len_y, 0)
        out_ref[x] = value[x * y_cells : (x + 1) * y_cells] - jnp.where(
            row < limit, earlier_ref[x], 0.0
        )
    start = pl.multiple_of(jnp.minimum((len_y - 3) // 8 * 8, y_cells - 16), 8)
    mine = pl.ds(pl.multiple_of(step * block, block), block)
    terms = [terms_ref[r, mine][:, None, :] for r in range(face_rows)]
    low_row = lax.broadcasted_iota(jnp.int32, (block, 8, z_cells), 1)
    high_row = start + lax.broadcasted_iota(jnp.int32, (block, 16, z_cells), 1)
    low = out_ref[:, 0:8, :]
    for r in range(3):
        low = low + jnp.where(low_row == r, terms[r], 0.0)
    out_ref[:, 0:8, :] = low
    high = out_ref[:, pl.ds(start, 16), :]
    for r in range(3):
        high = high + jnp.where(high_row == len_y - 3 + r, terms[3 + r], 0.0)
    out_ref[:, pl.ds(start, 16), :] = high


def z_inverse(blocks, earlier, terms, scalars, tables, seg_count, key, after=()):
    count = len(blocks)
    x_local, y_cells, z_cells = earlier.shape
    width = z_cells // count
    block = min(8, x_local)
    given = len(terms) == 1
    operands = [scalars, *map(array_in, blocks), earlier, tables, *terms, *after]
    return pl.pallas_call(
        functools.partial(z_inverse_kernel, count, 0 if given else seg_count),
        grid_spec=pltpu.PrefetchScalarGridSpec(
            num_scalar_prefetch=1,
            grid=(x_local // block,),
            in_specs=[
                block_spec(b, (block, width, y_cells), lambda i, s: (i, 0, 0)) for b in blocks
            ]
            + [pl.BlockSpec((block, y_cells, z_cells), lambda i, s: (i, 0, 0))]
            + [whole(t.shape) for t in (tables, *terms)]
            + [anywhere] * len(after),
            out_specs=pl.BlockSpec((block, y_cells, z_cells), lambda i, s: (i, 0, 0)),
            scratch_shapes=[] if given else [pltpu.VMEM((face_rows, x_local, z_cells), f32)],
        ),
        out_shape=array_of(earlier.shape),
        compiler_params=params,
        cost_estimate=cost(costs[key]),
        name="z_inverse",
    )(*operands)


def gate_kernel(*refs):
    pass


def gated(array, after):
    return pl.pallas_call(
        gate_kernel,
        in_specs=[anywhere] * (1 + len(after)),
        out_specs=anywhere,
        out_shape=array_of(array.shape),
        input_output_aliases={0: 0},
        compiler_params=params,
        cost_estimate=cost(costs["gate"]),
        name="gate",
    )(array, *after)


def pairs_at(count, distance):
    return [(i, i ^ distance) for i in range(count)]


def send(block, distance):
    count = lax.axis_size("sub")
    return lax.ppermute(block, "sub", pairs_at(count, distance))


def exchange(blocks):
    return [blocks[0]] + [send(blocks[k], k) for k in range(1, len(blocks))]


def local(adj_next, adj_later, box_sizes, holder, partner):
    part_count = holder.shape[0]
    seg_count = partner.shape[2]
    my_group = lax.axis_index("grp").astype(jnp.int32)
    me = lax.axis_index("sub").astype(jnp.int32)
    count = lax.axis_size("sub")
    _, x_local, y_cells, z_cells = adj_next.shape
    x_total = x_local * count
    z_local = z_cells // count
    z_fwd, z_inv = (jnp.asarray(t) for t in z_tables(z_cells, count))
    place = me.reshape(1)

    middle = count // 2
    parcel = z_forward(adj_next[0], place, z_fwd, count, 2, [], "forward_next")
    near = send(parcel[1], 1)
    first_a, first_b = (
        [parcel[0], near] + [send(parcel[k][c], k) for k in range(2, count)] for c in range(2)
    )

    ids = jnp.stack([me, my_group, jnp.int32(x_local)])
    scalars, tabs = make_tables(
        ids,
        box_sizes,
        holder,
        partner,
        (y_cells, x_total),
        z_fwd,
        z_inv,
        [parcel[0]],
    )
    later = z_forward(
        adj_later[0], place, z_fwd, count, 1, [tabs["squares"]], "forward_later", 0
    )
    pair = later[1]
    later = [later[0], None] + [b[0] for b in later[2:]]
    for k in range(2, middle + 1):
        later[k] = send(later[k], k)

    before = first_part(first_a, place, tabs, None, [later[0]], "first_a")
    waved, faces = first_part(first_b, place, tabs, before, [], "first_b")
    faces = exchange(faces)
    for k in range(middle + 1, count):
        later[k] = send(gated(later[k], [faces[1]]), k)
    back = inverse_part(waved, tabs, count, "back", pair)
    near = send(back[1], 1)
    later[1] = (near, 0)
    back[1] = (near, 1)
    own, outgoing = strips_part(
        faces,
        scalars,
        tabs["z_back"],
        seg_count,
        part_count,
        2,
        [back[0], *later[2 : middle + 1]],
        "strips_now",
    )
    for k in range(2, count):
        back[k] = send(gated(back[k], [outgoing]), k)
    got = lax.all_to_all(outgoing, "grp", 0, 0, tiled=True)
    partial = difference_part(later, waved, tabs, [outgoing])
    terms_now, sums = couple_part(
        own,
        got,
        scalars,
        tabs["z"],
        seg_count,
        count,
        [partial, *back[2 : middle + 1]],
        "couple_now",
    )
    last, faces = second_part(exchange(sums), partial, place, tabs)
    faces = exchange(faces)
    last = [last[0], None] + [send(last[k], k) for k in range(2, count)] + [last[1]]
    own, outgoing = strips_part(
        faces,
        scalars,
        tabs["z_back"],
        seg_count,
        part_count,
        1,
        [last[0], back[-1]],
        "strips_earlier",
    )
    last[1] = send(gated(last.pop(), [outgoing]), 1)
    got = lax.all_to_all(outgoing, "grp", 0, 0, tiled=True)
    adj_now = z_inverse(
        back,
        adj_later[0],
        [terms_now],
        scalars,
        tabs["z_back"],
        seg_count,
        "now",
        last[2 : middle + 1],
    )
    adj_earlier = z_inverse(
        last, adj_next[0], [own, got], scalars, tabs["z_back"], seg_count, "end", [adj_now]
    )
    return (adj_now[None], adj_earlier[None])


def solution(mesh):
    return jax.shard_map(
        local,
        mesh=mesh,
        in_specs=(P("grp", "sub", None, None), P("grp", "sub", None, None), P(), P(), P()),
        out_specs=(P("grp", "sub", None, None), P("grp", "sub", None, None)),
        check_vma=False,
    )
```

```python
import functools
import math

import jax
import jax.numpy as jnp
import numpy as np
from jax import lax
from jax.experimental import pallas as pl
from jax.experimental.pallas import tpu as pltpu
from jax.sharding import PartitionSpec as P

f32 = jnp.float32
bf16 = jnp.bfloat16
time_step = 0.5
half_phase = (math.pi * time_step / 2.0) ** 2
pair_limit = 3
face_rows = 6
padded_rows = 8
plane_block = 16
x_block = 16
costs = {"lead": 0, "forward_next": 2, "tables": 32, "forward_later": 8, "first_a": 0, "first_b": 32, "back": 10, "strips_now": 8, "later": 0, "couple_now": 0, "second": 16, "strips_earlier": 8, "now": 2, "end": 1, "gate": 0.0}
stencil = np.array(
    (
        (0, 0, -2, 2, 0, 0),
        (0, 2, -27, 27, -2, 0),
        (-2, 27, -270, 270, -27, 2),
        (2, -27, 270, -270, 27, -2),
        (0, -2, 27, -27, 2, 0),
        (0, 0, 2, -2, 0, 0),
    ),
    np.float32,
)
weights = np.transpose(stencil) / np.float32(180.0)
params = pltpu.CompilerParams(vmem_limit_bytes=64 * 2**20 - 65536)


anywhere = pl.BlockSpec(memory_space=pl.ANY)


def array_of(shape, dtype=f32):
    return jax.ShapeDtypeStruct(shape, dtype)


def cost(work):
    return pl.CostEstimate(flops=int(work * 1e9), bytes_accessed=1024, transcendentals=0)


def stacked_constant(table):
    high = table.astype(np.float32).astype(jnp.bfloat16)
    low = (table - high.astype(np.float64)).astype(np.float32).astype(jnp.bfloat16)
    row = np.concatenate([high, low], axis=1)
    return np.concatenate([row, row], axis=0)


def z_tables(z_cells, count):
    modes = np.arange(z_cells)[:, None]
    cells = np.arange(z_cells)[None, :]
    table = np.sqrt(np.where(modes == 0, 1.0, 2.0) / z_cells) * np.cos(
        np.pi * modes * (cells + 0.5) / z_cells
    )
    width = z_cells // count
    forward, inverse = [], []
    for me in range(count):
        order = np.concatenate([np.arange(width) + (me ^ k) * width for k in range(count)])
        mine = table[order]
        forward.append(stacked_constant(mine.T))
        inverse.append(stacked_constant(mine))
    return np.stack(forward), np.stack(inverse)


def split(value):
    high = value.astype(bf16)
    low = (value - high.astype(f32)).astype(bf16)
    return high, low


def times(value, table):
    product = jnp.dot(
        jnp.concatenate(split(value), axis=1), table, preferred_element_type=f32
    )
    width = product.shape[1] // 2
    return product[:, :width] + product[:, width:]


def flip(value, count):
    rows = value.shape[0] // count
    return jnp.concatenate([value[i * rows : (i + 1) * rows].T for i in range(count)], axis=0)


def lanes_of(refs, row, parts):
    pieces = []
    for ref in refs:
        width = ref.shape[1] // (parts * padded_rows)
        for c in range(parts):
            first = (c * padded_rows + row) * width
            pieces.append(ref[:, first : first + width])
    return jnp.concatenate(pieces, axis=1)


def sine_ratio(square, terms):
    total = jnp.full_like(square, (-1.0) ** (terms - 1) / math.factorial(2 * terms - 1))
    for n in reversed(range(terms - 1)):
        total = total * square + (-1.0) ** n / math.factorial(2 * n + 1)
    return total


def cosine_entries(modes, cells, length):
    extent = jnp.full(modes.shape, length).astype(f32)
    steps = (modes * (2 * cells + 1)).astype(f32)
    period = 4.0 * extent
    turns = steps - period * jnp.floor(steps / period)
    turns = jnp.where(turns < 0.0, turns + period, turns)
    turns = jnp.where(turns >= period, turns - period, turns)
    turns = jnp.minimum(turns, period - turns)
    angle = (extent - turns) * (f32(math.pi / 2) / extent)
    scaling = jnp.sqrt(jnp.where(modes == 0, 1.0, 2.0) / extent)
    inside = (modes < length) & (cells < length) & (cells >= 0)
    return jnp.where(inside, scaling * angle * sine_ratio(angle * angle, 8), 0.0)


def stacked(table):
    row = jnp.concatenate(split(table), axis=1)
    return jnp.concatenate([row, row], axis=0)


def links(seg_count, ids_ref, box_ref, holder_ref, partner_ref, scalars_ref):
    item_count = 2 * seg_count
    part_count = holder_ref.shape[0]
    me, group, x_local = ids_ref[0], ids_ref[1], ids_ref[2]

    def find(p, found):
        return jnp.where(holder_ref[p] == group, p, found)

    part = lax.fori_loop(0, part_count, find, jnp.int32(0))
    len_x, len_y = box_ref[part, 0], box_ref[part, 1]
    head = [me, len_x, len_y, me * x_local]
    mine = [partner_ref[part, i] for i in range(item_count)]
    peers = [jnp.where(m < 0, -1, lax.div(jnp.maximum(m, 0), seg_count)) for m in mine]
    for item in range(item_count):
        wall = mine[item] < 0
        peer = jnp.maximum(peers[item], 0)
        seg = lax.rem(jnp.maximum(mine[item], 0), seg_count)
        peer_item = (1 - item // seg_count) * seg_count + seg
        send_slot, get_slot = jnp.int32(0), jnp.int32(0)
        for i in range(item_count):
            if i < item:
                send_slot += jnp.where(peers[i] == peer, 1, 0)
            link = partner_ref[peer, i]
            back = jnp.where(link < 0, -1, lax.div(jnp.maximum(link, 0), seg_count))
            get_slot += jnp.where((back == part) & (i < peer_item), 1, 0)
        scalars_ref[0, item] = head[item] if item < len(head) else jnp.int32(0)
        scalars_ref[1, item] = jnp.where(wall, 0, holder_ref[peer])
        scalars_ref[2, item] = jnp.minimum(send_slot, pair_limit - 1)
        scalars_ref[3, item] = jnp.where(wall, 0, jnp.minimum(get_slot, pair_limit - 1))
        scalars_ref[4, item] = jnp.where(wall, 0, jnp.minimum(len_x, box_ref[peer, 0]))
        scalars_ref[5, item] = jnp.where(wall, 1, 0)
    return me, len_x, len_y


def tables_kernel(seg_count, ids_ref, box_ref, holder_ref, partner_ref, *refs):
    z_ref, z_back_ref = refs[:2]
    refs = refs[-10:]
    scalars_ref, x_ref, x_back_ref, y_ref, y_back_ref, face_ref, place_ref = refs[:7]
    squares_ref, my_z_ref, my_z_back_ref = refs[7:]
    my_z_ref[...] = z_ref[ids_ref[0]]
    my_z_back_ref[...] = z_back_ref[ids_ref[0]]
    y_cells, x_cells = squares_ref.shape
    me, len_x, len_y = links(seg_count, ids_ref, box_ref, holder_ref, partner_ref, scalars_ref)
    x_local = ids_ref[2]

    def index(shape, axis):
        return lax.broadcasted_iota(jnp.int32, shape, axis)

    def cells_x(axis):
        cell = index((x_cells, x_cells), axis)
        return (lax.div(cell, x_local) ^ me) * x_local + lax.rem(cell, x_local)

    square = (x_cells, x_cells)
    x_ref[...] = stacked(cosine_entries(index(square, 1), cells_x(0), len_x))
    x_back_ref[...] = stacked(cosine_entries(index(square, 0), cells_x(1), len_x))
    square = (y_cells, y_cells)
    y_ref[...] = stacked(cosine_entries(index(square, 1), index(square, 0), len_y))
    y_back_ref[...] = stacked(cosine_entries(index(square, 0), index(square, 1), len_y))

    def cell_rows(rows):
        return jnp.where(rows < 3, rows, jnp.where(rows < face_rows, len_y - face_rows + rows, -1))

    shape = (padded_rows, y_cells)
    face = cosine_entries(index(shape, 1), cell_rows(index(shape, 0)), len_y)
    high = face.astype(bf16).astype(f32)
    both = jnp.concatenate([high, face - high], axis=0)
    face_ref[...] = jnp.concatenate([both, both], axis=1).astype(bf16)
    shape = (y_cells, 4 * padded_rows)
    column = index(shape, 1)
    turned = cosine_entries(index(shape, 0), cell_rows(lax.rem(column, padded_rows)), len_y)
    high = turned.astype(bf16).astype(f32)
    part = jnp.where(column < 2 * padded_rows, high, turned - high)
    place_ref[...] = jnp.where(column < 3 * padded_rows, part, 0.0).astype(bf16)

    shape = (y_cells, x_cells)
    ratio_x = index(shape, 1).astype(f32) / jnp.full(shape, len_x).astype(f32)
    ratio_y = index(shape, 0).astype(f32) / jnp.full(shape, len_y).astype(f32)
    squares_ref[...] = (ratio_x * ratio_x + ratio_y * ratio_y) * half_phase


def make_tables(ids, box_sizes, holder, partner, shape, z_fwd, z_inv, after):
    y_cells, x_cells = shape
    part_count, _, seg_count = partner.shape
    item_count = 2 * seg_count
    out_shapes = [
        (6, item_count),
        (2 * x_cells, 2 * x_cells),
        (2 * x_cells, 2 * x_cells),
        (2 * y_cells, 2 * y_cells),
        (2 * y_cells, 2 * y_cells),
        (2 * padded_rows, 2 * y_cells),
        (y_cells, 4 * padded_rows),
        shape,
        z_fwd.shape[1:],
        z_inv.shape[1:],
    ]
    types = [bf16] * 6 + [f32] + [bf16] * 2
    smem = pl.BlockSpec(memory_space=pltpu.SMEM)
    vmem = pl.BlockSpec(memory_space=pltpu.VMEM)
    out = pl.pallas_call(
        functools.partial(tables_kernel, seg_count),
        in_specs=[smem] * 4 + [vmem] * 2 + [anywhere] * len(after),
        out_specs=[smem] + [vmem] * 9,
        out_shape=[jax.ShapeDtypeStruct(out_shapes[0], jnp.int32)]
        + [array_of(s, t) for s, t in zip(out_shapes[1:], types)],
        compiler_params=params,
        cost_estimate=cost(costs["tables"]),
        name="tables",
    )(ids, box_sizes, holder, partner.reshape(part_count, item_count), z_fwd, z_inv, *after)
    names = ("x", "x_back", "y", "y_back", "face", "place", "squares", "z", "z_back")
    return out[0], dict(zip(names, out[1:]))


def factors(squares, plane, z_total):
    ratio_z = jnp.full(squares.shape, plane).astype(f32) * (1.0 / z_total)
    halved = squares + ratio_z * ratio_z * half_phase
    ratio = sine_ratio(halved, 6)
    source = (time_step**2 * ratio) * ratio
    return 2.0 - (4.0 / time_step**2) * (halved * source), source


def parcel_shapes(whole_shape, part_shape, count, parts, paired):
    near = array_of((2,) + whole_shape if paired else whole_shape)
    return [array_of(whole_shape), near] + [array_of(part_shape)] * (
        (count - 2) * parts
    )


def near_spec(shape, which, index):
    if which is None:
        return pl.BlockSpec(shape, index)
    return pl.BlockSpec((None,) + shape, lambda *a: (which,) + index(*a))


def parcel_of(out, parts):
    return [out[0], out[1]] + [out[i : i + parts] for i in range(2, len(out), parts)]


def array_in(block):
    return block[0] if isinstance(block, tuple) else block


def block_spec(block, shape, index):
    if isinstance(block, tuple):
        return pl.BlockSpec((None,) + shape, lambda *a: (block[1],) + index(*a))
    return pl.BlockSpec(shape, index)


def z_modes(field_ref, table_ref):
    block, y_cells, z_cells = field_ref.shape
    modes = times(field_ref[...].reshape(block * y_cells, z_cells), table_ref[0])
    return [modes[x * y_cells : (x + 1) * y_cells].T for x in range(block)]


def z_lead_kernel(count, me_ref, field_ref, table_ref, *out_refs):
    width = field_ref.shape[2] // count
    for x, turned in enumerate(z_modes(field_ref, table_ref)):
        for k in range(2, count):
            out_refs[k - 2][x] = turned[k * width : (k + 1) * width]


def z_forward_kernel(count, parts, after, me_ref, field_ref, table_ref, *refs):
    out_refs = refs[after:]
    width = field_ref.shape[2] // count
    part = width // parts
    for x, turned in enumerate(z_modes(field_ref, table_ref)):
        out_refs[0][x] = turned[:width]
        out_refs[1][x] = turned[width : 2 * width]
        for i, ref in enumerate(out_refs[2:]):
            start = 2 * width + i * part
            ref[x] = turned[start : start + part]


def z_in_specs(field, tables):
    _, y_cells, z_cells = field.shape
    return [
        pl.BlockSpec((x_block, y_cells, z_cells), lambda i, me: (i, 0, 0)),
        pl.BlockSpec((1,) + tables.shape[1:], lambda i, me: (me[0], 0, 0)),
    ]


def z_lead(field, me, tables, count):
    _, y_cells, z_cells = field.shape
    shape = (x_block, z_cells // count, y_cells)
    return pl.pallas_call(
        functools.partial(z_lead_kernel, count),
        grid_spec=pltpu.PrefetchScalarGridSpec(
            num_scalar_prefetch=1,
            grid=(1,),
            in_specs=z_in_specs(field, tables),
            out_specs=[pl.BlockSpec(shape, lambda i, me: (0, 0, 0))] * (count - 2),
        ),
        out_shape=[array_of(shape)] * (count - 2),
        compiler_params=params,
        cost_estimate=cost(costs["lead"]),
        name="z_lead",
    )(me, field, tables)


def z_forward(field, me, tables, count, parts, after, key, which=None, lead=0):
    size, y_cells, z_cells = field.shape
    width = z_cells // count
    part = width // parts
    rest = (count - 2) * parts
    far = size - lead * x_block
    out = pl.pallas_call(
        functools.partial(z_forward_kernel, count, parts, len(after)),
        grid_spec=pltpu.PrefetchScalarGridSpec(
            num_scalar_prefetch=1,
            grid=(size // x_block,),
            in_specs=z_in_specs(field, tables) + [anywhere] * len(after),
            out_specs=[
                pl.BlockSpec((x_block, width, y_cells), lambda i, me: (i, 0, 0)),
                near_spec((x_block, width, y_cells), which, lambda i, me: (i, 0, 0)),
            ]
            + [
                pl.BlockSpec(
                    (x_block, part, y_cells), lambda i, me: (jnp.maximum(i - lead, 0), 0, 0)
                )
            ]
            * rest,
        ),
        out_shape=parcel_shapes(
            (size, width, y_cells), (far, part, y_cells), count, parts, which is not None
        ),
        compiler_params=params,
        cost_estimate=cost(costs[key]),
        name="z_forward",
    )(me, field, tables, *after)
    return parcel_of(out, parts)


def plane_forward(block_refs, y_table, x_table):
    planes = block_refs[0].shape[1]
    value = jnp.concatenate([ref[...] for ref in block_refs], axis=0)
    x_cells, _, y_cells = value.shape
    value = jnp.swapaxes(value, 0, 1).reshape(planes * x_cells, y_cells)
    value = flip(times(value, y_table), planes)
    return times(value, x_table)


def store_faces(step, total, forced, face_table, rows_ref):
    planes = len(forced)
    for j, value in enumerate(forced):
        both = jnp.dot(
            face_table, jnp.concatenate(split(value), axis=0), preferred_element_type=f32
        )
        rows = both[:padded_rows] + both[padded_rows:]
        rows_ref[pl.ds(step * planes + j, padded_rows, stride=total), :] = rows


def send_faces(rows, x_table, face_refs):
    value = times(rows, x_table).T
    x_local = face_refs[0].shape[0]
    for k, ref in enumerate(face_refs):
        ref[...] = value[k * x_local : (k + 1) * x_local]


def first_kernel(count, held, last, offset, z_total, me_ref, *refs):
    blocks, refs = refs[:held], refs[held:]
    squares_ref, y_ref, x_ref, face_ref = refs[:4]
    spectral = plane_forward(blocks, y_ref[...], x_ref[...])
    if not last:
        out_ref, rows_ref = refs[-2:]
    else:
        x_back_ref, before_ref = refs[4:6]
        out_ref, face_refs, rows_ref = refs[-2 - count], refs[-1 - count : -1], refs[-1]
    planes, y_modes, x_modes = out_ref.shape
    total = rows_ref.shape[0] // padded_rows
    first = me_ref[0] * (z_total // count) + offset + pl.program_id(0) * planes
    forced = []
    for j in range(planes):
        mine = spectral[j * y_modes : (j + 1) * y_modes]
        wave, source = factors(squares_ref[...], first + j, z_total)
        out_ref[j] = wave * mine
        forced.append(source * mine)
    store_faces(pl.program_id(0), total, forced, face_ref[...], rows_ref)
    if last:

        @pl.when(pl.program_id(0) == pl.num_programs(0) - 1)
        def _():
            rows = jnp.concatenate([before_ref[...], rows_ref[...]], axis=0)
            send_faces(rows, x_back_ref[...], face_refs)


def difference_kernel(count, *refs):
    blocks = refs[:count]
    waved_ref, y_ref, x_ref, out_ref = refs[count : count + 3] + refs[-1:]
    spectral = plane_forward(blocks, y_ref[...], x_ref[...])
    out_ref[...] = waved_ref[...] - spectral.reshape(waved_ref.shape)


def second_kernel(count, skip, z_total, me_ref, *refs):
    sums, refs = refs[:count], refs[count:]
    partial_ref, squares_ref, x_ref, x_back_ref, y_back_ref, face_ref, place_ref = refs[:7]
    refs = refs[7 + skip :]
    out_refs, face_refs = refs[:count], refs[count : 2 * count]
    rows_ref, terms_ref = refs[2 * count :]
    step = pl.program_id(0)
    planes = partial_ref.shape[0]
    total = rows_ref.shape[0] // padded_rows

    @pl.when(step == 0)
    def _():
        value = jnp.concatenate([lanes_of(sums, r, 1) for r in range(padded_rows)], axis=0)
        terms_ref[...] = times(value, x_ref[...])

    waved, forced = [], []
    for j in range(planes):
        rows = terms_ref[pl.ds(step * planes + j, padded_rows, stride=total), :]
        high = rows.astype(bf16).astype(f32)
        low = rows - high
        stack = jnp.concatenate([high, low, high, jnp.zeros_like(rows)], axis=0).astype(bf16)
        added = jnp.dot(place_ref[...], stack, preferred_element_type=f32)
        mine = partial_ref[j] + added
        wave, source = factors(squares_ref[...], me_ref[0] * total + step * planes + j, z_total)
        waved.append(wave * mine)
        forced.append(source * mine)
    store_faces(step, total, forced, face_ref[...], rows_ref)
    store_cells(waved, x_back_ref[...], y_back_ref[...], out_refs)

    @pl.when(step == pl.num_programs(0) - 1)
    def _():
        send_faces(rows_ref[...], x_back_ref[...], face_refs)


def store_cells(waved, x_table, y_table, out_refs):
    planes = len(waved)
    value = times(jnp.concatenate(waved, axis=0), x_table)
    value = times(flip(value, planes), y_table)
    value = value.reshape(planes, value.shape[0] // planes, value.shape[1])
    value = jnp.swapaxes(value, 0, 1)
    x_local = out_refs[0].shape[0]
    for k, ref in enumerate(out_refs):
        ref[...] = value[k * x_local : (k + 1) * x_local]


def inverse_kernel(count, waved_ref, x_ref, y_ref, pair_ref, *out_refs):
    waved = [waved_ref[j] for j in range(waved_ref.shape[0])]
    store_cells(waved, x_ref[...], y_ref[...], out_refs)


def whole(shape):
    zeros = (0,) * len(shape)
    return pl.BlockSpec(shape, lambda i, *s: zeros)


def plane_specs(blocks, planes=None, first=0):
    specs = []
    for b in blocks:
        x_cells, held, y_cells = array_in(b).shape[-3:]
        start = first if held == planes else 0
        specs.append(
            block_spec(
                b, (x_cells, plane_block, y_cells), lambda i, *s, start=start: (0, start + i, 0)
            )
        )
    return specs


def mode_spec(shape, first=0):
    return pl.BlockSpec((plane_block,) + shape[1:], lambda i, *s: (first + i, 0, 0))


def first_part(blocks, place, tabs, before, after, key):
    own = blocks[-1].shape[1]
    x_local, planes, _ = blocks[0].shape
    y_modes, x_modes = tabs["squares"].shape
    small = [tabs["squares"], tabs["y"], tabs["x"], tabs["face"]]
    count = x_modes // x_local
    last = before is not None
    offset = planes - own if last else 0
    shape = (planes, y_modes, x_modes)
    operands = [place, *map(array_in, blocks), *small]
    in_specs = plane_specs(blocks, planes, offset // plane_block) + [whole(t.shape) for t in small]
    rows_shape = (padded_rows * own, x_modes)
    out_specs = [mode_spec(shape, offset // plane_block)]
    out_shape = [array_of(shape)]
    scratch, aliases = [], {}
    if last:
        waved, rows = before
        operands += [tabs["x_back"], rows, waved]
        in_specs += [whole(tabs["x_back"].shape), whole(rows.shape), anywhere]
        aliases = {len(operands) - 1: 0}
        face_shape = (x_local, padded_rows * planes)
        out_specs += [whole(face_shape)] * count
        out_shape += [array_of(face_shape)] * count
        scratch = [pltpu.VMEM(rows_shape, f32)]
    else:
        out_specs += [whole(rows_shape)]
        out_shape += [array_of(rows_shape)]
    operands += after
    in_specs += [anywhere] * len(after)
    out = pl.pallas_call(
        functools.partial(first_kernel, count, len(blocks), last, offset, planes * count),
        grid_spec=pltpu.PrefetchScalarGridSpec(
            num_scalar_prefetch=1,
            grid=(own // plane_block,),
            in_specs=in_specs,
            out_specs=out_specs,
            scratch_shapes=scratch,
        ),
        out_shape=out_shape,
        input_output_aliases=aliases,
        compiler_params=params,
        cost_estimate=cost(costs[key]),
        name="first_modes",
    )(*operands)
    return out[0], out[1:] if last else out[1]


def difference_part(blocks, waved, tabs, after):
    count = len(blocks)
    small = [tabs["y"], tabs["x"]]
    return pl.pallas_call(
        functools.partial(difference_kernel, count),
        grid=(waved.shape[0] // plane_block,),
        in_specs=plane_specs(blocks)
        + [mode_spec(waved.shape)]
        + [whole(t.shape) for t in small]
        + [anywhere] * len(after),
        out_specs=mode_spec(waved.shape),
        out_shape=array_of(waved.shape),
        compiler_params=params,
        cost_estimate=cost(costs["later"]),
        name="later_modes",
    )(*map(array_in, blocks), waved, *small, *after)


def second_part(sums, partial, place, tabs, after):
    count = len(sums)
    planes, y_modes, x_modes = partial.shape
    y_cells = tabs["y_back"].shape[1] // 2
    x_local = x_modes // count
    face_shape = (x_local, padded_rows * planes)
    shape = (x_local, planes, y_cells)
    small = [tabs[n] for n in ("squares", "x", "x_back", "y_back", "face", "place")]
    out = pl.pallas_call(
        functools.partial(second_kernel, count, len(after), planes * count),
        grid_spec=pltpu.PrefetchScalarGridSpec(
            num_scalar_prefetch=1,
            grid=(planes // plane_block,),
            in_specs=[whole(s.shape) for s in sums]
            + [mode_spec(partial.shape)]
            + [whole(t.shape) for t in small]
            + [anywhere] * len(after),
            out_specs=[pl.BlockSpec((x_local, plane_block, y_cells), lambda i, *s: (0, i, 0))]
            * count
            + [whole(face_shape)] * count,
            scratch_shapes=[
                pltpu.VMEM((padded_rows * planes, x_modes), f32),
                pltpu.VMEM((padded_rows * planes, x_modes), f32),
            ],
        ),
        out_shape=[array_of(shape)] * count + [array_of(face_shape)] * count,
        compiler_params=params,
        cost_estimate=cost(costs["second"]),
        name="second_modes",
    )(place, *sums, partial, *small, *after)
    return out[:count], out[count:]


def inverse_part(waved, tabs, count, key, pair):
    planes, y_modes, x_modes = waved.shape
    y_cells = tabs["y_back"].shape[1] // 2
    x_local = x_modes // count
    small = [tabs["x_back"], tabs["y_back"]]
    shape = (x_local, plane_block, y_cells)
    out = pl.pallas_call(
        functools.partial(inverse_kernel, count),
        grid=(planes // plane_block,),
        in_specs=[mode_spec(waved.shape)] + [whole(t.shape) for t in small] + [anywhere],
        out_specs=[pl.BlockSpec(shape, lambda i: (0, i, 0))]
        + [near_spec(shape, 1, lambda i: (0, i, 0))]
        + [pl.BlockSpec(shape, lambda i: (0, i, 0))] * (count - 2),
        out_shape=parcel_shapes(
            (x_local, planes, y_cells), (x_local, planes, y_cells), count, 1, True
        ),
        input_output_aliases={3: 1},
        compiler_params=params,
        cost_estimate=cost(costs[key]),
        name="modes_to_cells",
    )(waved, *small, pair)
    return list(out)


def strips_kernel(count, seg_count, parts, scalars_ref, *refs):
    faces, table_ref, (own_ref, send_ref) = refs[:count], refs[count], refs[-2:]
    rows, x_local, z_cells = own_ref.shape
    value = jnp.concatenate([lanes_of(faces, r, parts) for r in range(rows)], axis=0)
    value = times(value, table_ref[...]).reshape(rows, x_local, z_cells)
    own_ref[...] = value
    seg_cells = z_cells // seg_count
    groups = z_cells // seg_cells
    lane = lax.broadcasted_iota(jnp.int32, (8, z_cells), 1) // seg_cells
    for item in range(2 * seg_count):
        face, seg = item // seg_count, item % seg_count
        dest, slot, wall = scalars_ref[1, item], scalars_ref[2, item], scalars_ref[5, item]

        @pl.when(wall == 0)
        def _():
            for j in range(3):
                packed = jnp.zeros((8, z_cells), f32)
                for c in range(groups):
                    piece = value[face * 3 + j, 8 * c : 8 * (c + 1)]
                    shift = (c - seg) * seg_cells % z_cells
                    if shift:
                        piece = pltpu.roll(piece, shift, 1)
                    packed = jnp.where(lane == c, piece, packed)
                send_ref[dest, slot, j] = packed


def strips_part(faces, scalars, tables, seg_count, part_count, parts, after, key):
    count = len(faces)
    x_local = faces[0].shape[0]
    z_cells = tables.shape[1] // 2
    own_shape = (face_rows, x_local, z_cells)
    send_shape = (part_count, pair_limit, 3, 8, z_cells)
    return pl.pallas_call(
        functools.partial(strips_kernel, count, seg_count, parts),
        grid_spec=pltpu.PrefetchScalarGridSpec(
            num_scalar_prefetch=1,
            grid=(1,),
            in_specs=[pl.BlockSpec(f.shape, lambda i, s: (0, 0)) for f in faces]
            + [pl.BlockSpec(tables.shape, lambda i, s: (0, 0))]
            + [anywhere] * len(after),
            out_specs=[
                pl.BlockSpec(own_shape, lambda i, s: (0, 0, 0)),
                pl.BlockSpec(send_shape, lambda i, s: (0, 0, 0, 0, 0)),
            ],
        ),
        out_shape=[array_of(own_shape), array_of(send_shape)],
        compiler_params=params,
        cost_estimate=cost(costs[key]),
        name="strips",
    )(scalars, *faces, tables, *after)


def coupled_terms(seg_count, scalars_ref, own_ref, got_ref):
    _, x_local, z_cells = own_ref.shape
    seg_cells = z_cells // seg_count
    groups = z_cells // seg_cells
    lane = lax.broadcasted_iota(jnp.int32, (8, z_cells), 1) // seg_cells
    row_x = scalars_ref[0, 3] + lax.broadcasted_iota(jnp.int32, (x_local, z_cells), 0)
    lane_all = lax.broadcasted_iota(jnp.int32, (x_local, z_cells), 1) // seg_cells
    terms = []
    for face in range(2):
        limit = jnp.zeros((x_local, z_cells), jnp.int32)
        other = [[jnp.zeros((8, z_cells), f32)] * groups for _ in range(3)]
        for seg in range(seg_count):
            item = face * seg_count + seg
            source, slot = scalars_ref[1, item], scalars_ref[3, item]
            limit = jnp.where(lane_all == seg, scalars_ref[4, item], limit)
            for j in range(3):
                packed = got_ref[source, slot, j]
                for c in range(groups):
                    shift = (seg - c) * seg_cells % z_cells
                    piece = pltpu.roll(packed, shift, 1) if shift else packed
                    other[j][c] = jnp.where(lane == seg, piece, other[j][c])
        other = [jnp.concatenate(o, axis=0) for o in other]
        own = [own_ref[face * 3 + j] for j in range(3)]
        low, high = (other, own) if face == 0 else (own, other)
        keep = row_x < limit
        for i in range(3):
            row = weights[3 + i] if face == 0 else weights[i]
            total = jnp.zeros((x_local, z_cells), f32)
            for j in range(6):
                if row[j] != 0:
                    total = total + float(row[j]) * (low + high)[j]
            terms.append(jnp.where(keep, total, 0.0))
    return terms


def couple_kernel(count, seg_count, skip, scalars_ref, own_ref, got_ref, table_ref, *out_refs):
    out_refs = out_refs[skip:]
    terms = coupled_terms(seg_count, scalars_ref, own_ref, got_ref)
    for r, term in enumerate(terms):
        out_refs[0][r] = term
    _, x_local, z_cells = own_ref.shape
    blank = [jnp.zeros((x_local, z_cells), f32)] * (padded_rows - len(terms))
    value = times(jnp.concatenate(terms + blank, axis=0), table_ref[...]).T
    width = z_cells // count
    for k in range(count):
        out_refs[1 + k][...] = value[k * width : (k + 1) * width]


def couple_part(own, got, scalars, tables, seg_count, count, after, key):
    rows, x_local, z_cells = own.shape
    sum_shape = (z_cells // count, padded_rows * x_local)
    out = pl.pallas_call(
        functools.partial(couple_kernel, count, seg_count, len(after)),
        grid_spec=pltpu.PrefetchScalarGridSpec(
            num_scalar_prefetch=1,
            grid=(1,),
            in_specs=[
                pl.BlockSpec(own.shape, lambda i, s: (0, 0, 0)),
                pl.BlockSpec(got.shape, lambda i, s: (0, 0, 0, 0, 0)),
                pl.BlockSpec(tables.shape, lambda i, s: (0, 0)),
            ]
            + [anywhere] * len(after),
            out_specs=[pl.BlockSpec(own.shape, lambda i, s: (0, 0, 0))]
            + [pl.BlockSpec(sum_shape, lambda i, s: (0, 0))] * count,
        ),
        out_shape=[array_of(own.shape)] + [array_of(sum_shape)] * count,
        compiler_params=params,
        cost_estimate=cost(costs[key]),
        name="couple",
    )(scalars, own, got, tables, *after)
    return out[0], out[1:]


def z_inverse_kernel(count, seg_count, scalars_ref, *refs):
    blocks, (earlier_ref, table_ref) = refs[:count], refs[count : count + 2]
    block, y_cells, z_cells = earlier_ref.shape
    len_x, len_y = scalars_ref[0, 1], scalars_ref[0, 2]
    step = pl.program_id(0)
    if seg_count:
        own_ref, got_ref = refs[count + 2 : count + 4]
        out_ref, terms_ref = refs[-2:]

        @pl.when(step == 0)
        def _():
            for r, term in enumerate(coupled_terms(seg_count, scalars_ref, own_ref, got_ref)):
                terms_ref[r] = term

    else:
        terms_ref, out_ref = refs[count + 2], refs[-1]
    first = scalars_ref[0, 3] + step * block
    row = lax.broadcasted_iota(jnp.int32, (y_cells, z_cells), 0)
    pieces = []
    for x in range(block):
        modes = jnp.concatenate([ref[x] for ref in blocks], axis=0)
        pieces.append(modes.T)
    value = times(jnp.concatenate(pieces, axis=0), table_ref[...])
    for x in range(block):
        limit = jnp.where(first + x < len_x, len_y, 0)
        out_ref[x] = value[x * y_cells : (x + 1) * y_cells] - jnp.where(
            row < limit, earlier_ref[x], 0.0
        )
    start = pl.multiple_of(jnp.minimum((len_y - 3) // 8 * 8, y_cells - 16), 8)
    mine = pl.ds(pl.multiple_of(step * block, block), block)
    terms = [terms_ref[r, mine][:, None, :] for r in range(face_rows)]
    low_row = lax.broadcasted_iota(jnp.int32, (block, 8, z_cells), 1)
    high_row = start + lax.broadcasted_iota(jnp.int32, (block, 16, z_cells), 1)
    low = out_ref[:, 0:8, :]
    for r in range(3):
        low = low + jnp.where(low_row == r, terms[r], 0.0)
    out_ref[:, 0:8, :] = low
    high = out_ref[:, pl.ds(start, 16), :]
    for r in range(3):
        high = high + jnp.where(high_row == len_y - 3 + r, terms[3 + r], 0.0)
    out_ref[:, pl.ds(start, 16), :] = high


def z_inverse(blocks, earlier, terms, scalars, tables, seg_count, key, after=()):
    count = len(blocks)
    x_local, y_cells, z_cells = earlier.shape
    width = z_cells // count
    block = x_block
    given = len(terms) == 1
    operands = [scalars, *map(array_in, blocks), earlier, tables, *terms, *after]
    return pl.pallas_call(
        functools.partial(z_inverse_kernel, count, 0 if given else seg_count),
        grid_spec=pltpu.PrefetchScalarGridSpec(
            num_scalar_prefetch=1,
            grid=(x_local // block,),
            in_specs=[
                block_spec(b, (block, width, y_cells), lambda i, s: (i, 0, 0)) for b in blocks
            ]
            + [pl.BlockSpec((block, y_cells, z_cells), lambda i, s: (i, 0, 0))]
            + [whole(t.shape) for t in (tables, *terms)]
            + [anywhere] * len(after),
            out_specs=pl.BlockSpec((block, y_cells, z_cells), lambda i, s: (i, 0, 0)),
            scratch_shapes=[] if given else [pltpu.VMEM((face_rows, x_local, z_cells), f32)],
        ),
        out_shape=array_of(earlier.shape),
        compiler_params=params,
        cost_estimate=cost(costs[key]),
        name="z_inverse",
    )(*operands)


def gate_kernel(*refs):
    pass


def gated(array, after):
    return pl.pallas_call(
        gate_kernel,
        in_specs=[anywhere] * (1 + len(after)),
        out_specs=anywhere,
        out_shape=array_of(array.shape),
        input_output_aliases={0: 0},
        compiler_params=params,
        cost_estimate=cost(costs["gate"]),
        name="gate",
    )(array, *after)


def pairs_at(count, distance):
    return [(i, i ^ distance) for i in range(count)]


def send(block, distance):
    count = lax.axis_size("sub")
    return lax.ppermute(block, "sub", pairs_at(count, distance))


def exchange(blocks):
    return [blocks[0]] + [send(blocks[k], k) for k in range(1, len(blocks))]


def local(adj_next, adj_later, box_sizes, holder, partner):
    part_count = holder.shape[0]
    seg_count = partner.shape[2]
    my_group = lax.axis_index("grp").astype(jnp.int32)
    me = lax.axis_index("sub").astype(jnp.int32)
    count = lax.axis_size("sub")
    _, x_local, y_cells, z_cells = adj_next.shape
    x_total = x_local * count
    z_local = z_cells // count
    z_fwd, z_inv = (jnp.asarray(t) for t in z_tables(z_cells, count))
    place = me.reshape(1)

    middle = count // 2
    lead = z_lead(adj_next[0], place, z_fwd, count)
    parcel = z_forward(adj_next[0], place, z_fwd, count, 2, [lead[0]], "forward_next", lead=1)
    lead = [send(b, k) for k, b in enumerate(lead, 2)]
    first_a, first_b = [parcel[0], send(parcel[1], 1)], [parcel[0]]
    first_b.append(first_a[1])
    for c, blocks in enumerate((first_a, first_b)):
        for k in range(2, count):
            blocks += [lead[k - 2], send(parcel[k][c], k)]

    ids = jnp.stack([me, my_group, jnp.int32(x_local)])
    scalars, tabs = make_tables(
        ids,
        box_sizes,
        holder,
        partner,
        (y_cells, x_total),
        z_fwd,
        z_inv,
        [parcel[0]],
    )
    later = z_forward(
        adj_later[0], place, z_fwd, count, 1, [tabs["squares"]], "forward_later", 0
    )
    pair = later[1]
    later = [later[0], None] + [b[0] for b in later[2:]]
    for k in range(2, middle + 1):
        later[k] = send(later[k], k)

    before = first_part(first_a, place, tabs, None, [later[0]], "first_a")
    waved, faces = first_part(first_b, place, tabs, before, [], "first_b")
    faces = exchange(faces)
    for k in range(middle + 1, count):
        later[k] = send(gated(later[k], [faces[1]]), k)
    back = inverse_part(waved, tabs, count, "back", pair)
    near = send(back[1], 1)
    later[1] = (near, 0)
    back[1] = (near, 1)
    own, outgoing = strips_part(
        faces,
        scalars,
        tabs["z_back"],
        seg_count,
        part_count,
        2,
        [back[0], *later[2 : middle + 1]],
        "strips_now",
    )
    for k in range(2, count):
        back[k] = send(gated(back[k], [outgoing]), k)
    got = lax.all_to_all(outgoing, "grp", 0, 0, tiled=True)
    partial = difference_part(later, waved, tabs, [outgoing])
    terms_now, sums = couple_part(
        own,
        got,
        scalars,
        tabs["z"],
        seg_count,
        count,
        [partial],
        "couple_now",
    )
    last, faces = second_part(
        exchange(sums), partial, place, tabs, back[2 : middle + 1]
    )
    faces = exchange(faces)
    last = [last[0], None] + [send(last[k], k) for k in range(2, count)] + [last[1]]
    own, outgoing = strips_part(
        faces,
        scalars,
        tabs["z_back"],
        seg_count,
        part_count,
        1,
        [last[0], back[-1]],
        "strips_earlier",
    )
    last[1] = send(gated(last.pop(), [outgoing]), 1)
    got = lax.all_to_all(outgoing, "grp", 0, 0, tiled=True)
    adj_now = z_inverse(
        back,
        adj_later[0],
        [terms_now],
        scalars,
        tabs["z_back"],
        seg_count,
        "now",
        last[2 : middle + 1],
    )
    adj_earlier = z_inverse(
        last, adj_next[0], [own, got], scalars, tabs["z_back"], seg_count, "end", [adj_now]
    )
    return (adj_now[None], adj_earlier[None])


def solution(mesh):
    return jax.shard_map(
        local,
        mesh=mesh,
        in_specs=(P("grp", "sub", None, None), P("grp", "sub", None, None), P(), P(), P()),
        out_specs=(P("grp", "sub", None, None), P("grp", "sub", None, None)),
        check_vma=False,
    )
```

```python
import functools
import math

import jax
import jax.numpy as jnp
import numpy as np
from jax import lax
from jax.experimental import pallas as pl
from jax.experimental.pallas import tpu as pltpu
from jax.sharding import PartitionSpec as P

f32 = jnp.float32
bf16 = jnp.bfloat16
time_step = 0.5
half_phase = (math.pi * time_step / 2.0) ** 2
pair_limit = 3
face_rows = 6
padded_rows = 8
plane_block = 16
x_block = 16
costs = {"lead": 0, "forward_next": 2, "tables": 32, "forward_later": 8, "first_a": 0, "first_b": 32, "back": 10, "strips_now": 8, "later": 0, "couple_now": 0, "second": 16, "strips_earlier": 8, "now": 2, "end_a": 0, "end_b": 0, "gate": 0.0}
stencil = np.array(
    (
        (0, 0, -2, 2, 0, 0),
        (0, 2, -27, 27, -2, 0),
        (-2, 27, -270, 270, -27, 2),
        (2, -27, 270, -270, 27, -2),
        (0, -2, 27, -27, 2, 0),
        (0, 0, 2, -2, 0, 0),
    ),
    np.float32,
)
weights = np.transpose(stencil) / np.float32(180.0)
params = pltpu.CompilerParams(vmem_limit_bytes=64 * 2**20 - 65536)


anywhere = pl.BlockSpec(memory_space=pl.ANY)


def array_of(shape, dtype=f32):
    return jax.ShapeDtypeStruct(shape, dtype)


def cost(work):
    return pl.CostEstimate(flops=int(work * 1e9), bytes_accessed=1024, transcendentals=0)


def stacked_constant(table):
    high = table.astype(np.float32).astype(jnp.bfloat16)
    low = (table - high.astype(np.float64)).astype(np.float32).astype(jnp.bfloat16)
    row = np.concatenate([high, low], axis=1)
    return np.concatenate([row, row], axis=0)


def z_tables(z_cells, count):
    modes = np.arange(z_cells)[:, None]
    cells = np.arange(z_cells)[None, :]
    table = np.sqrt(np.where(modes == 0, 1.0, 2.0) / z_cells) * np.cos(
        np.pi * modes * (cells + 0.5) / z_cells
    )
    width = z_cells // count
    forward, inverse = [], []
    for me in range(count):
        order = np.concatenate([np.arange(width) + (me ^ k) * width for k in range(count)])
        mine = table[order]
        forward.append(stacked_constant(mine.T))
        inverse.append(stacked_constant(mine))
    return np.stack(forward), np.stack(inverse)


def split(value):
    high = value.astype(bf16)
    low = (value - high.astype(f32)).astype(bf16)
    return high, low


def times(value, table):
    product = jnp.dot(
        jnp.concatenate(split(value), axis=1), table, preferred_element_type=f32
    )
    width = product.shape[1] // 2
    return product[:, :width] + product[:, width:]


def flip(value, count):
    rows = value.shape[0] // count
    return jnp.concatenate([value[i * rows : (i + 1) * rows].T for i in range(count)], axis=0)


def packed(value):
    cells, width = value.shape[0], value.shape[1] // padded_rows
    rest = value[:, 4 * width : face_rows * width]
    rest = jnp.concatenate([rest[: cells // 2], rest[cells // 2 :]], axis=1)
    return jnp.concatenate([value[:, : 4 * width], rest], axis=0)


def packed_shape(cells, width):
    return cells + cells // 2, 4 * width


def lanes_of(refs, row):
    pieces = []
    for ref in refs:
        cells, width = ref.shape[0] * 2 // 3, ref.shape[1] // 4
        if row < 4:
            pieces.append(ref[:cells, row * width : (row + 1) * width])
        else:
            first = (row - 4) * width
            parts = [ref[cells:, s : s + width] for s in (first, first + 2 * width)]
            pieces.append(jnp.concatenate(parts, axis=0))
    return jnp.concatenate(pieces, axis=1)


def sine_ratio(square, terms):
    total = jnp.full_like(square, (-1.0) ** (terms - 1) / math.factorial(2 * terms - 1))
    for n in reversed(range(terms - 1)):
        total = total * square + (-1.0) ** n / math.factorial(2 * n + 1)
    return total


def cosine_entries(modes, cells, length):
    extent = jnp.full(modes.shape, length).astype(f32)
    steps = (modes * (2 * cells + 1)).astype(f32)
    period = 4.0 * extent
    turns = steps - period * jnp.floor(steps / period)
    turns = jnp.where(turns < 0.0, turns + period, turns)
    turns = jnp.where(turns >= period, turns - period, turns)
    turns = jnp.minimum(turns, period - turns)
    angle = (extent - turns) * (f32(math.pi / 2) / extent)
    scaling = jnp.sqrt(jnp.where(modes == 0, 1.0, 2.0) / extent)
    inside = (modes < length) & (cells < length) & (cells >= 0)
    return jnp.where(inside, scaling * angle * sine_ratio(angle * angle, 8), 0.0)


def stacked(table):
    row = jnp.concatenate(split(table), axis=1)
    return jnp.concatenate([row, row], axis=0)


def links(seg_count, ids_ref, box_ref, holder_ref, partner_ref, scalars_ref):
    item_count = 2 * seg_count
    part_count = holder_ref.shape[0]
    me, group, x_local = ids_ref[0], ids_ref[1], ids_ref[2]

    def find(p, found):
        return jnp.where(holder_ref[p] == group, p, found)

    part = lax.fori_loop(0, part_count, find, jnp.int32(0))
    len_x, len_y = box_ref[part, 0], box_ref[part, 1]
    head = [me, len_x, len_y, me * x_local]
    mine = [partner_ref[part, i] for i in range(item_count)]
    peers = [jnp.where(m < 0, -1, lax.div(jnp.maximum(m, 0), seg_count)) for m in mine]
    for item in range(item_count):
        wall = mine[item] < 0
        peer = jnp.maximum(peers[item], 0)
        seg = lax.rem(jnp.maximum(mine[item], 0), seg_count)
        peer_item = (1 - item // seg_count) * seg_count + seg
        send_slot, get_slot = jnp.int32(0), jnp.int32(0)
        for i in range(item_count):
            if i < item:
                send_slot += jnp.where(peers[i] == peer, 1, 0)
            link = partner_ref[peer, i]
            back = jnp.where(link < 0, -1, lax.div(jnp.maximum(link, 0), seg_count))
            get_slot += jnp.where((back == part) & (i < peer_item), 1, 0)
        scalars_ref[0, item] = head[item] if item < len(head) else jnp.int32(0)
        scalars_ref[1, item] = jnp.where(wall, 0, holder_ref[peer])
        scalars_ref[2, item] = jnp.minimum(send_slot, pair_limit - 1)
        scalars_ref[3, item] = jnp.where(wall, 0, jnp.minimum(get_slot, pair_limit - 1))
        scalars_ref[4, item] = jnp.where(wall, 0, jnp.minimum(len_x, box_ref[peer, 0]))
        scalars_ref[5, item] = jnp.where(wall, 1, 0)
    return me, len_x, len_y


def tables_kernel(seg_count, ids_ref, box_ref, holder_ref, partner_ref, *refs):
    z_ref, z_back_ref = refs[:2]
    refs = refs[-10:]
    scalars_ref, x_ref, x_back_ref, y_ref, y_back_ref, face_ref, place_ref = refs[:7]
    squares_ref, my_z_ref, my_z_back_ref = refs[7:]
    my_z_ref[...] = z_ref[ids_ref[0]]
    my_z_back_ref[...] = z_back_ref[ids_ref[0]]
    y_cells, x_cells = squares_ref.shape
    me, len_x, len_y = links(seg_count, ids_ref, box_ref, holder_ref, partner_ref, scalars_ref)
    x_local = ids_ref[2]

    def index(shape, axis):
        return lax.broadcasted_iota(jnp.int32, shape, axis)

    def cells_x(axis):
        cell = index((x_cells, x_cells), axis)
        return (lax.div(cell, x_local) ^ me) * x_local + lax.rem(cell, x_local)

    square = (x_cells, x_cells)
    x_ref[...] = stacked(cosine_entries(index(square, 1), cells_x(0), len_x))
    x_back_ref[...] = stacked(cosine_entries(index(square, 0), cells_x(1), len_x))
    square = (y_cells, y_cells)
    y_ref[...] = stacked(cosine_entries(index(square, 1), index(square, 0), len_y))
    y_back_ref[...] = stacked(cosine_entries(index(square, 0), index(square, 1), len_y))

    def cell_rows(rows):
        return jnp.where(rows < 3, rows, jnp.where(rows < face_rows, len_y - face_rows + rows, -1))

    shape = (padded_rows, y_cells)
    face = cosine_entries(index(shape, 1), cell_rows(index(shape, 0)), len_y)
    high = face.astype(bf16).astype(f32)
    both = jnp.concatenate([high, face - high], axis=0)
    face_ref[...] = jnp.concatenate([both, both], axis=1).astype(bf16)
    shape = (y_cells, 4 * padded_rows)
    column = index(shape, 1)
    turned = cosine_entries(index(shape, 0), cell_rows(lax.rem(column, padded_rows)), len_y)
    high = turned.astype(bf16).astype(f32)
    part = jnp.where(column < 2 * padded_rows, high, turned - high)
    place_ref[...] = jnp.where(column < 3 * padded_rows, part, 0.0).astype(bf16)

    shape = (y_cells, x_cells)
    ratio_x = index(shape, 1).astype(f32) / jnp.full(shape, len_x).astype(f32)
    ratio_y = index(shape, 0).astype(f32) / jnp.full(shape, len_y).astype(f32)
    squares_ref[...] = (ratio_x * ratio_x + ratio_y * ratio_y) * half_phase


def make_tables(ids, box_sizes, holder, partner, shape, z_fwd, z_inv, after):
    y_cells, x_cells = shape
    part_count, _, seg_count = partner.shape
    item_count = 2 * seg_count
    out_shapes = [
        (6, item_count),
        (2 * x_cells, 2 * x_cells),
        (2 * x_cells, 2 * x_cells),
        (2 * y_cells, 2 * y_cells),
        (2 * y_cells, 2 * y_cells),
        (2 * padded_rows, 2 * y_cells),
        (y_cells, 4 * padded_rows),
        shape,
        z_fwd.shape[1:],
        z_inv.shape[1:],
    ]
    types = [bf16] * 6 + [f32] + [bf16] * 2
    smem = pl.BlockSpec(memory_space=pltpu.SMEM)
    vmem = pl.BlockSpec(memory_space=pltpu.VMEM)
    out = pl.pallas_call(
        functools.partial(tables_kernel, seg_count),
        in_specs=[smem] * 4 + [vmem] * 2 + [anywhere] * len(after),
        out_specs=[smem] + [vmem] * 9,
        out_shape=[jax.ShapeDtypeStruct(out_shapes[0], jnp.int32)]
        + [array_of(s, t) for s, t in zip(out_shapes[1:], types)],
        compiler_params=params,
        cost_estimate=cost(costs["tables"]),
        name="tables",
    )(ids, box_sizes, holder, partner.reshape(part_count, item_count), z_fwd, z_inv, *after)
    names = ("x", "x_back", "y", "y_back", "face", "place", "squares", "z", "z_back")
    return out[0], dict(zip(names, out[1:]))


def factors(squares, plane, z_total):
    ratio_z = jnp.full(squares.shape, plane).astype(f32) * (1.0 / z_total)
    halved = squares + ratio_z * ratio_z * half_phase
    ratio = sine_ratio(halved, 6)
    source = (time_step**2 * ratio) * ratio
    return 2.0 - (4.0 / time_step**2) * (halved * source), source


def parcel_shapes(whole_shape, part_shape, count, parts, paired):
    near = array_of((2,) + whole_shape if paired else whole_shape)
    return [array_of(whole_shape), near] + [array_of(part_shape)] * (
        (count - 2) * parts
    )


def near_spec(shape, which, index):
    if which is None:
        return pl.BlockSpec(shape, index)
    return pl.BlockSpec((None,) + shape, lambda *a: (which,) + index(*a))


def parcel_of(out, parts):
    return [out[0], out[1]] + [out[i : i + parts] for i in range(2, len(out), parts)]


def array_in(block):
    return block[0] if isinstance(block, tuple) else block


def block_spec(block, shape, index):
    if isinstance(block, tuple):
        return pl.BlockSpec((None,) + shape, lambda *a: (block[1],) + index(*a))
    return pl.BlockSpec(shape, index)


def z_modes(field_ref, table_ref):
    block, y_cells, z_cells = field_ref.shape
    modes = times(field_ref[...].reshape(block * y_cells, z_cells), table_ref[0])
    return [modes[x * y_cells : (x + 1) * y_cells].T for x in range(block)]


def z_lead_kernel(count, me_ref, field_ref, table_ref, *out_refs):
    width = field_ref.shape[2] // count
    for x, turned in enumerate(z_modes(field_ref, table_ref)):
        for k in range(2, count):
            out_refs[k - 2][x] = turned[k * width : (k + 1) * width]


def z_forward_kernel(count, parts, after, me_ref, field_ref, table_ref, *refs):
    out_refs = refs[after:]
    width = field_ref.shape[2] // count
    part = width // parts
    for x, turned in enumerate(z_modes(field_ref, table_ref)):
        out_refs[0][x] = turned[:width]
        out_refs[1][x] = turned[width : 2 * width]
        for i, ref in enumerate(out_refs[2:]):
            start = 2 * width + i * part
            ref[x] = turned[start : start + part]


def z_in_specs(field, tables):
    _, y_cells, z_cells = field.shape
    return [
        pl.BlockSpec((x_block, y_cells, z_cells), lambda i, me: (i, 0, 0)),
        pl.BlockSpec((1,) + tables.shape[1:], lambda i, me: (me[0], 0, 0)),
    ]


def z_lead(field, me, tables, count):
    _, y_cells, z_cells = field.shape
    shape = (x_block, z_cells // count, y_cells)
    return pl.pallas_call(
        functools.partial(z_lead_kernel, count),
        grid_spec=pltpu.PrefetchScalarGridSpec(
            num_scalar_prefetch=1,
            grid=(1,),
            in_specs=z_in_specs(field, tables),
            out_specs=[pl.BlockSpec(shape, lambda i, me: (0, 0, 0))] * (count - 2),
        ),
        out_shape=[array_of(shape)] * (count - 2),
        compiler_params=params,
        cost_estimate=cost(costs["lead"]),
        name="z_lead",
    )(me, field, tables)


def z_forward(field, me, tables, count, parts, after, key, which=None, lead=0):
    size, y_cells, z_cells = field.shape
    width = z_cells // count
    part = width // parts
    rest = (count - 2) * parts
    far = size - lead * x_block
    out = pl.pallas_call(
        functools.partial(z_forward_kernel, count, parts, len(after)),
        grid_spec=pltpu.PrefetchScalarGridSpec(
            num_scalar_prefetch=1,
            grid=(size // x_block,),
            in_specs=z_in_specs(field, tables) + [anywhere] * len(after),
            out_specs=[
                pl.BlockSpec((x_block, width, y_cells), lambda i, me: (i, 0, 0)),
                near_spec((x_block, width, y_cells), which, lambda i, me: (i, 0, 0)),
            ]
            + [
                pl.BlockSpec(
                    (x_block, part, y_cells), lambda i, me: (jnp.maximum(i - lead, 0), 0, 0)
                )
            ]
            * rest,
        ),
        out_shape=parcel_shapes(
            (size, width, y_cells), (far, part, y_cells), count, parts, which is not None
        ),
        compiler_params=params,
        cost_estimate=cost(costs[key]),
        name="z_forward",
    )(me, field, tables, *after)
    return parcel_of(out, parts)


def plane_forward(block_refs, y_table, x_table):
    planes = block_refs[0].shape[1]
    value = jnp.concatenate([ref[...] for ref in block_refs], axis=0)
    x_cells, _, y_cells = value.shape
    value = jnp.swapaxes(value, 0, 1).reshape(planes * x_cells, y_cells)
    value = flip(times(value, y_table), planes)
    return times(value, x_table)


def store_faces(step, total, forced, face_table, rows_ref):
    planes = len(forced)
    for j, value in enumerate(forced):
        both = jnp.dot(
            face_table, jnp.concatenate(split(value), axis=0), preferred_element_type=f32
        )
        rows = both[:padded_rows] + both[padded_rows:]
        rows_ref[pl.ds(step * planes + j, padded_rows, stride=total), :] = rows


def send_faces(rows, x_table, face_refs):
    value = times(rows, x_table).T
    x_local = value.shape[0] // len(face_refs)
    for k, ref in enumerate(face_refs):
        ref[...] = packed(value[k * x_local : (k + 1) * x_local])


def first_kernel(count, held, last, offset, z_total, me_ref, *refs):
    blocks, refs = refs[:held], refs[held:]
    squares_ref, y_ref, x_ref, face_ref = refs[:4]
    spectral = plane_forward(blocks, y_ref[...], x_ref[...])
    if not last:
        out_ref, rows_ref = refs[-2:]
    else:
        x_back_ref, before_ref = refs[4:6]
        out_ref, face_refs, rows_ref = refs[-2 - count], refs[-1 - count : -1], refs[-1]
    planes, y_modes, x_modes = out_ref.shape
    total = rows_ref.shape[0] // padded_rows
    first = me_ref[0] * (z_total // count) + offset + pl.program_id(0) * planes
    forced = []
    for j in range(planes):
        mine = spectral[j * y_modes : (j + 1) * y_modes]
        wave, source = factors(squares_ref[...], first + j, z_total)
        out_ref[j] = wave * mine
        forced.append(source * mine)
    store_faces(pl.program_id(0), total, forced, face_ref[...], rows_ref)
    if last:

        @pl.when(pl.program_id(0) == pl.num_programs(0) - 1)
        def _():
            rows = []
            for r in range(padded_rows):
                rows += [ref[r * total : (r + 1) * total] for ref in (before_ref, rows_ref)]
            send_faces(jnp.concatenate(rows, axis=0), x_back_ref[...], face_refs)


def difference_kernel(count, *refs):
    blocks = refs[:count]
    waved_ref, y_ref, x_ref, out_ref = refs[count : count + 3] + refs[-1:]
    spectral = plane_forward(blocks, y_ref[...], x_ref[...])
    out_ref[...] = waved_ref[...] - spectral.reshape(waved_ref.shape)


def second_kernel(count, skip, z_total, me_ref, *refs):
    sums, refs = refs[:count], refs[count:]
    partial_ref, squares_ref, x_ref, x_back_ref, y_back_ref, face_ref, place_ref = refs[:7]
    refs = refs[7 + skip :]
    out_refs, face_refs = refs[: count + 1], refs[count + 1 : 2 * count + 1]
    rows_ref, terms_ref = refs[2 * count + 1 :]
    step = pl.program_id(0)
    planes = partial_ref.shape[0]
    total = rows_ref.shape[0] // padded_rows

    @pl.when(step == 0)
    def _():
        rows = [lanes_of(sums, r) for r in range(face_rows)]
        rows += [jnp.zeros_like(rows[0])] * (padded_rows - face_rows)
        terms_ref[...] = times(jnp.concatenate(rows, axis=0), x_ref[...])

    waved, forced = [], []
    for j in range(planes):
        rows = terms_ref[pl.ds(step * planes + j, padded_rows, stride=total), :]
        high = rows.astype(bf16).astype(f32)
        low = rows - high
        stack = jnp.concatenate([high, low, high, jnp.zeros_like(rows)], axis=0).astype(bf16)
        added = jnp.dot(place_ref[...], stack, preferred_element_type=f32)
        mine = partial_ref[j] + added
        wave, source = factors(squares_ref[...], me_ref[0] * total + step * planes + j, z_total)
        waved.append(wave * mine)
        forced.append(source * mine)
    store_faces(step, total, forced, face_ref[...], rows_ref)
    store_cells(waved, x_back_ref[...], y_back_ref[...], out_refs)

    @pl.when(step == pl.num_programs(0) - 1)
    def _():
        send_faces(rows_ref[...], x_back_ref[...], face_refs)


def store_cells(waved, x_table, y_table, out_refs):
    planes = len(waved)
    value = times(jnp.concatenate(waved, axis=0), x_table)
    value = times(flip(value, planes), y_table)
    value = value.reshape(planes, value.shape[0] // planes, value.shape[1])
    value = jnp.swapaxes(value, 0, 1)
    first = 0
    for ref in out_refs:
        ref[...] = value[first : first + ref.shape[0]]
        first += ref.shape[0]


def inverse_kernel(count, waved_ref, x_ref, y_ref, pair_ref, *out_refs):
    waved = [waved_ref[j] for j in range(waved_ref.shape[0])]
    store_cells(waved, x_ref[...], y_ref[...], out_refs)


def whole(shape):
    zeros = (0,) * len(shape)
    return pl.BlockSpec(shape, lambda i, *s: zeros)


def plane_specs(blocks, planes=None, first=0):
    specs = []
    for b in blocks:
        x_cells, held, y_cells = array_in(b).shape[-3:]
        start = first if held == planes else 0
        specs.append(
            block_spec(
                b, (x_cells, plane_block, y_cells), lambda i, *s, start=start: (0, start + i, 0)
            )
        )
    return specs


def mode_spec(shape, first=0):
    return pl.BlockSpec((plane_block,) + shape[1:], lambda i, *s: (first + i, 0, 0))


def first_part(blocks, place, tabs, before, after, key):
    own = blocks[-1].shape[1]
    x_local, planes, _ = blocks[0].shape
    y_modes, x_modes = tabs["squares"].shape
    small = [tabs["squares"], tabs["y"], tabs["x"], tabs["face"]]
    count = x_modes // x_local
    last = before is not None
    offset = planes - own if last else 0
    shape = (planes, y_modes, x_modes)
    operands = [place, *map(array_in, blocks), *small]
    in_specs = plane_specs(blocks, planes, offset // plane_block) + [whole(t.shape) for t in small]
    rows_shape = (padded_rows * own, x_modes)
    out_specs = [mode_spec(shape, offset // plane_block)]
    out_shape = [array_of(shape)]
    scratch, aliases = [], {}
    if last:
        waved, rows = before
        operands += [tabs["x_back"], rows, waved]
        in_specs += [whole(tabs["x_back"].shape), whole(rows.shape), anywhere]
        aliases = {len(operands) - 1: 0}
        face_shape = packed_shape(x_local, planes)
        out_specs += [whole(face_shape)] * count
        out_shape += [array_of(face_shape)] * count
        scratch = [pltpu.VMEM(rows_shape, f32)]
    else:
        out_specs += [whole(rows_shape)]
        out_shape += [array_of(rows_shape)]
    operands += after
    in_specs += [anywhere] * len(after)
    out = pl.pallas_call(
        functools.partial(first_kernel, count, len(blocks), last, offset, planes * count),
        grid_spec=pltpu.PrefetchScalarGridSpec(
            num_scalar_prefetch=1,
            grid=(own // plane_block,),
            in_specs=in_specs,
            out_specs=out_specs,
            scratch_shapes=scratch,
        ),
        out_shape=out_shape,
        input_output_aliases=aliases,
        compiler_params=params,
        cost_estimate=cost(costs[key]),
        name="first_modes",
    )(*operands)
    return out[0], out[1:] if last else out[1]


def difference_part(blocks, waved, tabs, after):
    count = len(blocks)
    small = [tabs["y"], tabs["x"]]
    return pl.pallas_call(
        functools.partial(difference_kernel, count),
        grid=(waved.shape[0] // plane_block,),
        in_specs=plane_specs(blocks)
        + [mode_spec(waved.shape)]
        + [whole(t.shape) for t in small]
        + [anywhere] * len(after),
        out_specs=mode_spec(waved.shape),
        out_shape=array_of(waved.shape),
        compiler_params=params,
        cost_estimate=cost(costs["later"]),
        name="later_modes",
    )(*map(array_in, blocks), waved, *small, *after)


def second_part(sums, partial, place, tabs, after):
    count = len(sums)
    planes, y_modes, x_modes = partial.shape
    y_cells = tabs["y_back"].shape[1] // 2
    x_local = x_modes // count
    face_shape = packed_shape(x_local, planes)
    sizes = [x_local] * (count - 1) + [x_local // 2] * 2
    small = [tabs[n] for n in ("squares", "x", "x_back", "y_back", "face", "place")]
    out = pl.pallas_call(
        functools.partial(second_kernel, count, len(after), planes * count),
        grid_spec=pltpu.PrefetchScalarGridSpec(
            num_scalar_prefetch=1,
            grid=(planes // plane_block,),
            in_specs=[whole(s.shape) for s in sums]
            + [mode_spec(partial.shape)]
            + [whole(t.shape) for t in small]
            + [anywhere] * len(after),
            out_specs=[
                pl.BlockSpec((n, plane_block, y_cells), lambda i, *s: (0, i, 0)) for n in sizes
            ]
            + [whole(face_shape)] * count,
            scratch_shapes=[
                pltpu.VMEM((padded_rows * planes, x_modes), f32),
                pltpu.VMEM((padded_rows * planes, x_modes), f32),
            ],
        ),
        out_shape=[array_of((n, planes, y_cells)) for n in sizes]
        + [array_of(face_shape)] * count,
        compiler_params=params,
        cost_estimate=cost(costs["second"]),
        name="second_modes",
    )(place, *sums, partial, *small, *after)
    return list(out[: count + 1]), out[count + 1 :]


def inverse_part(waved, tabs, count, key, pair):
    planes, y_modes, x_modes = waved.shape
    y_cells = tabs["y_back"].shape[1] // 2
    x_local = x_modes // count
    small = [tabs["x_back"], tabs["y_back"]]
    shape = (x_local, plane_block, y_cells)
    out = pl.pallas_call(
        functools.partial(inverse_kernel, count),
        grid=(planes // plane_block,),
        in_specs=[mode_spec(waved.shape)] + [whole(t.shape) for t in small] + [anywhere],
        out_specs=[pl.BlockSpec(shape, lambda i: (0, i, 0))]
        + [near_spec(shape, 1, lambda i: (0, i, 0))]
        + [pl.BlockSpec(shape, lambda i: (0, i, 0))] * (count - 2),
        out_shape=parcel_shapes(
            (x_local, planes, y_cells), (x_local, planes, y_cells), count, 1, True
        ),
        input_output_aliases={3: 1},
        compiler_params=params,
        cost_estimate=cost(costs[key]),
        name="modes_to_cells",
    )(waved, *small, pair)
    return list(out)


def strips_kernel(count, seg_count, scalars_ref, *refs):
    faces, table_ref, (own_ref, send_ref) = refs[:count], refs[count], refs[-2:]
    rows, x_local, z_cells = own_ref.shape
    value = jnp.concatenate([lanes_of(faces, r) for r in range(rows)], axis=0)
    value = times(value, table_ref[...]).reshape(rows, x_local, z_cells)
    own_ref[...] = value
    seg_cells = z_cells // seg_count
    groups = z_cells // seg_cells
    lane = lax.broadcasted_iota(jnp.int32, (8, z_cells), 1) // seg_cells
    for item in range(2 * seg_count):
        face, seg = item // seg_count, item % seg_count
        dest, slot, wall = scalars_ref[1, item], scalars_ref[2, item], scalars_ref[5, item]

        @pl.when(wall == 0)
        def _():
            for j in range(3):
                packed = jnp.zeros((8, z_cells), f32)
                for c in range(groups):
                    piece = value[face * 3 + j, 8 * c : 8 * (c + 1)]
                    shift = (c - seg) * seg_cells % z_cells
                    if shift:
                        piece = pltpu.roll(piece, shift, 1)
                    packed = jnp.where(lane == c, piece, packed)
                send_ref[dest, slot, j] = packed


def strips_part(faces, scalars, tables, seg_count, part_count, x_local, after, key):
    count = len(faces)
    z_cells = tables.shape[1] // 2
    own_shape = (face_rows, x_local, z_cells)
    send_shape = (part_count, pair_limit, 3, 8, z_cells)
    return pl.pallas_call(
        functools.partial(strips_kernel, count, seg_count),
        grid_spec=pltpu.PrefetchScalarGridSpec(
            num_scalar_prefetch=1,
            grid=(1,),
            in_specs=[pl.BlockSpec(f.shape, lambda i, s: (0, 0)) for f in faces]
            + [pl.BlockSpec(tables.shape, lambda i, s: (0, 0))]
            + [anywhere] * len(after),
            out_specs=[
                pl.BlockSpec(own_shape, lambda i, s: (0, 0, 0)),
                pl.BlockSpec(send_shape, lambda i, s: (0, 0, 0, 0, 0)),
            ],
        ),
        out_shape=[array_of(own_shape), array_of(send_shape)],
        compiler_params=params,
        cost_estimate=cost(costs[key]),
        name="strips",
    )(scalars, *faces, tables, *after)


def coupled_terms(seg_count, scalars_ref, own_ref, got_ref):
    _, x_local, z_cells = own_ref.shape
    seg_cells = z_cells // seg_count
    groups = z_cells // seg_cells
    lane = lax.broadcasted_iota(jnp.int32, (8, z_cells), 1) // seg_cells
    row_x = scalars_ref[0, 3] + lax.broadcasted_iota(jnp.int32, (x_local, z_cells), 0)
    lane_all = lax.broadcasted_iota(jnp.int32, (x_local, z_cells), 1) // seg_cells
    terms = []
    for face in range(2):
        limit = jnp.zeros((x_local, z_cells), jnp.int32)
        other = [[jnp.zeros((8, z_cells), f32)] * groups for _ in range(3)]
        for seg in range(seg_count):
            item = face * seg_count + seg
            source, slot = scalars_ref[1, item], scalars_ref[3, item]
            limit = jnp.where(lane_all == seg, scalars_ref[4, item], limit)
            for j in range(3):
                packed = got_ref[source, slot, j]
                for c in range(groups):
                    shift = (seg - c) * seg_cells % z_cells
                    piece = pltpu.roll(packed, shift, 1) if shift else packed
                    other[j][c] = jnp.where(lane == seg, piece, other[j][c])
        other = [jnp.concatenate(o, axis=0) for o in other]
        own = [own_ref[face * 3 + j] for j in range(3)]
        low, high = (other, own) if face == 0 else (own, other)
        keep = row_x < limit
        for i in range(3):
            row = weights[3 + i] if face == 0 else weights[i]
            total = jnp.zeros((x_local, z_cells), f32)
            for j in range(6):
                if row[j] != 0:
                    total = total + float(row[j]) * (low + high)[j]
            terms.append(jnp.where(keep, total, 0.0))
    return terms


def couple_kernel(count, seg_count, skip, scalars_ref, own_ref, got_ref, table_ref, *out_refs):
    out_refs = out_refs[skip:]
    terms = coupled_terms(seg_count, scalars_ref, own_ref, got_ref)
    for r, term in enumerate(terms):
        out_refs[0][r] = term
    _, x_local, z_cells = own_ref.shape
    blank = [jnp.zeros((x_local, z_cells), f32)] * (padded_rows - len(terms))
    value = times(jnp.concatenate(terms + blank, axis=0), table_ref[...]).T
    width = z_cells // count
    for k in range(count):
        out_refs[1 + k][...] = packed(value[k * width : (k + 1) * width])


def couple_part(own, got, scalars, tables, seg_count, count, after, key):
    rows, x_local, z_cells = own.shape
    sum_shape = packed_shape(z_cells // count, x_local)
    out = pl.pallas_call(
        functools.partial(couple_kernel, count, seg_count, len(after)),
        grid_spec=pltpu.PrefetchScalarGridSpec(
            num_scalar_prefetch=1,
            grid=(1,),
            in_specs=[
                pl.BlockSpec(own.shape, lambda i, s: (0, 0, 0)),
                pl.BlockSpec(got.shape, lambda i, s: (0, 0, 0, 0, 0)),
                pl.BlockSpec(tables.shape, lambda i, s: (0, 0)),
            ]
            + [anywhere] * len(after),
            out_specs=[pl.BlockSpec(own.shape, lambda i, s: (0, 0, 0))]
            + [pl.BlockSpec(sum_shape, lambda i, s: (0, 0))] * count,
        ),
        out_shape=[array_of(own.shape)] + [array_of(sum_shape)] * count,
        compiler_params=params,
        cost_estimate=cost(costs[key]),
        name="couple",
    )(scalars, own, got, tables, *after)
    return out[0], out[1:]


def z_inverse_kernel(count, seg_count, offset, scalars_ref, *refs):
    blocks, (earlier_ref, table_ref) = refs[:count], refs[count : count + 2]
    block, y_cells, z_cells = earlier_ref.shape
    len_x, len_y = scalars_ref[0, 1], scalars_ref[0, 2]
    step = offset + pl.program_id(0)
    if seg_count:
        own_ref, got_ref = refs[count + 2 : count + 4]
        out_ref, terms_ref = refs[-2:]

        @pl.when(pl.program_id(0) == 0)
        def _():
            for r, term in enumerate(coupled_terms(seg_count, scalars_ref, own_ref, got_ref)):
                terms_ref[r] = term

    else:
        terms_ref, out_ref = refs[count + 2], refs[-1]
    first = scalars_ref[0, 3] + step * block
    row = lax.broadcasted_iota(jnp.int32, (y_cells, z_cells), 0)
    pieces = []
    for x in range(block):
        modes = jnp.concatenate([ref[x] for ref in blocks], axis=0)
        pieces.append(modes.T)
    value = times(jnp.concatenate(pieces, axis=0), table_ref[...])
    for x in range(block):
        limit = jnp.where(first + x < len_x, len_y, 0)
        out_ref[x] = value[x * y_cells : (x + 1) * y_cells] - jnp.where(
            row < limit, earlier_ref[x], 0.0
        )
    start = pl.multiple_of(jnp.minimum((len_y - 3) // 8 * 8, y_cells - 16), 8)
    mine = pl.ds(pl.multiple_of(step * block, block), block)
    terms = [terms_ref[r, mine][:, None, :] for r in range(face_rows)]
    low_row = lax.broadcasted_iota(jnp.int32, (block, 8, z_cells), 1)
    high_row = start + lax.broadcasted_iota(jnp.int32, (block, 16, z_cells), 1)
    low = out_ref[:, 0:8, :]
    for r in range(3):
        low = low + jnp.where(low_row == r, terms[r], 0.0)
    out_ref[:, 0:8, :] = low
    high = out_ref[:, pl.ds(start, 16), :]
    for r in range(3):
        high = high + jnp.where(high_row == len_y - 3 + r, terms[3 + r], 0.0)
    out_ref[:, pl.ds(start, 16), :] = high


def z_inverse(
    blocks, earlier, terms, scalars, tables, seg_count, key, after=(), first=0, filled=None
):
    count = len(blocks)
    x_local, y_cells, z_cells = earlier.shape
    width = z_cells // count
    start = first // x_block
    given = len(terms) == 1
    operands = [scalars, *map(array_in, blocks), earlier, tables, *terms, *after]
    aliases = {}
    if filled is not None:
        aliases = {len(operands): 0}
        operands.append(filled)
    terms_shape = (face_rows, x_local, z_cells)

    def rows_from(begin):
        return lambda i, s: (begin + i, 0, 0)

    out = pl.pallas_call(
        functools.partial(z_inverse_kernel, count, 0 if given else seg_count, start),
        grid_spec=pltpu.PrefetchScalarGridSpec(
            num_scalar_prefetch=1,
            grid=(array_in(blocks[-1]).shape[-3] // x_block,),
            in_specs=[
                block_spec(
                    b,
                    (x_block, width, y_cells),
                    rows_from(start if array_in(b).shape[-3] == x_local else 0),
                )
                for b in blocks
            ]
            + [pl.BlockSpec((x_block, y_cells, z_cells), rows_from(start))]
            + [whole(t.shape) for t in (tables, *terms)]
            + [anywhere] * (len(after) + len(aliases)),
            out_specs=[pl.BlockSpec((x_block, y_cells, z_cells), rows_from(start))]
            + ([] if given else [whole(terms_shape)]),
        ),
        out_shape=[array_of(earlier.shape)] + ([] if given else [array_of(terms_shape)]),
        input_output_aliases=aliases,
        compiler_params=params,
        cost_estimate=cost(costs[key]),
        name="z_inverse",
    )(*operands)
    return out[0] if given else out


def gate_kernel(*refs):
    pass


def gated(array, after):
    return pl.pallas_call(
        gate_kernel,
        in_specs=[anywhere] * (1 + len(after)),
        out_specs=anywhere,
        out_shape=array_of(array.shape),
        input_output_aliases={0: 0},
        compiler_params=params,
        cost_estimate=cost(costs["gate"]),
        name="gate",
    )(array, *after)


def pairs_at(count, distance):
    return [(i, i ^ distance) for i in range(count)]


def send(block, distance):
    count = lax.axis_size("sub")
    return lax.ppermute(block, "sub", pairs_at(count, distance))


def exchange(blocks):
    return [blocks[0]] + [send(blocks[k], k) for k in range(1, len(blocks))]


def local(adj_next, adj_later, box_sizes, holder, partner):
    part_count = holder.shape[0]
    seg_count = partner.shape[2]
    my_group = lax.axis_index("grp").astype(jnp.int32)
    me = lax.axis_index("sub").astype(jnp.int32)
    count = lax.axis_size("sub")
    _, x_local, y_cells, z_cells = adj_next.shape
    x_total = x_local * count
    z_local = z_cells // count
    z_fwd, z_inv = (jnp.asarray(t) for t in z_tables(z_cells, count))
    place = me.reshape(1)

    middle = count // 2
    lead = z_lead(adj_next[0], place, z_fwd, count)
    parcel = z_forward(adj_next[0], place, z_fwd, count, 2, [lead[0]], "forward_next", lead=1)
    lead = [send(b, k) for k, b in enumerate(lead, 2)]
    first_a, first_b = [parcel[0], send(parcel[1], 1)], [parcel[0]]
    first_b.append(first_a[1])
    for c, blocks in enumerate((first_a, first_b)):
        for k in range(2, count):
            blocks += [lead[k - 2], send(parcel[k][c], k)]

    ids = jnp.stack([me, my_group, jnp.int32(x_local)])
    scalars, tabs = make_tables(
        ids,
        box_sizes,
        holder,
        partner,
        (y_cells, x_total),
        z_fwd,
        z_inv,
        [parcel[0]],
    )
    later = z_forward(
        adj_later[0], place, z_fwd, count, 1, [tabs["squares"]], "forward_later", 0
    )
    pair = later[1]
    later = [later[0], None] + [b[0] for b in later[2:]]
    for k in range(2, middle + 1):
        later[k] = send(later[k], k)

    before = first_part(first_a, place, tabs, None, [later[0]], "first_a")
    waved, faces = first_part(first_b, place, tabs, before, [], "first_b")
    faces = exchange(faces)
    for k in range(middle + 1, count):
        later[k] = send(gated(later[k], [faces[1]]), k)
    back = inverse_part(waved, tabs, count, "back", pair)
    near = send(back[1], 1)
    later[1] = (near, 0)
    back[1] = (near, 1)
    own, outgoing = strips_part(
        faces,
        scalars,
        tabs["z_back"],
        seg_count,
        part_count,
        x_local,
        [back[0], *later[2 : middle + 1]],
        "strips_now",
    )
    for k in range(2, count):
        back[k] = send(gated(back[k], [outgoing]), k)
    got = lax.all_to_all(outgoing, "grp", 0, 0, tiled=True)
    partial = difference_part(later, waved, tabs, [outgoing])
    terms_now, sums = couple_part(
        own,
        got,
        scalars,
        tabs["z"],
        seg_count,
        count,
        [partial],
        "couple_now",
    )
    last, faces = second_part(
        exchange(sums), partial, place, tabs, back[2 : middle + 1]
    )
    faces = exchange(faces)
    near = last[1]
    last[2:] = [send(b, min(k, count - 1)) for k, b in enumerate(last[2:], 2)]
    own, outgoing = strips_part(
        faces,
        scalars,
        tabs["z_back"],
        seg_count,
        part_count,
        x_local,
        [last[0], back[-1]],
        "strips_earlier",
    )
    last[1] = send(gated(near, [outgoing]), 1)
    got = lax.all_to_all(outgoing, "grp", 0, 0, tiled=True)
    adj_now = z_inverse(
        back,
        adj_later[0],
        [terms_now],
        scalars,
        tabs["z_back"],
        seg_count,
        "now",
        last[2 : middle + 1],
    )
    common = (scalars, tabs["z_back"], seg_count)
    adj_earlier, terms = z_inverse(
        last[:-1], adj_next[0], [own, got], *common, "end_a", [adj_now]
    )
    adj_earlier = z_inverse(
        last[:-2] + last[-1:],
        adj_next[0],
        [terms],
        *common,
        "end_b",
        [],
        x_local // 2,
        adj_earlier,
    )
    return (adj_now[None], adj_earlier[None])


def solution(mesh):
    return jax.shard_map(
        local,
        mesh=mesh,
        in_specs=(P("grp", "sub", None, None), P("grp", "sub", None, None), P(), P(), P()),
        out_specs=(P("grp", "sub", None, None), P("grp", "sub", None, None)),
        check_vma=False,
    )
```

```python
import functools
import math

import jax
import jax.numpy as jnp
import numpy as np
from jax import lax
from jax.experimental import pallas as pl
from jax.experimental.pallas import tpu as pltpu
from jax.sharding import PartitionSpec as P

f32 = jnp.float32
bf16 = jnp.bfloat16
time_step = 0.5
half_phase = (math.pi * time_step / 2.0) ** 2
pair_limit = 3
face_rows = 6
padded_rows = 8
plane_block = 16
x_block = 16
costs = {"lead": 0, "forward_next": 2, "tables": 32, "forward_later": 8, "first_a": 0, "first_b": 32, "back": 10, "strips_now": 8, "later": 0, "couple_now": 0, "second": 16, "strips_earlier": 8, "now": 2, "end_a": 0, "end_b": 0, "gate": 0.0}
stencil = np.array(
    (
        (0, 0, -2, 2, 0, 0),
        (0, 2, -27, 27, -2, 0),
        (-2, 27, -270, 270, -27, 2),
        (2, -27, 270, -270, 27, -2),
        (0, -2, 27, -27, 2, 0),
        (0, 0, 2, -2, 0, 0),
    ),
    np.float32,
)
weights = np.transpose(stencil) / np.float32(180.0)
params = pltpu.CompilerParams(vmem_limit_bytes=64 * 2**20 - 65536)


anywhere = pl.BlockSpec(memory_space=pl.ANY)
smem = pl.BlockSpec(memory_space=pltpu.SMEM)


def array_of(shape, dtype=f32):
    return jax.ShapeDtypeStruct(shape, dtype)


def cost(work):
    return pl.CostEstimate(flops=int(work * 1e9), bytes_accessed=1024, transcendentals=0)


def stacked_constant(table):
    high = table.astype(np.float32).astype(jnp.bfloat16)
    low = (table - high.astype(np.float64)).astype(np.float32).astype(jnp.bfloat16)
    row = np.concatenate([high, low], axis=1)
    return np.concatenate([row, row], axis=0)


def z_tables(z_cells, count):
    modes = np.arange(z_cells)[:, None]
    cells = np.arange(z_cells)[None, :]
    table = np.sqrt(np.where(modes == 0, 1.0, 2.0) / z_cells) * np.cos(
        np.pi * modes * (cells + 0.5) / z_cells
    )
    width = z_cells // count
    forward, inverse = [], []
    for me in range(count):
        order = np.concatenate([np.arange(width) + (me ^ k) * width for k in range(count)])
        mine = table[order]
        forward.append(stacked_constant(mine.T))
        inverse.append(stacked_constant(mine))
    return np.stack(forward), np.stack(inverse)


def split(value):
    high = value.astype(bf16)
    low = (value - high.astype(f32)).astype(bf16)
    return high, low


def times(value, table):
    product = jnp.dot(
        jnp.concatenate(split(value), axis=1), table, preferred_element_type=f32
    )
    width = product.shape[1] // 2
    return product[:, :width] + product[:, width:]


def flip(value, count):
    rows = value.shape[0] // count
    return jnp.concatenate([value[i * rows : (i + 1) * rows].T for i in range(count)], axis=0)


def packed(value):
    cells, width = value.shape[0], value.shape[1] // padded_rows
    rest = value[:, 4 * width : face_rows * width]
    rest = jnp.concatenate([rest[: cells // 2], rest[cells // 2 :]], axis=1)
    return jnp.concatenate([value[:, : 4 * width], rest], axis=0)


def packed_shape(cells, width):
    return cells + cells // 2, 4 * width


def lanes_of(refs, row):
    pieces = []
    for ref in refs:
        cells, width = ref.shape[0] * 2 // 3, ref.shape[1] // 4
        if row < 4:
            pieces.append(ref[:cells, row * width : (row + 1) * width])
        else:
            first = (row - 4) * width
            parts = [ref[cells:, s : s + width] for s in (first, first + 2 * width)]
            pieces.append(jnp.concatenate(parts, axis=0))
    return jnp.concatenate(pieces, axis=1)


def sine_ratio(square, terms):
    total = jnp.full_like(square, (-1.0) ** (terms - 1) / math.factorial(2 * terms - 1))
    for n in reversed(range(terms - 1)):
        total = total * square + (-1.0) ** n / math.factorial(2 * n + 1)
    return total


def cosine_entries(modes, cells, length):
    extent = jnp.full(modes.shape, length).astype(f32)
    steps = (modes * (2 * cells + 1)).astype(f32)
    period = 4.0 * extent
    turns = steps - period * jnp.floor(steps / period)
    turns = jnp.where(turns < 0.0, turns + period, turns)
    turns = jnp.where(turns >= period, turns - period, turns)
    turns = jnp.minimum(turns, period - turns)
    angle = (extent - turns) * (f32(math.pi / 2) / extent)
    scaling = jnp.sqrt(jnp.where(modes == 0, 1.0, 2.0) / extent)
    inside = (modes < length) & (cells < length) & (cells >= 0)
    return jnp.where(inside, scaling * angle * sine_ratio(angle * angle, 8), 0.0)


def stacked(table):
    row = jnp.concatenate(split(table), axis=1)
    return jnp.concatenate([row, row], axis=0)


def links(seg_count, ids_ref, box_ref, holder_ref, partner_ref, scalars_ref):
    item_count = 2 * seg_count
    part_count = holder_ref.shape[0]
    me, group, x_local = ids_ref[0], ids_ref[1], ids_ref[2]

    def find(p, found):
        return jnp.where(holder_ref[p] == group, p, found)

    part = lax.fori_loop(0, part_count, find, jnp.int32(0))
    len_x, len_y = box_ref[part, 0], box_ref[part, 1]
    head = [me, len_x, len_y, me * x_local]
    mine = [partner_ref[part, i] for i in range(item_count)]
    peers = [jnp.where(m < 0, -1, lax.div(jnp.maximum(m, 0), seg_count)) for m in mine]
    for item in range(item_count):
        wall = mine[item] < 0
        peer = jnp.maximum(peers[item], 0)
        seg = lax.rem(jnp.maximum(mine[item], 0), seg_count)
        peer_item = (1 - item // seg_count) * seg_count + seg
        send_slot, get_slot = jnp.int32(0), jnp.int32(0)
        for i in range(item_count):
            if i < item:
                send_slot += jnp.where(peers[i] == peer, 1, 0)
            link = partner_ref[peer, i]
            back = jnp.where(link < 0, -1, lax.div(jnp.maximum(link, 0), seg_count))
            get_slot += jnp.where((back == part) & (i < peer_item), 1, 0)
        scalars_ref[0, item] = head[item] if item < len(head) else jnp.int32(0)
        scalars_ref[1, item] = jnp.where(wall, 0, holder_ref[peer])
        scalars_ref[2, item] = jnp.minimum(send_slot, pair_limit - 1)
        scalars_ref[3, item] = jnp.where(wall, 0, jnp.minimum(get_slot, pair_limit - 1))
        scalars_ref[4, item] = jnp.where(wall, 0, jnp.minimum(len_x, box_ref[peer, 0]))
        scalars_ref[5, item] = jnp.where(wall, 1, 0)
    return me, len_x, len_y


def tables_kernel(seg_count, ids_ref, box_ref, holder_ref, partner_ref, *refs):
    z_ref, z_back_ref = refs[:2]
    refs = refs[-10:]
    scalars_ref, x_ref, x_back_ref, y_ref, y_back_ref, face_ref, place_ref = refs[:7]
    squares_ref, my_z_ref, my_z_back_ref = refs[7:]
    my_z_ref[...] = z_ref[ids_ref[0]]
    my_z_back_ref[...] = z_back_ref[ids_ref[0]]
    y_cells, x_cells = squares_ref.shape
    me, len_x, len_y = links(seg_count, ids_ref, box_ref, holder_ref, partner_ref, scalars_ref)
    x_local = ids_ref[2]

    def index(shape, axis):
        return lax.broadcasted_iota(jnp.int32, shape, axis)

    def cells_x(axis):
        cell = index((x_cells, x_cells), axis)
        return (lax.div(cell, x_local) ^ me) * x_local + lax.rem(cell, x_local)

    square = (x_cells, x_cells)
    x_ref[...] = stacked(cosine_entries(index(square, 1), cells_x(0), len_x))
    x_back_ref[...] = stacked(cosine_entries(index(square, 0), cells_x(1), len_x))
    square = (y_cells, y_cells)
    y_ref[...] = stacked(cosine_entries(index(square, 1), index(square, 0), len_y))
    y_back_ref[...] = stacked(cosine_entries(index(square, 0), index(square, 1), len_y))

    def cell_rows(rows):
        return jnp.where(rows < 3, rows, jnp.where(rows < face_rows, len_y - face_rows + rows, -1))

    shape = (padded_rows, y_cells)
    face = cosine_entries(index(shape, 1), cell_rows(index(shape, 0)), len_y)
    high = face.astype(bf16).astype(f32)
    both = jnp.concatenate([high, face - high], axis=0)
    face_ref[...] = jnp.concatenate([both, both], axis=1).astype(bf16)
    shape = (y_cells, 4 * padded_rows)
    column = index(shape, 1)
    turned = cosine_entries(index(shape, 0), cell_rows(lax.rem(column, padded_rows)), len_y)
    high = turned.astype(bf16).astype(f32)
    part = jnp.where(column < 2 * padded_rows, high, turned - high)
    place_ref[...] = jnp.where(column < 3 * padded_rows, part, 0.0).astype(bf16)

    shape = (y_cells, x_cells)
    ratio_x = index(shape, 1).astype(f32) / jnp.full(shape, len_x).astype(f32)
    ratio_y = index(shape, 0).astype(f32) / jnp.full(shape, len_y).astype(f32)
    squares_ref[...] = (ratio_x * ratio_x + ratio_y * ratio_y) * half_phase


def make_tables(ids, box_sizes, holder, partner, shape, z_fwd, z_inv, after):
    y_cells, x_cells = shape
    part_count, _, seg_count = partner.shape
    item_count = 2 * seg_count
    out_shapes = [
        (6, item_count),
        (2 * x_cells, 2 * x_cells),
        (2 * x_cells, 2 * x_cells),
        (2 * y_cells, 2 * y_cells),
        (2 * y_cells, 2 * y_cells),
        (2 * padded_rows, 2 * y_cells),
        (y_cells, 4 * padded_rows),
        shape,
        z_fwd.shape[1:],
        z_inv.shape[1:],
    ]
    types = [bf16] * 6 + [f32] + [bf16] * 2
    vmem = pl.BlockSpec(memory_space=pltpu.VMEM)
    out = pl.pallas_call(
        functools.partial(tables_kernel, seg_count),
        in_specs=[smem] * 4 + [vmem] * 2 + [anywhere] * len(after),
        out_specs=[smem] + [vmem] * 9,
        out_shape=[jax.ShapeDtypeStruct(out_shapes[0], jnp.int32)]
        + [array_of(s, t) for s, t in zip(out_shapes[1:], types)],
        compiler_params=params,
        cost_estimate=cost(costs["tables"]),
        name="tables",
    )(ids, box_sizes, holder, partner.reshape(part_count, item_count), z_fwd, z_inv, *after)
    names = ("x", "x_back", "y", "y_back", "face", "place", "squares", "z", "z_back")
    return out[0], dict(zip(names, out[1:]))


def factors(squares, plane, z_total):
    ratio_z = jnp.full(squares.shape, plane).astype(f32) * (1.0 / z_total)
    halved = squares + ratio_z * ratio_z * half_phase
    ratio = sine_ratio(halved, 6)
    source = (time_step**2 * ratio) * ratio
    return 2.0 - (4.0 / time_step**2) * (halved * source), source


def parcel_shapes(whole_shape, part_shape, count, parts, paired):
    near = array_of((2,) + whole_shape if paired else whole_shape)
    return [array_of(whole_shape), near] + [array_of(part_shape)] * (
        (count - 2) * parts
    )


def near_spec(shape, which, index):
    if which is None:
        return pl.BlockSpec(shape, index)
    return pl.BlockSpec((None,) + shape, lambda *a: (which,) + index(*a))


def parcel_of(out, parts):
    return [out[0], out[1]] + [out[i : i + parts] for i in range(2, len(out), parts)]


def array_in(block):
    return block[0] if isinstance(block, tuple) else block


def block_spec(block, shape, index):
    if isinstance(block, tuple):
        return pl.BlockSpec((None,) + shape, lambda *a: (block[1],) + index(*a))
    return pl.BlockSpec(shape, index)


def z_modes(field_ref, table):
    block, y_cells, z_cells = field_ref.shape
    modes = times(field_ref[...].reshape(block * y_cells, z_cells), table)
    return [modes[x * y_cells : (x + 1) * y_cells].T for x in range(block)]


def z_lead_kernel(count, me_ref, field_ref, table_ref, *refs):
    out_refs, modes_ref = refs[:-1], refs[-1]
    width = field_ref.shape[2] // count
    for x, turned in enumerate(z_modes(field_ref, table_ref[0])):
        modes_ref[x] = turned
    for k, ref in enumerate(out_refs, 2):
        start = pl.multiple_of((me_ref[0] ^ k) * width, width)
        ref[...] = modes_ref[:, pl.ds(start, width), :]


def z_forward_kernel(count, parts, after, me_ref, field_ref, table_ref, *refs):
    out_refs = refs[after:]
    width = field_ref.shape[2] // count
    part = width // parts
    for x, turned in enumerate(z_modes(field_ref, table_ref[0])):
        out_refs[0][x] = turned[:width]
        out_refs[1][x] = turned[width : 2 * width]
        for i, ref in enumerate(out_refs[2:]):
            start = 2 * width + i * part
            ref[x] = turned[start : start + part]


def z_in_specs(field, tables):
    _, y_cells, z_cells = field.shape
    return [
        pl.BlockSpec((x_block, y_cells, z_cells), lambda i, me: (i, 0, 0)),
        pl.BlockSpec((1,) + tables.shape[1:], lambda i, me: (me[0], 0, 0)),
    ]


def z_lead(field, me, tables, count):
    _, y_cells, z_cells = field.shape
    shape = (x_block, z_cells // count, y_cells)
    return pl.pallas_call(
        functools.partial(z_lead_kernel, count),
        grid=(1,),
        in_specs=[
            smem,
            pl.BlockSpec((x_block, y_cells, z_cells), lambda i: (0, 0, 0)),
            pl.BlockSpec((1,) + tables.shape[1:], lambda i: (0, 0, 0)),
        ],
        out_specs=[pl.BlockSpec(shape, lambda i: (0, 0, 0))] * (count - 2),
        out_shape=[array_of(shape)] * (count - 2),
        scratch_shapes=[pltpu.VMEM((x_block, z_cells, y_cells), f32)],
        compiler_params=params,
        cost_estimate=cost(costs["lead"]),
        name="z_lead",
    )(me, field, tables)


def z_forward(field, me, tables, count, parts, after, key, which=None, lead=0):
    size, y_cells, z_cells = field.shape
    width = z_cells // count
    part = width // parts
    rest = (count - 2) * parts
    far = size - lead * x_block
    out = pl.pallas_call(
        functools.partial(z_forward_kernel, count, parts, len(after)),
        grid_spec=pltpu.PrefetchScalarGridSpec(
            num_scalar_prefetch=1,
            grid=(size // x_block,),
            in_specs=z_in_specs(field, tables) + [anywhere] * len(after),
            out_specs=[
                pl.BlockSpec((x_block, width, y_cells), lambda i, me: (i, 0, 0)),
                near_spec((x_block, width, y_cells), which, lambda i, me: (i, 0, 0)),
            ]
            + [
                pl.BlockSpec(
                    (x_block, part, y_cells), lambda i, me: (jnp.maximum(i - lead, 0), 0, 0)
                )
            ]
            * rest,
        ),
        out_shape=parcel_shapes(
            (size, width, y_cells), (far, part, y_cells), count, parts, which is not None
        ),
        compiler_params=params,
        cost_estimate=cost(costs[key]),
        name="z_forward",
    )(me, field, tables, *after)
    return parcel_of(out, parts)


def plane_forward(block_refs, y_table, x_table):
    planes = block_refs[0].shape[1]
    value = jnp.concatenate([ref[...] for ref in block_refs], axis=0)
    x_cells, _, y_cells = value.shape
    value = jnp.swapaxes(value, 0, 1).reshape(planes * x_cells, y_cells)
    value = flip(times(value, y_table), planes)
    return times(value, x_table)


def store_faces(step, total, forced, face_table, rows_ref):
    planes = len(forced)
    for j, value in enumerate(forced):
        both = jnp.dot(
            face_table, jnp.concatenate(split(value), axis=0), preferred_element_type=f32
        )
        rows = both[:padded_rows] + both[padded_rows:]
        rows_ref[pl.ds(step * planes + j, padded_rows, stride=total), :] = rows


def send_faces(rows, x_table, face_refs):
    value = times(rows, x_table).T
    x_local = value.shape[0] // len(face_refs)
    for k, ref in enumerate(face_refs):
        ref[...] = packed(value[k * x_local : (k + 1) * x_local])


def first_kernel(count, held, last, offset, z_total, me_ref, *refs):
    blocks, refs = refs[:held], refs[held:]
    squares_ref, y_ref, x_ref, face_ref = refs[:4]
    spectral = plane_forward(blocks, y_ref[...], x_ref[...])
    if not last:
        out_ref, rows_ref = refs[-2:]
    else:
        x_back_ref, before_ref = refs[4:6]
        out_ref, face_refs, rows_ref = refs[-2 - count], refs[-1 - count : -1], refs[-1]
    planes, y_modes, x_modes = out_ref.shape
    total = rows_ref.shape[0] // padded_rows
    first = me_ref[0] * (z_total // count) + offset + pl.program_id(0) * planes
    forced = []
    for j in range(planes):
        mine = spectral[j * y_modes : (j + 1) * y_modes]
        wave, source = factors(squares_ref[...], first + j, z_total)
        out_ref[j] = wave * mine
        forced.append(source * mine)
    store_faces(pl.program_id(0), total, forced, face_ref[...], rows_ref)
    if last:

        @pl.when(pl.program_id(0) == pl.num_programs(0) - 1)
        def _():
            rows = []
            for r in range(padded_rows):
                rows += [ref[r * total : (r + 1) * total] for ref in (before_ref, rows_ref)]
            send_faces(jnp.concatenate(rows, axis=0), x_back_ref[...], face_refs)


def difference_kernel(count, *refs):
    blocks = refs[:count]
    waved_ref, y_ref, x_ref, out_ref = refs[count : count + 3] + refs[-1:]
    spectral = plane_forward(blocks, y_ref[...], x_ref[...])
    out_ref[...] = waved_ref[...] - spectral.reshape(waved_ref.shape)


def second_kernel(count, skip, z_total, me_ref, *refs):
    sums, refs = refs[:count], refs[count:]
    partial_ref, squares_ref, x_ref, x_back_ref, y_back_ref, face_ref, place_ref = refs[:7]
    refs = refs[7 + skip :]
    out_refs, face_refs = refs[: count + 1], refs[count + 1 : 2 * count + 1]
    rows_ref, terms_ref = refs[2 * count + 1 :]
    step = pl.program_id(0)
    planes = partial_ref.shape[0]
    total = rows_ref.shape[0] // padded_rows

    @pl.when(step == 0)
    def _():
        rows = [lanes_of(sums, r) for r in range(face_rows)]
        rows += [jnp.zeros_like(rows[0])] * (padded_rows - face_rows)
        terms_ref[...] = times(jnp.concatenate(rows, axis=0), x_ref[...])

    waved, forced = [], []
    for j in range(planes):
        rows = terms_ref[pl.ds(step * planes + j, padded_rows, stride=total), :]
        high = rows.astype(bf16).astype(f32)
        low = rows - high
        stack = jnp.concatenate([high, low, high, jnp.zeros_like(rows)], axis=0).astype(bf16)
        added = jnp.dot(place_ref[...], stack, preferred_element_type=f32)
        mine = partial_ref[j] + added
        wave, source = factors(squares_ref[...], me_ref[0] * total + step * planes + j, z_total)
        waved.append(wave * mine)
        forced.append(source * mine)
    store_faces(step, total, forced, face_ref[...], rows_ref)
    store_cells(waved, x_back_ref[...], y_back_ref[...], out_refs)

    @pl.when(step == pl.num_programs(0) - 1)
    def _():
        send_faces(rows_ref[...], x_back_ref[...], face_refs)


def store_cells(waved, x_table, y_table, out_refs):
    planes = len(waved)
    value = times(jnp.concatenate(waved, axis=0), x_table)
    value = times(flip(value, planes), y_table)
    value = value.reshape(planes, value.shape[0] // planes, value.shape[1])
    value = jnp.swapaxes(value, 0, 1)
    first = 0
    for ref in out_refs:
        ref[...] = value[first : first + ref.shape[0]]
        first += ref.shape[0]


def inverse_kernel(count, waved_ref, x_ref, y_ref, pair_ref, *out_refs):
    waved = [waved_ref[j] for j in range(waved_ref.shape[0])]
    store_cells(waved, x_ref[...], y_ref[...], out_refs)


def whole(shape):
    zeros = (0,) * len(shape)
    return pl.BlockSpec(shape, lambda i, *s: zeros)


def plane_specs(blocks, planes=None, first=0):
    specs = []
    for b in blocks:
        x_cells, held, y_cells = array_in(b).shape[-3:]
        start = first if held == planes else 0
        specs.append(
            block_spec(
                b, (x_cells, plane_block, y_cells), lambda i, *s, start=start: (0, start + i, 0)
            )
        )
    return specs


def mode_spec(shape, first=0):
    return pl.BlockSpec((plane_block,) + shape[1:], lambda i, *s: (first + i, 0, 0))


def first_part(blocks, place, tabs, before, after, key):
    own = blocks[-1].shape[1]
    x_local, planes, _ = blocks[0].shape
    y_modes, x_modes = tabs["squares"].shape
    small = [tabs["squares"], tabs["y"], tabs["x"], tabs["face"]]
    count = x_modes // x_local
    last = before is not None
    offset = planes - own if last else 0
    shape = (planes, y_modes, x_modes)
    operands = [place, *map(array_in, blocks), *small]
    in_specs = plane_specs(blocks, planes, offset // plane_block) + [whole(t.shape) for t in small]
    rows_shape = (padded_rows * own, x_modes)
    out_specs = [mode_spec(shape, offset // plane_block)]
    out_shape = [array_of(shape)]
    scratch, aliases = [], {}
    if last:
        waved, rows = before
        operands += [tabs["x_back"], rows, waved]
        in_specs += [whole(tabs["x_back"].shape), whole(rows.shape), anywhere]
        aliases = {len(operands) - 1: 0}
        face_shape = packed_shape(x_local, planes)
        out_specs += [whole(face_shape)] * count
        out_shape += [array_of(face_shape)] * count
        scratch = [pltpu.VMEM(rows_shape, f32)]
    else:
        out_specs += [whole(rows_shape)]
        out_shape += [array_of(rows_shape)]
    operands += after
    in_specs += [anywhere] * len(after)
    out = pl.pallas_call(
        functools.partial(first_kernel, count, len(blocks), last, offset, planes * count),
        grid_spec=pltpu.PrefetchScalarGridSpec(
            num_scalar_prefetch=0,
            grid=(own // plane_block,),
            in_specs=[smem]
            + in_specs,
            out_specs=out_specs,
            scratch_shapes=scratch,
        ),
        out_shape=out_shape,
        input_output_aliases=aliases,
        compiler_params=params,
        cost_estimate=cost(costs[key]),
        name="first_modes",
    )(*operands)
    return out[0], out[1:] if last else out[1]


def difference_part(blocks, waved, tabs, after):
    count = len(blocks)
    small = [tabs["y"], tabs["x"]]
    return pl.pallas_call(
        functools.partial(difference_kernel, count),
        grid=(waved.shape[0] // plane_block,),
        in_specs=plane_specs(blocks)
        + [mode_spec(waved.shape)]
        + [whole(t.shape) for t in small]
        + [anywhere] * len(after),
        out_specs=mode_spec(waved.shape),
        out_shape=array_of(waved.shape),
        compiler_params=params,
        cost_estimate=cost(costs["later"]),
        name="later_modes",
    )(*map(array_in, blocks), waved, *small, *after)


def second_part(sums, partial, place, tabs, after):
    count = len(sums)
    planes, y_modes, x_modes = partial.shape
    y_cells = tabs["y_back"].shape[1] // 2
    x_local = x_modes // count
    face_shape = packed_shape(x_local, planes)
    sizes = [x_local] * (count - 1) + [x_local // 2] * 2
    small = [tabs[n] for n in ("squares", "x", "x_back", "y_back", "face", "place")]
    out = pl.pallas_call(
        functools.partial(second_kernel, count, len(after), planes * count),
        grid_spec=pltpu.PrefetchScalarGridSpec(
            num_scalar_prefetch=0,
            grid=(planes // plane_block,),
            in_specs=[smem]
            + [whole(s.shape) for s in sums]
            + [mode_spec(partial.shape)]
            + [whole(t.shape) for t in small]
            + [anywhere] * len(after),
            out_specs=[
                pl.BlockSpec((n, plane_block, y_cells), lambda i, *s: (0, i, 0)) for n in sizes
            ]
            + [whole(face_shape)] * count,
            scratch_shapes=[
                pltpu.VMEM((padded_rows * planes, x_modes), f32),
                pltpu.VMEM((padded_rows * planes, x_modes), f32),
            ],
        ),
        out_shape=[array_of((n, planes, y_cells)) for n in sizes]
        + [array_of(face_shape)] * count,
        compiler_params=params,
        cost_estimate=cost(costs["second"]),
        name="second_modes",
    )(place, *sums, partial, *small, *after)
    return list(out[: count + 1]), out[count + 1 :]


def inverse_part(waved, tabs, count, key, pair):
    planes, y_modes, x_modes = waved.shape
    y_cells = tabs["y_back"].shape[1] // 2
    x_local = x_modes // count
    small = [tabs["x_back"], tabs["y_back"]]
    shape = (x_local, plane_block, y_cells)
    out = pl.pallas_call(
        functools.partial(inverse_kernel, count),
        grid=(planes // plane_block,),
        in_specs=[mode_spec(waved.shape)] + [whole(t.shape) for t in small] + [anywhere],
        out_specs=[pl.BlockSpec(shape, lambda i: (0, i, 0))]
        + [near_spec(shape, 1, lambda i: (0, i, 0))]
        + [pl.BlockSpec(shape, lambda i: (0, i, 0))] * (count - 2),
        out_shape=parcel_shapes(
            (x_local, planes, y_cells), (x_local, planes, y_cells), count, 1, True
        ),
        input_output_aliases={3: 1},
        compiler_params=params,
        cost_estimate=cost(costs[key]),
        name="modes_to_cells",
    )(waved, *small, pair)
    return list(out)


def strips_kernel(count, seg_count, scalars_ref, *refs):
    faces, table_ref, (own_ref, send_ref) = refs[:count], refs[count], refs[-2:]
    rows, x_local, z_cells = own_ref.shape
    value = jnp.concatenate([lanes_of(faces, r) for r in range(rows)], axis=0)
    value = times(value, table_ref[...]).reshape(rows, x_local, z_cells)
    own_ref[...] = value
    seg_cells = z_cells // seg_count
    groups = z_cells // seg_cells
    lane = lax.broadcasted_iota(jnp.int32, (8, z_cells), 1) // seg_cells
    for item in range(2 * seg_count):
        face, seg = item // seg_count, item % seg_count
        dest, slot, wall = scalars_ref[1, item], scalars_ref[2, item], scalars_ref[5, item]

        @pl.when(wall == 0)
        def _():
            for j in range(3):
                packed = jnp.zeros((8, z_cells), f32)
                for c in range(groups):
                    piece = value[face * 3 + j, 8 * c : 8 * (c + 1)]
                    shift = (c - seg) * seg_cells % z_cells
                    if shift:
                        piece = pltpu.roll(piece, shift, 1)
                    packed = jnp.where(lane == c, piece, packed)
                send_ref[dest, slot, j] = packed


def strips_part(faces, scalars, tables, seg_count, part_count, x_local, after, key):
    count = len(faces)
    z_cells = tables.shape[1] // 2
    own_shape = (face_rows, x_local, z_cells)
    send_shape = (part_count, pair_limit, 3, 8, z_cells)
    return pl.pallas_call(
        functools.partial(strips_kernel, count, seg_count),
        grid_spec=pltpu.PrefetchScalarGridSpec(
            num_scalar_prefetch=0,
            grid=(1,),
            in_specs=[smem]
            + [pl.BlockSpec(f.shape, lambda i: (0, 0)) for f in faces]
            + [pl.BlockSpec(tables.shape, lambda i: (0, 0))]
            + [anywhere] * len(after),
            out_specs=[
                pl.BlockSpec(own_shape, lambda i: (0, 0, 0)),
                pl.BlockSpec(send_shape, lambda i: (0, 0, 0, 0, 0)),
            ],
        ),
        out_shape=[array_of(own_shape), array_of(send_shape)],
        compiler_params=params,
        cost_estimate=cost(costs[key]),
        name="strips",
    )(scalars, *faces, tables, *after)


def coupled_terms(seg_count, scalars_ref, own_ref, got_ref):
    _, x_local, z_cells = own_ref.shape
    seg_cells = z_cells // seg_count
    groups = z_cells // seg_cells
    lane = lax.broadcasted_iota(jnp.int32, (8, z_cells), 1) // seg_cells
    row_x = scalars_ref[0, 3] + lax.broadcasted_iota(jnp.int32, (x_local, z_cells), 0)
    lane_all = lax.broadcasted_iota(jnp.int32, (x_local, z_cells), 1) // seg_cells
    terms = []
    for face in range(2):
        limit = jnp.zeros((x_local, z_cells), jnp.int32)
        other = [[jnp.zeros((8, z_cells), f32)] * groups for _ in range(3)]
        for seg in range(seg_count):
            item = face * seg_count + seg
            source, slot = scalars_ref[1, item], scalars_ref[3, item]
            limit = jnp.where(lane_all == seg, scalars_ref[4, item], limit)
            for j in range(3):
                packed = got_ref[source, slot, j]
                for c in range(groups):
                    shift = (seg - c) * seg_cells % z_cells
                    piece = pltpu.roll(packed, shift, 1) if shift else packed
                    other[j][c] = jnp.where(lane == seg, piece, other[j][c])
        other = [jnp.concatenate(o, axis=0) for o in other]
        own = [own_ref[face * 3 + j] for j in range(3)]
        low, high = (other, own) if face == 0 else (own, other)
        keep = row_x < limit
        for i in range(3):
            row = weights[3 + i] if face == 0 else weights[i]
            total = jnp.zeros((x_local, z_cells), f32)
            for j in range(6):
                if row[j] != 0:
                    total = total + float(row[j]) * (low + high)[j]
            terms.append(jnp.where(keep, total, 0.0))
    return terms


def couple_kernel(count, seg_count, skip, scalars_ref, own_ref, got_ref, table_ref, *out_refs):
    out_refs = out_refs[skip:]
    terms = coupled_terms(seg_count, scalars_ref, own_ref, got_ref)
    for r, term in enumerate(terms):
        out_refs[0][r] = term
    _, x_local, z_cells = own_ref.shape
    blank = [jnp.zeros((x_local, z_cells), f32)] * (padded_rows - len(terms))
    value = times(jnp.concatenate(terms + blank, axis=0), table_ref[...]).T
    width = z_cells // count
    for k in range(count):
        out_refs[1 + k][...] = packed(value[k * width : (k + 1) * width])


def couple_part(own, got, scalars, tables, seg_count, count, after, key):
    rows, x_local, z_cells = own.shape
    sum_shape = packed_shape(z_cells // count, x_local)
    out = pl.pallas_call(
        functools.partial(couple_kernel, count, seg_count, len(after)),
        grid_spec=pltpu.PrefetchScalarGridSpec(
            num_scalar_prefetch=0,
            grid=(1,),
            in_specs=[smem]
            + [
                pl.BlockSpec(own.shape, lambda i: (0, 0, 0)),
                pl.BlockSpec(got.shape, lambda i: (0, 0, 0, 0, 0)),
                pl.BlockSpec(tables.shape, lambda i: (0, 0)),
            ]
            + [anywhere] * len(after),
            out_specs=[pl.BlockSpec(own.shape, lambda i: (0, 0, 0))]
            + [pl.BlockSpec(sum_shape, lambda i: (0, 0))] * count,
        ),
        out_shape=[array_of(own.shape)] + [array_of(sum_shape)] * count,
        compiler_params=params,
        cost_estimate=cost(costs[key]),
        name="couple",
    )(scalars, own, got, tables, *after)
    return out[0], out[1:]


def z_inverse_kernel(count, seg_count, offset, scalars_ref, *refs):
    blocks, (earlier_ref, table_ref) = refs[:count], refs[count : count + 2]
    block, y_cells, z_cells = earlier_ref.shape
    len_x, len_y = scalars_ref[0, 1], scalars_ref[0, 2]
    step = offset + pl.program_id(0)
    if seg_count:
        own_ref, got_ref = refs[count + 2 : count + 4]
        out_ref, terms_ref = refs[-2:]

        @pl.when(pl.program_id(0) == 0)
        def _():
            for r, term in enumerate(coupled_terms(seg_count, scalars_ref, own_ref, got_ref)):
                terms_ref[r] = term

    else:
        terms_ref, out_ref = refs[count + 2], refs[-1]
    first = scalars_ref[0, 3] + step * block
    row = lax.broadcasted_iota(jnp.int32, (y_cells, z_cells), 0)
    pieces = []
    for x in range(block):
        modes = jnp.concatenate([ref[x] for ref in blocks], axis=0)
        pieces.append(modes.T)
    value = times(jnp.concatenate(pieces, axis=0), table_ref[...])
    for x in range(block):
        limit = jnp.where(first + x < len_x, len_y, 0)
        out_ref[x] = value[x * y_cells : (x + 1) * y_cells] - jnp.where(
            row < limit, earlier_ref[x], 0.0
        )
    start = pl.multiple_of(jnp.minimum((len_y - 3) // 8 * 8, y_cells - 16), 8)
    mine = pl.ds(pl.multiple_of(step * block, block), block)
    terms = [terms_ref[r, mine][:, None, :] for r in range(face_rows)]
    low_row = lax.broadcasted_iota(jnp.int32, (block, 8, z_cells), 1)
    high_row = start + lax.broadcasted_iota(jnp.int32, (block, 16, z_cells), 1)
    low = out_ref[:, 0:8, :]
    for r in range(3):
        low = low + jnp.where(low_row == r, terms[r], 0.0)
    out_ref[:, 0:8, :] = low
    high = out_ref[:, pl.ds(start, 16), :]
    for r in range(3):
        high = high + jnp.where(high_row == len_y - 3 + r, terms[3 + r], 0.0)
    out_ref[:, pl.ds(start, 16), :] = high


def z_inverse(
    blocks, earlier, terms, scalars, tables, seg_count, key, after=(), first=0, filled=None
):
    count = len(blocks)
    x_local, y_cells, z_cells = earlier.shape
    width = z_cells // count
    start = first // x_block
    given = len(terms) == 1
    operands = [scalars, *map(array_in, blocks), earlier, tables, *terms, *after]
    aliases = {}
    if filled is not None:
        aliases = {len(operands): 0}
        operands.append(filled)
    terms_shape = (face_rows, x_local, z_cells)

    def rows_from(begin):
        return lambda i: (begin + i, 0, 0)

    out = pl.pallas_call(
        functools.partial(z_inverse_kernel, count, 0 if given else seg_count, start),
        grid_spec=pl.GridSpec(
            grid=(array_in(blocks[-1]).shape[-3] // x_block,),
            in_specs=[smem]
            + [
                block_spec(
                    b,
                    (x_block, width, y_cells),
                    rows_from(start if array_in(b).shape[-3] == x_local else 0),
                )
                for b in blocks
            ]
            + [pl.BlockSpec((x_block, y_cells, z_cells), rows_from(start))]
            + [whole(t.shape) for t in (tables, *terms)]
            + [anywhere] * (len(after) + len(aliases)),
            out_specs=[pl.BlockSpec((x_block, y_cells, z_cells), rows_from(start))]
            + ([] if given else [whole(terms_shape)]),
        ),
        out_shape=[array_of(earlier.shape)] + ([] if given else [array_of(terms_shape)]),
        input_output_aliases=aliases,
        compiler_params=params,
        cost_estimate=cost(costs[key]),
        name="z_inverse",
    )(*operands)
    return out[0] if given else out


def gate_kernel(*refs):
    pass


def gated(array, after):
    return pl.pallas_call(
        gate_kernel,
        in_specs=[anywhere] * (1 + len(after)),
        out_specs=anywhere,
        out_shape=array_of(array.shape),
        input_output_aliases={0: 0},
        compiler_params=params,
        cost_estimate=cost(costs["gate"]),
        name="gate",
    )(array, *after)


def pairs_at(count, distance):
    return [(i, i ^ distance) for i in range(count)]


def send(block, distance):
    count = lax.axis_size("sub")
    return lax.ppermute(block, "sub", pairs_at(count, distance))


def exchange(blocks):
    return [blocks[0]] + [send(blocks[k], k) for k in range(1, len(blocks))]


def local(adj_next, adj_later, box_sizes, holder, partner):
    part_count = holder.shape[0]
    seg_count = partner.shape[2]
    my_group = lax.axis_index("grp").astype(jnp.int32)
    me = lax.axis_index("sub").astype(jnp.int32)
    count = lax.axis_size("sub")
    _, x_local, y_cells, z_cells = adj_next.shape
    x_total = x_local * count
    z_local = z_cells // count
    z_fwd, z_inv = (jnp.asarray(t) for t in z_tables(z_cells, count))
    place = me.reshape(1)

    middle = count // 2
    lead = z_lead(adj_next[0], place, z_fwd, count)
    parcel = z_forward(adj_next[0], place, z_fwd, count, 2, [lead[0]], "forward_next", lead=1)
    lead = [send(b, k) for k, b in enumerate(lead, 2)]
    first_a, first_b = [parcel[0], send(parcel[1], 1)], [parcel[0]]
    first_b.append(first_a[1])
    for c, blocks in enumerate((first_a, first_b)):
        for k in range(2, count):
            blocks += [lead[k - 2], send(parcel[k][c], k)]

    ids = jnp.stack([me, my_group, jnp.int32(x_local)])
    scalars, tabs = make_tables(
        ids,
        box_sizes,
        holder,
        partner,
        (y_cells, x_total),
        z_fwd,
        z_inv,
        [parcel[0]],
    )
    later = z_forward(
        adj_later[0], place, z_fwd, count, 1, [tabs["squares"]], "forward_later", 0
    )
    pair = later[1]
    later = [later[0], None] + [b[0] for b in later[2:]]
    for k in range(2, middle + 1):
        later[k] = send(later[k], k)

    before = first_part(first_a, place, tabs, None, [later[0]], "first_a")
    waved, faces = first_part(first_b, place, tabs, before, [], "first_b")
    faces = exchange(faces)
    for k in range(middle + 1, count):
        later[k] = send(gated(later[k], [faces[1]]), k)
    back = inverse_part(waved, tabs, count, "back", pair)
    near = send(back[1], 1)
    later[1] = (near, 0)
    back[1] = (near, 1)
    own, outgoing = strips_part(
        faces,
        scalars,
        tabs["z_back"],
        seg_count,
        part_count,
        x_local,
        [back[0], *later[2 : middle + 1]],
        "strips_now",
    )
    for k in range(2, count):
        back[k] = send(gated(back[k], [outgoing]), k)
    got = lax.all_to_all(outgoing, "grp", 0, 0, tiled=True)
    partial = difference_part(later, waved, tabs, [outgoing])
    terms_now, sums = couple_part(
        own,
        got,
        scalars,
        tabs["z"],
        seg_count,
        count,
        [partial],
        "couple_now",
    )
    last, faces = second_part(
        exchange(sums), partial, place, tabs, back[2 : middle + 1]
    )
    faces = exchange(faces)
    near = last[1]
    last[2:] = [send(b, min(k, count - 1)) for k, b in enumerate(last[2:], 2)]
    own, outgoing = strips_part(
        faces,
        scalars,
        tabs["z_back"],
        seg_count,
        part_count,
        x_local,
        [last[0], back[-1]],
        "strips_earlier",
    )
    last[1] = send(gated(near, [outgoing]), 1)
    got = lax.all_to_all(outgoing, "grp", 0, 0, tiled=True)
    adj_now = z_inverse(
        back,
        adj_later[0],
        [terms_now],
        scalars,
        tabs["z_back"],
        seg_count,
        "now",
        last[2 : middle + 1],
    )
    common = (scalars, tabs["z_back"], seg_count)
    adj_earlier, terms = z_inverse(
        last[:-1], adj_next[0], [own, got], *common, "end_a", [adj_now]
    )
    adj_earlier = z_inverse(
        last[:-2] + last[-1:],
        adj_next[0],
        [terms],
        *common,
        "end_b",
        [],
        x_local // 2,
        adj_earlier,
    )
    return (adj_now[None], adj_earlier[None])


def solution(mesh):
    return jax.shard_map(
        local,
        mesh=mesh,
        in_specs=(P("grp", "sub", None, None), P("grp", "sub", None, None), P(), P(), P()),
        out_specs=(P("grp", "sub", None, None), P("grp", "sub", None, None)),
        check_vma=False,
    )
```

```python
import functools
import math

import jax
import jax.numpy as jnp
import numpy as np
from jax import lax
from jax.experimental import pallas as pl
from jax.experimental.pallas import tpu as pltpu
from jax.sharding import PartitionSpec as P

f32 = jnp.float32
bf16 = jnp.bfloat16
time_step = 0.5
half_phase = (math.pi * time_step / 2.0) ** 2
pair_limit = 3
face_rows = 6
padded_rows = 8
plane_block = 16
x_block = 16
last_block = 8
costs = {"lead": 0, "forward_next": 2, "tables": 32, "forward_later": 8, "first_a": 0, "first_b": 32, "back": 10, "strips_now": 8, "later": 0, "couple_now": 0, "second": 16, "strips_earlier": 8, "now": 2, "end_a": 0, "end_b": 0, "gate": 0.0}
stencil = np.array(
    (
        (0, 0, -2, 2, 0, 0),
        (0, 2, -27, 27, -2, 0),
        (-2, 27, -270, 270, -27, 2),
        (2, -27, 270, -270, 27, -2),
        (0, -2, 27, -27, 2, 0),
        (0, 0, 2, -2, 0, 0),
    ),
    np.float32,
)
weights = np.transpose(stencil) / np.float32(180.0)
params = pltpu.CompilerParams(vmem_limit_bytes=64 * 2**20 - 65536)


anywhere = pl.BlockSpec(memory_space=pl.ANY)
smem = pl.BlockSpec(memory_space=pltpu.SMEM)


def array_of(shape, dtype=f32):
    return jax.ShapeDtypeStruct(shape, dtype)


def cost(work):
    return pl.CostEstimate(flops=int(work * 1e9), bytes_accessed=1024, transcendentals=0)


def stacked_constant(table):
    high = table.astype(np.float32).astype(jnp.bfloat16)
    low = (table - high.astype(np.float64)).astype(np.float32).astype(jnp.bfloat16)
    row = np.concatenate([high, low], axis=1)
    return np.concatenate([row, row], axis=0)


def z_tables(z_cells, count):
    modes = np.arange(z_cells)[:, None]
    cells = np.arange(z_cells)[None, :]
    table = np.sqrt(np.where(modes == 0, 1.0, 2.0) / z_cells) * np.cos(
        np.pi * modes * (cells + 0.5) / z_cells
    )
    width = z_cells // count
    forward, inverse = [], []
    for me in range(count):
        order = np.concatenate([np.arange(width) + (me ^ k) * width for k in range(count)])
        mine = table[order]
        forward.append(stacked_constant(mine.T))
        inverse.append(stacked_constant(mine))
    return np.stack(forward), np.stack(inverse)


def split(value):
    high = value.astype(bf16)
    low = (value - high.astype(f32)).astype(bf16)
    return high, low


def times(value, table):
    product = jnp.dot(
        jnp.concatenate(split(value), axis=1), table, preferred_element_type=f32
    )
    width = product.shape[1] // 2
    return product[:, :width] + product[:, width:]


def flip(value, count):
    rows = value.shape[0] // count
    return jnp.concatenate([value[i * rows : (i + 1) * rows].T for i in range(count)], axis=0)


def packed(value):
    cells, width = value.shape[0], value.shape[1] // padded_rows
    rest = value[:, 4 * width : face_rows * width]
    rest = jnp.concatenate([rest[: cells // 2], rest[cells // 2 :]], axis=1)
    return jnp.concatenate([value[:, : 4 * width], rest], axis=0)


def packed_shape(cells, width):
    return cells + cells // 2, 4 * width


def lanes_of(refs, row):
    pieces = []
    for ref in refs:
        cells, width = ref.shape[0] * 2 // 3, ref.shape[1] // 4
        if row < 4:
            pieces.append(ref[:cells, row * width : (row + 1) * width])
        else:
            first = (row - 4) * width
            parts = [ref[cells:, s : s + width] for s in (first, first + 2 * width)]
            pieces.append(jnp.concatenate(parts, axis=0))
    return jnp.concatenate(pieces, axis=1)


def sine_ratio(square, terms):
    total = jnp.full_like(square, (-1.0) ** (terms - 1) / math.factorial(2 * terms - 1))
    for n in reversed(range(terms - 1)):
        total = total * square + (-1.0) ** n / math.factorial(2 * n + 1)
    return total


def cosine_entries(modes, cells, length):
    extent = jnp.full(modes.shape, length).astype(f32)
    steps = (modes * (2 * cells + 1)).astype(f32)
    period = 4.0 * extent
    turns = steps - period * jnp.floor(steps / period)
    turns = jnp.where(turns < 0.0, turns + period, turns)
    turns = jnp.where(turns >= period, turns - period, turns)
    turns = jnp.minimum(turns, period - turns)
    angle = (extent - turns) * (f32(math.pi / 2) / extent)
    scaling = jnp.sqrt(jnp.where(modes == 0, 1.0, 2.0) / extent)
    inside = (modes < length) & (cells < length) & (cells >= 0)
    return jnp.where(inside, scaling * angle * sine_ratio(angle * angle, 8), 0.0)


def stacked(table):
    row = jnp.concatenate(split(table), axis=1)
    return jnp.concatenate([row, row], axis=0)


def links(seg_count, ids_ref, box_ref, holder_ref, partner_ref, scalars_ref):
    item_count = 2 * seg_count
    part_count = holder_ref.shape[0]
    me, group, x_local = ids_ref[0], ids_ref[1], ids_ref[2]

    def find(p, found):
        return jnp.where(holder_ref[p] == group, p, found)

    part = lax.fori_loop(0, part_count, find, jnp.int32(0))
    len_x, len_y = box_ref[part, 0], box_ref[part, 1]
    head = [me, len_x, len_y, me * x_local]
    mine = [partner_ref[part, i] for i in range(item_count)]
    peers = [jnp.where(m < 0, -1, lax.div(jnp.maximum(m, 0), seg_count)) for m in mine]
    for item in range(item_count):
        wall = mine[item] < 0
        peer = jnp.maximum(peers[item], 0)
        seg = lax.rem(jnp.maximum(mine[item], 0), seg_count)
        peer_item = (1 - item // seg_count) * seg_count + seg
        send_slot, get_slot = jnp.int32(0), jnp.int32(0)
        for i in range(item_count):
            if i < item:
                send_slot += jnp.where(peers[i] == peer, 1, 0)
            link = partner_ref[peer, i]
            back = jnp.where(link < 0, -1, lax.div(jnp.maximum(link, 0), seg_count))
            get_slot += jnp.where((back == part) & (i < peer_item), 1, 0)
        scalars_ref[0, item] = head[item] if item < len(head) else jnp.int32(0)
        scalars_ref[1, item] = jnp.where(wall, 0, holder_ref[peer])
        scalars_ref[2, item] = jnp.minimum(send_slot, pair_limit - 1)
        scalars_ref[3, item] = jnp.where(wall, 0, jnp.minimum(get_slot, pair_limit - 1))
        scalars_ref[4, item] = jnp.where(wall, 0, jnp.minimum(len_x, box_ref[peer, 0]))
        scalars_ref[5, item] = jnp.where(wall, 1, 0)
    return me, len_x, len_y


def tables_kernel(seg_count, ids_ref, box_ref, holder_ref, partner_ref, *refs):
    z_ref, z_back_ref = refs[:2]
    refs = refs[-10:]
    scalars_ref, x_ref, x_back_ref, y_ref, y_back_ref, face_ref, place_ref = refs[:7]
    squares_ref, my_z_ref, my_z_back_ref = refs[7:]
    my_z_ref[...] = z_ref[ids_ref[0]]
    my_z_back_ref[...] = z_back_ref[ids_ref[0]]
    y_cells, x_cells = squares_ref.shape
    me, len_x, len_y = links(seg_count, ids_ref, box_ref, holder_ref, partner_ref, scalars_ref)
    x_local = ids_ref[2]

    def index(shape, axis):
        return lax.broadcasted_iota(jnp.int32, shape, axis)

    def cells_x(axis):
        cell = index((x_cells, x_cells), axis)
        return (lax.div(cell, x_local) ^ me) * x_local + lax.rem(cell, x_local)

    square = (x_cells, x_cells)
    x_ref[...] = stacked(cosine_entries(index(square, 1), cells_x(0), len_x))
    x_back_ref[...] = stacked(cosine_entries(index(square, 0), cells_x(1), len_x))
    square = (y_cells, y_cells)
    y_ref[...] = stacked(cosine_entries(index(square, 1), index(square, 0), len_y))
    y_back_ref[...] = stacked(cosine_entries(index(square, 0), index(square, 1), len_y))

    def cell_rows(rows):
        return jnp.where(rows < 3, rows, jnp.where(rows < face_rows, len_y - face_rows + rows, -1))

    shape = (padded_rows, y_cells)
    face = cosine_entries(index(shape, 1), cell_rows(index(shape, 0)), len_y)
    high = face.astype(bf16).astype(f32)
    both = jnp.concatenate([high, face - high], axis=0)
    face_ref[...] = jnp.concatenate([both, both], axis=1).astype(bf16)
    shape = (y_cells, 4 * padded_rows)
    column = index(shape, 1)
    turned = cosine_entries(index(shape, 0), cell_rows(lax.rem(column, padded_rows)), len_y)
    high = turned.astype(bf16).astype(f32)
    part = jnp.where(column < 2 * padded_rows, high, turned - high)
    place_ref[...] = jnp.where(column < 3 * padded_rows, part, 0.0).astype(bf16)

    shape = (y_cells, x_cells)
    ratio_x = index(shape, 1).astype(f32) / jnp.full(shape, len_x).astype(f32)
    ratio_y = index(shape, 0).astype(f32) / jnp.full(shape, len_y).astype(f32)
    squares_ref[...] = (ratio_x * ratio_x + ratio_y * ratio_y) * half_phase


def make_tables(ids, box_sizes, holder, partner, shape, z_fwd, z_inv, after):
    y_cells, x_cells = shape
    part_count, _, seg_count = partner.shape
    item_count = 2 * seg_count
    out_shapes = [
        (6, item_count),
        (2 * x_cells, 2 * x_cells),
        (2 * x_cells, 2 * x_cells),
        (2 * y_cells, 2 * y_cells),
        (2 * y_cells, 2 * y_cells),
        (2 * padded_rows, 2 * y_cells),
        (y_cells, 4 * padded_rows),
        shape,
        z_fwd.shape[1:],
        z_inv.shape[1:],
    ]
    types = [bf16] * 6 + [f32] + [bf16] * 2
    vmem = pl.BlockSpec(memory_space=pltpu.VMEM)
    out = pl.pallas_call(
        functools.partial(tables_kernel, seg_count),
        in_specs=[smem] * 4 + [vmem] * 2 + [anywhere] * len(after),
        out_specs=[smem] + [vmem] * 9,
        out_shape=[jax.ShapeDtypeStruct(out_shapes[0], jnp.int32)]
        + [array_of(s, t) for s, t in zip(out_shapes[1:], types)],
        compiler_params=params,
        cost_estimate=cost(costs["tables"]),
        name="tables",
    )(ids, box_sizes, holder, partner.reshape(part_count, item_count), z_fwd, z_inv, *after)
    names = ("x", "x_back", "y", "y_back", "face", "place", "squares", "z", "z_back")
    return out[0], dict(zip(names, out[1:]))


def factors(squares, plane, z_total):
    ratio_z = jnp.full(squares.shape, plane).astype(f32) * (1.0 / z_total)
    halved = squares + ratio_z * ratio_z * half_phase
    ratio = sine_ratio(halved, 6)
    source = (time_step**2 * ratio) * ratio
    return 2.0 - (4.0 / time_step**2) * (halved * source), source


def parcel_shapes(whole_shape, part_shape, count, parts, paired):
    near = array_of((2,) + whole_shape if paired else whole_shape)
    return [array_of(whole_shape), near] + [array_of(part_shape)] * (
        (count - 2) * parts
    )


def near_spec(shape, which, index):
    if which is None:
        return pl.BlockSpec(shape, index)
    return pl.BlockSpec((None,) + shape, lambda *a: (which,) + index(*a))


def parcel_of(out, parts):
    return [out[0], out[1]] + [out[i : i + parts] for i in range(2, len(out), parts)]


def array_in(block):
    return block[0] if isinstance(block, tuple) else block


def block_spec(block, shape, index):
    if isinstance(block, tuple):
        return pl.BlockSpec((None,) + shape, lambda *a: (block[1],) + index(*a))
    return pl.BlockSpec(shape, index)


def z_modes(field_ref, table):
    block, y_cells, z_cells = field_ref.shape
    modes = times(field_ref[...].reshape(block * y_cells, z_cells), table)
    return [modes[x * y_cells : (x + 1) * y_cells].T for x in range(block)]


def z_lead_kernel(count, me_ref, field_ref, table_ref, *refs):
    out_refs, modes_ref = refs[:-1], refs[-1]
    width = field_ref.shape[2] // count
    for x, turned in enumerate(z_modes(field_ref, table_ref[0])):
        modes_ref[x] = turned
    for k, ref in enumerate(out_refs, 2):
        start = pl.multiple_of((me_ref[0] ^ k) * width, width)
        ref[...] = modes_ref[:, pl.ds(start, width), :]


def z_forward_kernel(count, parts, after, me_ref, field_ref, table_ref, *refs):
    out_refs = refs[after:]
    width = field_ref.shape[2] // count
    part = width // parts
    for x, turned in enumerate(z_modes(field_ref, table_ref[0])):
        out_refs[0][x] = turned[:width]
        out_refs[1][x] = turned[width : 2 * width]
        for i, ref in enumerate(out_refs[2:]):
            start = 2 * width + i * part
            ref[x] = turned[start : start + part]


def z_in_specs(field, tables):
    _, y_cells, z_cells = field.shape
    return [
        pl.BlockSpec((x_block, y_cells, z_cells), lambda i, me: (i, 0, 0)),
        pl.BlockSpec((1,) + tables.shape[1:], lambda i, me: (me[0], 0, 0)),
    ]


def z_lead(field, me, tables, count):
    _, y_cells, z_cells = field.shape
    shape = (x_block, z_cells // count, y_cells)
    return pl.pallas_call(
        functools.partial(z_lead_kernel, count),
        grid=(1,),
        in_specs=[
            smem,
            pl.BlockSpec((x_block, y_cells, z_cells), lambda i: (0, 0, 0)),
            pl.BlockSpec((1,) + tables.shape[1:], lambda i: (0, 0, 0)),
        ],
        out_specs=[pl.BlockSpec(shape, lambda i: (0, 0, 0))] * (count - 2),
        out_shape=[array_of(shape)] * (count - 2),
        scratch_shapes=[pltpu.VMEM((x_block, z_cells, y_cells), f32)],
        compiler_params=params,
        cost_estimate=cost(costs["lead"]),
        name="z_lead",
    )(me, field, tables)


def z_forward(field, me, tables, count, parts, after, key, which=None, lead=0):
    size, y_cells, z_cells = field.shape
    width = z_cells // count
    part = width // parts
    rest = (count - 2) * parts
    far = size - lead * x_block
    out = pl.pallas_call(
        functools.partial(z_forward_kernel, count, parts, len(after)),
        grid_spec=pltpu.PrefetchScalarGridSpec(
            num_scalar_prefetch=1,
            grid=(size // x_block,),
            in_specs=z_in_specs(field, tables) + [anywhere] * len(after),
            out_specs=[
                pl.BlockSpec((x_block, width, y_cells), lambda i, me: (i, 0, 0)),
                near_spec((x_block, width, y_cells), which, lambda i, me: (i, 0, 0)),
            ]
            + [
                pl.BlockSpec(
                    (x_block, part, y_cells), lambda i, me: (jnp.maximum(i - lead, 0), 0, 0)
                )
            ]
            * rest,
        ),
        out_shape=parcel_shapes(
            (size, width, y_cells), (far, part, y_cells), count, parts, which is not None
        ),
        compiler_params=params,
        cost_estimate=cost(costs[key]),
        name="z_forward",
    )(me, field, tables, *after)
    return parcel_of(out, parts)


def plane_forward(block_refs, y_table, x_table):
    planes = block_refs[0].shape[1]
    value = jnp.concatenate([ref[...] for ref in block_refs], axis=0)
    x_cells, _, y_cells = value.shape
    value = jnp.swapaxes(value, 0, 1).reshape(planes * x_cells, y_cells)
    value = flip(times(value, y_table), planes)
    return times(value, x_table)


def store_faces(step, total, forced, face_table, rows_ref):
    planes = len(forced)
    for j, value in enumerate(forced):
        both = jnp.dot(
            face_table, jnp.concatenate(split(value), axis=0), preferred_element_type=f32
        )
        rows = both[:padded_rows] + both[padded_rows:]
        rows_ref[pl.ds(step * planes + j, padded_rows, stride=total), :] = rows


def send_faces(rows, x_table, face_refs):
    value = times(rows, x_table).T
    x_local = value.shape[0] // len(face_refs)
    for k, ref in enumerate(face_refs):
        ref[...] = packed(value[k * x_local : (k + 1) * x_local])


def first_kernel(count, held, last, offset, z_total, me_ref, *refs):
    blocks, refs = refs[:held], refs[held:]
    squares_ref, y_ref, x_ref, face_ref = refs[:4]
    spectral = plane_forward(blocks, y_ref[...], x_ref[...])
    if not last:
        out_ref, rows_ref = refs[-2:]
    else:
        x_back_ref, before_ref = refs[4:6]
        out_ref, face_refs, rows_ref = refs[-2 - count], refs[-1 - count : -1], refs[-1]
    planes, y_modes, x_modes = out_ref.shape
    total = rows_ref.shape[0] // padded_rows
    first = me_ref[0] * (z_total // count) + offset + pl.program_id(0) * planes
    forced = []
    for j in range(planes):
        mine = spectral[j * y_modes : (j + 1) * y_modes]
        wave, source = factors(squares_ref[...], first + j, z_total)
        out_ref[j] = wave * mine
        forced.append(source * mine)
    store_faces(pl.program_id(0), total, forced, face_ref[...], rows_ref)
    if last:

        @pl.when(pl.program_id(0) == pl.num_programs(0) - 1)
        def _():
            rows = []
            for r in range(padded_rows):
                rows += [ref[r * total : (r + 1) * total] for ref in (before_ref, rows_ref)]
            send_faces(jnp.concatenate(rows, axis=0), x_back_ref[...], face_refs)


def difference_kernel(count, *refs):
    blocks = refs[:count]
    waved_ref, y_ref, x_ref, out_ref = refs[count : count + 3] + refs[-1:]
    spectral = plane_forward(blocks, y_ref[...], x_ref[...])
    out_ref[...] = waved_ref[...] - spectral.reshape(waved_ref.shape)


def second_kernel(count, skip, z_total, me_ref, *refs):
    sums, refs = refs[:count], refs[count:]
    partial_ref, squares_ref, x_ref, x_back_ref, y_back_ref, face_ref, place_ref = refs[:7]
    refs = refs[7 + skip :]
    out_refs, face_refs = refs[: count + 1], refs[count + 1 : 2 * count + 1]
    rows_ref, terms_ref = refs[2 * count + 1 :]
    step = pl.program_id(0)
    planes = partial_ref.shape[0]
    total = rows_ref.shape[0] // padded_rows

    @pl.when(step == 0)
    def _():
        rows = [lanes_of(sums, r) for r in range(face_rows)]
        rows += [jnp.zeros_like(rows[0])] * (padded_rows - face_rows)
        terms_ref[...] = times(jnp.concatenate(rows, axis=0), x_ref[...])

    waved, forced = [], []
    for j in range(planes):
        rows = terms_ref[pl.ds(step * planes + j, padded_rows, stride=total), :]
        high = rows.astype(bf16).astype(f32)
        low = rows - high
        stack = jnp.concatenate([high, low, high, jnp.zeros_like(rows)], axis=0).astype(bf16)
        added = jnp.dot(place_ref[...], stack, preferred_element_type=f32)
        mine = partial_ref[j] + added
        wave, source = factors(squares_ref[...], me_ref[0] * total + step * planes + j, z_total)
        waved.append(wave * mine)
        forced.append(source * mine)
    store_faces(step, total, forced, face_ref[...], rows_ref)
    store_cells(waved, x_back_ref[...], y_back_ref[...], out_refs)

    @pl.when(step == pl.num_programs(0) - 1)
    def _():
        send_faces(rows_ref[...], x_back_ref[...], face_refs)


def store_cells(waved, x_table, y_table, out_refs):
    planes = len(waved)
    value = times(jnp.concatenate(waved, axis=0), x_table)
    value = times(flip(value, planes), y_table)
    value = value.reshape(planes, value.shape[0] // planes, value.shape[1])
    value = jnp.swapaxes(value, 0, 1)
    first = 0
    for ref in out_refs:
        ref[...] = value[first : first + ref.shape[0]]
        first += ref.shape[0]


def inverse_kernel(count, waved_ref, x_ref, y_ref, pair_ref, *out_refs):
    waved = [waved_ref[j] for j in range(waved_ref.shape[0])]
    store_cells(waved, x_ref[...], y_ref[...], out_refs)


def whole(shape):
    zeros = (0,) * len(shape)
    return pl.BlockSpec(shape, lambda i, *s: zeros)


def plane_specs(blocks, planes=None, first=0):
    specs = []
    for b in blocks:
        x_cells, held, y_cells = array_in(b).shape[-3:]
        start = first if held == planes else 0
        specs.append(
            block_spec(
                b, (x_cells, plane_block, y_cells), lambda i, *s, start=start: (0, start + i, 0)
            )
        )
    return specs


def mode_spec(shape, first=0):
    return pl.BlockSpec((plane_block,) + shape[1:], lambda i, *s: (first + i, 0, 0))


def first_part(blocks, place, tabs, before, after, key):
    own = blocks[-1].shape[1]
    x_local, planes, _ = blocks[0].shape
    y_modes, x_modes = tabs["squares"].shape
    small = [tabs["squares"], tabs["y"], tabs["x"], tabs["face"]]
    count = x_modes // x_local
    last = before is not None
    offset = planes - own if last else 0
    shape = (planes, y_modes, x_modes)
    operands = [place, *map(array_in, blocks), *small]
    in_specs = plane_specs(blocks, planes, offset // plane_block) + [whole(t.shape) for t in small]
    rows_shape = (padded_rows * own, x_modes)
    out_specs = [mode_spec(shape, offset // plane_block)]
    out_shape = [array_of(shape)]
    scratch, aliases = [], {}
    if last:
        waved, rows = before
        operands += [tabs["x_back"], rows, waved]
        in_specs += [whole(tabs["x_back"].shape), whole(rows.shape), anywhere]
        aliases = {len(operands) - 1: 0}
        face_shape = packed_shape(x_local, planes)
        out_specs += [whole(face_shape)] * count
        out_shape += [array_of(face_shape)] * count
        scratch = [pltpu.VMEM(rows_shape, f32)]
    else:
        out_specs += [whole(rows_shape)]
        out_shape += [array_of(rows_shape)]
    operands += after
    in_specs += [anywhere] * len(after)
    out = pl.pallas_call(
        functools.partial(first_kernel, count, len(blocks), last, offset, planes * count),
        grid_spec=pltpu.PrefetchScalarGridSpec(
            num_scalar_prefetch=0,
            grid=(own // plane_block,),
            in_specs=[smem]
            + in_specs,
            out_specs=out_specs,
            scratch_shapes=scratch,
        ),
        out_shape=out_shape,
        input_output_aliases=aliases,
        compiler_params=params,
        cost_estimate=cost(costs[key]),
        name="first_modes",
    )(*operands)
    return out[0], out[1:] if last else out[1]


def difference_part(blocks, waved, tabs, after):
    count = len(blocks)
    small = [tabs["y"], tabs["x"]]
    return pl.pallas_call(
        functools.partial(difference_kernel, count),
        grid=(waved.shape[0] // plane_block,),
        in_specs=plane_specs(blocks)
        + [mode_spec(waved.shape)]
        + [whole(t.shape) for t in small]
        + [anywhere] * len(after),
        out_specs=mode_spec(waved.shape),
        out_shape=array_of(waved.shape),
        compiler_params=params,
        cost_estimate=cost(costs["later"]),
        name="later_modes",
    )(*map(array_in, blocks), waved, *small, *after)


def second_part(sums, partial, place, tabs, after):
    count = len(sums)
    planes, y_modes, x_modes = partial.shape
    y_cells = tabs["y_back"].shape[1] // 2
    x_local = x_modes // count
    face_shape = packed_shape(x_local, planes)
    sizes = [x_local] * (count - 1) + [x_local // 2] * 2
    small = [tabs[n] for n in ("squares", "x", "x_back", "y_back", "face", "place")]
    out = pl.pallas_call(
        functools.partial(second_kernel, count, len(after), planes * count),
        grid_spec=pltpu.PrefetchScalarGridSpec(
            num_scalar_prefetch=0,
            grid=(planes // plane_block,),
            in_specs=[smem]
            + [whole(s.shape) for s in sums]
            + [mode_spec(partial.shape)]
            + [whole(t.shape) for t in small]
            + [anywhere] * len(after),
            out_specs=[
                pl.BlockSpec((n, plane_block, y_cells), lambda i, *s: (0, i, 0)) for n in sizes
            ]
            + [whole(face_shape)] * count,
            scratch_shapes=[
                pltpu.VMEM((padded_rows * planes, x_modes), f32),
                pltpu.VMEM((padded_rows * planes, x_modes), f32),
            ],
        ),
        out_shape=[array_of((n, planes, y_cells)) for n in sizes]
        + [array_of(face_shape)] * count,
        compiler_params=params,
        cost_estimate=cost(costs["second"]),
        name="second_modes",
    )(place, *sums, partial, *small, *after)
    return list(out[: count + 1]), out[count + 1 :]


def inverse_part(waved, tabs, count, key, pair):
    planes, y_modes, x_modes = waved.shape
    y_cells = tabs["y_back"].shape[1] // 2
    x_local = x_modes // count
    small = [tabs["x_back"], tabs["y_back"]]
    shape = (x_local, plane_block, y_cells)
    out = pl.pallas_call(
        functools.partial(inverse_kernel, count),
        grid=(planes // plane_block,),
        in_specs=[mode_spec(waved.shape)] + [whole(t.shape) for t in small] + [anywhere],
        out_specs=[pl.BlockSpec(shape, lambda i: (0, i, 0))]
        + [near_spec(shape, 1, lambda i: (0, i, 0))]
        + [pl.BlockSpec(shape, lambda i: (0, i, 0))] * (count - 2),
        out_shape=parcel_shapes(
            (x_local, planes, y_cells), (x_local, planes, y_cells), count, 1, True
        ),
        input_output_aliases={3: 1},
        compiler_params=params,
        cost_estimate=cost(costs[key]),
        name="modes_to_cells",
    )(waved, *small, pair)
    return list(out)


def strips_kernel(count, seg_count, scalars_ref, *refs):
    faces, table_ref, (own_ref, send_ref) = refs[:count], refs[count], refs[-2:]
    rows, x_local, z_cells = own_ref.shape
    value = jnp.concatenate([lanes_of(faces, r) for r in range(rows)], axis=0)
    value = times(value, table_ref[...]).reshape(rows, x_local, z_cells)
    own_ref[...] = value
    seg_cells = z_cells // seg_count
    groups = z_cells // seg_cells
    lane = lax.broadcasted_iota(jnp.int32, (8, z_cells), 1) // seg_cells
    for item in range(2 * seg_count):
        face, seg = item // seg_count, item % seg_count
        dest, slot, wall = scalars_ref[1, item], scalars_ref[2, item], scalars_ref[5, item]

        @pl.when(wall == 0)
        def _():
            for j in range(3):
                packed = jnp.zeros((8, z_cells), f32)
                for c in range(groups):
                    piece = value[face * 3 + j, 8 * c : 8 * (c + 1)]
                    shift = (c - seg) * seg_cells % z_cells
                    if shift:
                        piece = pltpu.roll(piece, shift, 1)
                    packed = jnp.where(lane == c, piece, packed)
                send_ref[dest, slot, j] = packed


def strips_part(faces, scalars, tables, seg_count, part_count, x_local, after, key):
    count = len(faces)
    z_cells = tables.shape[1] // 2
    own_shape = (face_rows, x_local, z_cells)
    send_shape = (part_count, pair_limit, 3, 8, z_cells)
    return pl.pallas_call(
        functools.partial(strips_kernel, count, seg_count),
        grid_spec=pltpu.PrefetchScalarGridSpec(
            num_scalar_prefetch=0,
            grid=(1,),
            in_specs=[smem]
            + [pl.BlockSpec(f.shape, lambda i: (0, 0)) for f in faces]
            + [pl.BlockSpec(tables.shape, lambda i: (0, 0))]
            + [anywhere] * len(after),
            out_specs=[
                pl.BlockSpec(own_shape, lambda i: (0, 0, 0)),
                pl.BlockSpec(send_shape, lambda i: (0, 0, 0, 0, 0)),
            ],
        ),
        out_shape=[array_of(own_shape), array_of(send_shape)],
        compiler_params=params,
        cost_estimate=cost(costs[key]),
        name="strips",
    )(scalars, *faces, tables, *after)


def coupled_terms(seg_count, scalars_ref, own_ref, got_ref):
    _, x_local, z_cells = own_ref.shape
    seg_cells = z_cells // seg_count
    groups = z_cells // seg_cells
    lane = lax.broadcasted_iota(jnp.int32, (8, z_cells), 1) // seg_cells
    row_x = scalars_ref[0, 3] + lax.broadcasted_iota(jnp.int32, (x_local, z_cells), 0)
    lane_all = lax.broadcasted_iota(jnp.int32, (x_local, z_cells), 1) // seg_cells
    terms = []
    for face in range(2):
        limit = jnp.zeros((x_local, z_cells), jnp.int32)
        other = [[jnp.zeros((8, z_cells), f32)] * groups for _ in range(3)]
        for seg in range(seg_count):
            item = face * seg_count + seg
            source, slot = scalars_ref[1, item], scalars_ref[3, item]
            limit = jnp.where(lane_all == seg, scalars_ref[4, item], limit)
            for j in range(3):
                packed = got_ref[source, slot, j]
                for c in range(groups):
                    shift = (seg - c) * seg_cells % z_cells
                    piece = pltpu.roll(packed, shift, 1) if shift else packed
                    other[j][c] = jnp.where(lane == seg, piece, other[j][c])
        other = [jnp.concatenate(o, axis=0) for o in other]
        own = [own_ref[face * 3 + j] for j in range(3)]
        low, high = (other, own) if face == 0 else (own, other)
        keep = row_x < limit
        for i in range(3):
            row = weights[3 + i] if face == 0 else weights[i]
            total = jnp.zeros((x_local, z_cells), f32)
            for j in range(6):
                if row[j] != 0:
                    total = total + float(row[j]) * (low + high)[j]
            terms.append(jnp.where(keep, total, 0.0))
    return terms


def couple_kernel(count, seg_count, skip, scalars_ref, own_ref, got_ref, table_ref, *out_refs):
    out_refs = out_refs[skip:]
    terms = coupled_terms(seg_count, scalars_ref, own_ref, got_ref)
    for r, term in enumerate(terms):
        out_refs[0][r] = term
    _, x_local, z_cells = own_ref.shape
    blank = [jnp.zeros((x_local, z_cells), f32)] * (padded_rows - len(terms))
    value = times(jnp.concatenate(terms + blank, axis=0), table_ref[...]).T
    width = z_cells // count
    for k in range(count):
        out_refs[1 + k][...] = packed(value[k * width : (k + 1) * width])


def couple_part(own, got, scalars, tables, seg_count, count, after, key):
    rows, x_local, z_cells = own.shape
    sum_shape = packed_shape(z_cells // count, x_local)
    out = pl.pallas_call(
        functools.partial(couple_kernel, count, seg_count, len(after)),
        grid_spec=pltpu.PrefetchScalarGridSpec(
            num_scalar_prefetch=0,
            grid=(1,),
            in_specs=[smem]
            + [
                pl.BlockSpec(own.shape, lambda i: (0, 0, 0)),
                pl.BlockSpec(got.shape, lambda i: (0, 0, 0, 0, 0)),
                pl.BlockSpec(tables.shape, lambda i: (0, 0)),
            ]
            + [anywhere] * len(after),
            out_specs=[pl.BlockSpec(own.shape, lambda i: (0, 0, 0))]
            + [pl.BlockSpec(sum_shape, lambda i: (0, 0))] * count,
        ),
        out_shape=[array_of(own.shape)] + [array_of(sum_shape)] * count,
        compiler_params=params,
        cost_estimate=cost(costs[key]),
        name="couple",
    )(scalars, own, got, tables, *after)
    return out[0], out[1:]


def z_inverse_kernel(count, seg_count, offset, scalars_ref, *refs):
    blocks, (earlier_ref, table_ref) = refs[:count], refs[count : count + 2]
    block, y_cells, z_cells = earlier_ref.shape
    len_x, len_y = scalars_ref[0, 1], scalars_ref[0, 2]
    step = offset + pl.program_id(0)
    if seg_count:
        own_ref, got_ref = refs[count + 2 : count + 4]
        out_ref, terms_ref = refs[-2:]

        @pl.when(pl.program_id(0) == 0)
        def _():
            for r, term in enumerate(coupled_terms(seg_count, scalars_ref, own_ref, got_ref)):
                terms_ref[r] = term

    else:
        terms_ref, out_ref = refs[count + 2], refs[-1]
    first = scalars_ref[0, 3] + step * block
    row = lax.broadcasted_iota(jnp.int32, (y_cells, z_cells), 0)
    pieces = []
    for x in range(block):
        modes = jnp.concatenate([ref[x] for ref in blocks], axis=0)
        pieces.append(modes.T)
    value = times(jnp.concatenate(pieces, axis=0), table_ref[...])
    for x in range(block):
        limit = jnp.where(first + x < len_x, len_y, 0)
        out_ref[x] = value[x * y_cells : (x + 1) * y_cells] - jnp.where(
            row < limit, earlier_ref[x], 0.0
        )
    start = pl.multiple_of(jnp.minimum((len_y - 3) // 8 * 8, y_cells - 16), 8)
    mine = pl.ds(pl.multiple_of(step * block, block), block)
    terms = [terms_ref[r, mine][:, None, :] for r in range(face_rows)]
    low_row = lax.broadcasted_iota(jnp.int32, (block, 8, z_cells), 1)
    high_row = start + lax.broadcasted_iota(jnp.int32, (block, 16, z_cells), 1)
    low = out_ref[:, 0:8, :]
    for r in range(3):
        low = low + jnp.where(low_row == r, terms[r], 0.0)
    out_ref[:, 0:8, :] = low
    high = out_ref[:, pl.ds(start, 16), :]
    for r in range(3):
        high = high + jnp.where(high_row == len_y - 3 + r, terms[3 + r], 0.0)
    out_ref[:, pl.ds(start, 16), :] = high


def z_inverse(
    blocks, earlier, terms, scalars, tables, seg_count, key, after=(), first=0, filled=None
):
    count = len(blocks)
    x_local, y_cells, z_cells = earlier.shape
    width = z_cells // count
    block = last_block if first else x_block
    start = first // block
    given = len(terms) == 1
    operands = [scalars, *map(array_in, blocks), earlier, tables, *terms, *after]
    aliases = {}
    if filled is not None:
        aliases = {len(operands): 0}
        operands.append(filled)
    terms_shape = (face_rows, x_local, z_cells)

    def rows_from(begin):
        return lambda i: (begin + i, 0, 0)

    out = pl.pallas_call(
        functools.partial(z_inverse_kernel, count, 0 if given else seg_count, start),
        grid_spec=pl.GridSpec(
            grid=(array_in(blocks[-1]).shape[-3] // block,),
            in_specs=[smem]
            + [
                block_spec(
                    b,
                    (block, width, y_cells),
                    rows_from(start if array_in(b).shape[-3] == x_local else 0),
                )
                for b in blocks
            ]
            + [pl.BlockSpec((block, y_cells, z_cells), rows_from(start))]
            + [whole(t.shape) for t in (tables, *terms)]
            + [anywhere] * (len(after) + len(aliases)),
            out_specs=[pl.BlockSpec((block, y_cells, z_cells), rows_from(start))]
            + ([] if given else [whole(terms_shape)]),
        ),
        out_shape=[array_of(earlier.shape)] + ([] if given else [array_of(terms_shape)]),
        input_output_aliases=aliases,
        compiler_params=params,
        cost_estimate=cost(costs[key]),
        name="z_inverse",
    )(*operands)
    return out[0] if given else out


def gate_kernel(*refs):
    pass


def gated(array, after):
    return pl.pallas_call(
        gate_kernel,
        in_specs=[anywhere] * (1 + len(after)),
        out_specs=anywhere,
        out_shape=array_of(array.shape),
        input_output_aliases={0: 0},
        compiler_params=params,
        cost_estimate=cost(costs["gate"]),
        name="gate",
    )(array, *after)


def pairs_at(count, distance):
    return [(i, i ^ distance) for i in range(count)]


def send(block, distance):
    count = lax.axis_size("sub")
    return lax.ppermute(block, "sub", pairs_at(count, distance))


def exchange(blocks):
    return [blocks[0]] + [send(blocks[k], k) for k in range(1, len(blocks))]


def local(adj_next, adj_later, box_sizes, holder, partner):
    part_count = holder.shape[0]
    seg_count = partner.shape[2]
    my_group = lax.axis_index("grp").astype(jnp.int32)
    me = lax.axis_index("sub").astype(jnp.int32)
    count = lax.axis_size("sub")
    _, x_local, y_cells, z_cells = adj_next.shape
    x_total = x_local * count
    z_local = z_cells // count
    z_fwd, z_inv = (jnp.asarray(t) for t in z_tables(z_cells, count))
    place = me.reshape(1)

    middle = count // 2
    lead = z_lead(adj_next[0], place, z_fwd, count)
    parcel = z_forward(adj_next[0], place, z_fwd, count, 2, [lead[0]], "forward_next", lead=1)
    lead = [send(b, k) for k, b in enumerate(lead, 2)]
    first_a, first_b = [parcel[0], send(parcel[1], 1)], [parcel[0]]
    first_b.append(first_a[1])
    for c, blocks in enumerate((first_a, first_b)):
        for k in range(2, count):
            blocks += [lead[k - 2], send(parcel[k][c], k)]

    ids = jnp.stack([me, my_group, jnp.int32(x_local)])
    scalars, tabs = make_tables(
        ids,
        box_sizes,
        holder,
        partner,
        (y_cells, x_total),
        z_fwd,
        z_inv,
        [parcel[0]],
    )
    later = z_forward(
        adj_later[0], place, z_fwd, count, 1, [tabs["squares"]], "forward_later", 0
    )
    pair = later[1]
    later = [later[0], None] + [b[0] for b in later[2:]]
    for k in range(2, middle + 1):
        later[k] = send(later[k], k)

    before = first_part(first_a, place, tabs, None, [later[0]], "first_a")
    waved, faces = first_part(first_b, place, tabs, before, [], "first_b")
    faces = exchange(faces)
    for k in range(middle + 1, count):
        later[k] = send(gated(later[k], [faces[1]]), k)
    back = inverse_part(waved, tabs, count, "back", pair)
    near = send(back[1], 1)
    later[1] = (near, 0)
    back[1] = (near, 1)
    own, outgoing = strips_part(
        faces,
        scalars,
        tabs["z_back"],
        seg_count,
        part_count,
        x_local,
        [back[0], *later[2 : middle + 1]],
        "strips_now",
    )
    for k in range(2, count):
        back[k] = send(gated(back[k], [outgoing]), k)
    got = lax.all_to_all(outgoing, "grp", 0, 0, tiled=True)
    partial = difference_part(later, waved, tabs, [outgoing])
    terms_now, sums = couple_part(
        own,
        got,
        scalars,
        tabs["z"],
        seg_count,
        count,
        [partial],
        "couple_now",
    )
    last, faces = second_part(
        exchange(sums), partial, place, tabs, back[2 : middle + 1]
    )
    faces = exchange(faces)
    near = last[1]
    last[2:] = [send(b, min(k, count - 1)) for k, b in enumerate(last[2:], 2)]
    own, outgoing = strips_part(
        faces,
        scalars,
        tabs["z_back"],
        seg_count,
        part_count,
        x_local,
        [last[0], back[-1]],
        "strips_earlier",
    )
    last[1] = send(gated(near, [outgoing]), 1)
    got = lax.all_to_all(outgoing, "grp", 0, 0, tiled=True)
    adj_now = z_inverse(
        back,
        adj_later[0],
        [terms_now],
        scalars,
        tabs["z_back"],
        seg_count,
        "now",
        last[2 : middle + 1],
    )
    common = (scalars, tabs["z_back"], seg_count)
    adj_earlier, terms = z_inverse(
        last[:-1], adj_next[0], [own, got], *common, "end_a", [adj_now]
    )
    adj_earlier = z_inverse(
        last[:-2] + last[-1:],
        adj_next[0],
        [terms],
        *common,
        "end_b",
        [],
        x_local // 2,
        adj_earlier,
    )
    return (adj_now[None], adj_earlier[None])


def solution(mesh):
    return jax.shard_map(
        local,
        mesh=mesh,
        in_specs=(P("grp", "sub", None, None), P("grp", "sub", None, None), P(), P(), P()),
        out_specs=(P("grp", "sub", None, None), P("grp", "sub", None, None)),
        check_vma=False,
    )
```

```python
import functools
import math

import jax
import jax.numpy as jnp
import numpy as np
from jax import lax
from jax.experimental import pallas as pl
from jax.experimental.pallas import tpu as pltpu
from jax.sharding import PartitionSpec as P

f32 = jnp.float32
bf16 = jnp.bfloat16
time_step = 0.5
half_phase = (math.pi * time_step / 2.0) ** 2
pair_limit = 3
face_rows = 6
padded_rows = 8
plane_block = 16
x_block = 16
lead_block = 8
costs = {"lead": 0, "forward_next": 2, "tables": 32, "forward_later": 8, "first_a": 0, "first_b": 32, "back": 10, "strips_now": 8, "later": 0, "couple_now": 0, "second": 16, "strips_earlier": 8, "now": 2, "end_a": 0, "end_b": 0, "gate": 0.0}
stencil = np.array(
    (
        (0, 0, -2, 2, 0, 0),
        (0, 2, -27, 27, -2, 0),
        (-2, 27, -270, 270, -27, 2),
        (2, -27, 270, -270, 27, -2),
        (0, -2, 27, -27, 2, 0),
        (0, 0, 2, -2, 0, 0),
    ),
    np.float32,
)
weights = np.transpose(stencil) / np.float32(180.0)
params = pltpu.CompilerParams(vmem_limit_bytes=64 * 2**20 - 65536)


anywhere = pl.BlockSpec(memory_space=pl.ANY)
smem = pl.BlockSpec(memory_space=pltpu.SMEM)


def array_of(shape, dtype=f32):
    return jax.ShapeDtypeStruct(shape, dtype)


def cost(work):
    return pl.CostEstimate(flops=int(work * 1e9), bytes_accessed=1024, transcendentals=0)


def stacked_constant(table):
    high = table.astype(np.float32).astype(jnp.bfloat16)
    low = (table - high.astype(np.float64)).astype(np.float32).astype(jnp.bfloat16)
    row = np.concatenate([high, low], axis=1)
    return np.concatenate([row, row], axis=0)


def z_tables(z_cells, count):
    modes = np.arange(z_cells)[:, None]
    cells = np.arange(z_cells)[None, :]
    table = np.sqrt(np.where(modes == 0, 1.0, 2.0) / z_cells) * np.cos(
        np.pi * modes * (cells + 0.5) / z_cells
    )
    width = z_cells // count
    forward, inverse = [], []
    for me in range(count):
        order = np.concatenate([np.arange(width) + (me ^ k) * width for k in range(count)])
        mine = table[order]
        forward.append(stacked_constant(mine.T))
        inverse.append(stacked_constant(mine))
    return np.stack(forward), np.stack(inverse)


def split(value):
    high = value.astype(bf16)
    low = (value - high.astype(f32)).astype(bf16)
    return high, low


def times(value, table):
    product = jnp.dot(
        jnp.concatenate(split(value), axis=1), table, preferred_element_type=f32
    )
    width = product.shape[1] // 2
    return product[:, :width] + product[:, width:]


def flip(value, count):
    rows = value.shape[0] // count
    return jnp.concatenate([value[i * rows : (i + 1) * rows].T for i in range(count)], axis=0)


def packed(value):
    cells, width = value.shape[0], value.shape[1] // padded_rows
    rest = value[:, 4 * width : face_rows * width]
    rest = jnp.concatenate([rest[: cells // 2], rest[cells // 2 :]], axis=1)
    return jnp.concatenate([value[:, : 4 * width], rest], axis=0)


def packed_shape(cells, width):
    return cells + cells // 2, 4 * width


def lanes_of(refs, row):
    pieces = []
    for ref in refs:
        cells, width = ref.shape[0] * 2 // 3, ref.shape[1] // 4
        if row < 4:
            pieces.append(ref[:cells, row * width : (row + 1) * width])
        else:
            first = (row - 4) * width
            parts = [ref[cells:, s : s + width] for s in (first, first + 2 * width)]
            pieces.append(jnp.concatenate(parts, axis=0))
    return jnp.concatenate(pieces, axis=1)


def sine_ratio(square, terms):
    total = jnp.full_like(square, (-1.0) ** (terms - 1) / math.factorial(2 * terms - 1))
    for n in reversed(range(terms - 1)):
        total = total * square + (-1.0) ** n / math.factorial(2 * n + 1)
    return total


def cosine_entries(modes, cells, length):
    extent = jnp.full(modes.shape, length).astype(f32)
    steps = (modes * (2 * cells + 1)).astype(f32)
    period = 4.0 * extent
    turns = steps - period * jnp.floor(steps / period)
    turns = jnp.where(turns < 0.0, turns + period, turns)
    turns = jnp.where(turns >= period, turns - period, turns)
    turns = jnp.minimum(turns, period - turns)
    angle = (extent - turns) * (f32(math.pi / 2) / extent)
    scaling = jnp.sqrt(jnp.where(modes == 0, 1.0, 2.0) / extent)
    inside = (modes < length) & (cells < length) & (cells >= 0)
    return jnp.where(inside, scaling * angle * sine_ratio(angle * angle, 8), 0.0)


def stacked(table):
    row = jnp.concatenate(split(table), axis=1)
    return jnp.concatenate([row, row], axis=0)


def links(seg_count, ids_ref, box_ref, holder_ref, partner_ref, scalars_ref):
    item_count = 2 * seg_count
    part_count = holder_ref.shape[0]
    me, group, x_local = ids_ref[0], ids_ref[1], ids_ref[2]

    def find(p, found):
        return jnp.where(holder_ref[p] == group, p, found)

    part = lax.fori_loop(0, part_count, find, jnp.int32(0))
    len_x, len_y = box_ref[part, 0], box_ref[part, 1]
    head = [me, len_x, len_y, me * x_local]
    mine = [partner_ref[part, i] for i in range(item_count)]
    peers = [jnp.where(m < 0, -1, lax.div(jnp.maximum(m, 0), seg_count)) for m in mine]
    for item in range(item_count):
        wall = mine[item] < 0
        peer = jnp.maximum(peers[item], 0)
        seg = lax.rem(jnp.maximum(mine[item], 0), seg_count)
        peer_item = (1 - item // seg_count) * seg_count + seg
        send_slot, get_slot = jnp.int32(0), jnp.int32(0)
        for i in range(item_count):
            if i < item:
                send_slot += jnp.where(peers[i] == peer, 1, 0)
            link = partner_ref[peer, i]
            back = jnp.where(link < 0, -1, lax.div(jnp.maximum(link, 0), seg_count))
            get_slot += jnp.where((back == part) & (i < peer_item), 1, 0)
        scalars_ref[0, item] = head[item] if item < len(head) else jnp.int32(0)
        scalars_ref[1, item] = jnp.where(wall, 0, holder_ref[peer])
        scalars_ref[2, item] = jnp.minimum(send_slot, pair_limit - 1)
        scalars_ref[3, item] = jnp.where(wall, 0, jnp.minimum(get_slot, pair_limit - 1))
        scalars_ref[4, item] = jnp.where(wall, 0, jnp.minimum(len_x, box_ref[peer, 0]))
        scalars_ref[5, item] = jnp.where(wall, 1, 0)
    return me, len_x, len_y


def tables_kernel(seg_count, ids_ref, box_ref, holder_ref, partner_ref, *refs):
    z_ref, z_back_ref = refs[:2]
    refs = refs[-10:]
    scalars_ref, x_ref, x_back_ref, y_ref, y_back_ref, face_ref, place_ref = refs[:7]
    squares_ref, my_z_ref, my_z_back_ref = refs[7:]
    my_z_ref[...] = z_ref[ids_ref[0]]
    my_z_back_ref[...] = z_back_ref[ids_ref[0]]
    y_cells, x_cells = squares_ref.shape
    me, len_x, len_y = links(seg_count, ids_ref, box_ref, holder_ref, partner_ref, scalars_ref)
    x_local = ids_ref[2]

    def index(shape, axis):
        return lax.broadcasted_iota(jnp.int32, shape, axis)

    def cells_x(axis):
        cell = index((x_cells, x_cells), axis)
        return (lax.div(cell, x_local) ^ me) * x_local + lax.rem(cell, x_local)

    square = (x_cells, x_cells)
    x_ref[...] = stacked(cosine_entries(index(square, 1), cells_x(0), len_x))
    x_back_ref[...] = stacked(cosine_entries(index(square, 0), cells_x(1), len_x))
    square = (y_cells, y_cells)
    y_ref[...] = stacked(cosine_entries(index(square, 1), index(square, 0), len_y))
    y_back_ref[...] = stacked(cosine_entries(index(square, 0), index(square, 1), len_y))

    def cell_rows(rows):
        return jnp.where(rows < 3, rows, jnp.where(rows < face_rows, len_y - face_rows + rows, -1))

    shape = (padded_rows, y_cells)
    face = cosine_entries(index(shape, 1), cell_rows(index(shape, 0)), len_y)
    high = face.astype(bf16).astype(f32)
    both = jnp.concatenate([high, face - high], axis=0)
    face_ref[...] = jnp.concatenate([both, both], axis=1).astype(bf16)
    shape = (y_cells, 4 * padded_rows)
    column = index(shape, 1)
    turned = cosine_entries(index(shape, 0), cell_rows(lax.rem(column, padded_rows)), len_y)
    high = turned.astype(bf16).astype(f32)
    part = jnp.where(column < 2 * padded_rows, high, turned - high)
    place_ref[...] = jnp.where(column < 3 * padded_rows, part, 0.0).astype(bf16)

    shape = (y_cells, x_cells)
    ratio_x = index(shape, 1).astype(f32) / jnp.full(shape, len_x).astype(f32)
    ratio_y = index(shape, 0).astype(f32) / jnp.full(shape, len_y).astype(f32)
    squares_ref[...] = (ratio_x * ratio_x + ratio_y * ratio_y) * half_phase


def make_tables(ids, box_sizes, holder, partner, shape, z_fwd, z_inv, after):
    y_cells, x_cells = shape
    part_count, _, seg_count = partner.shape
    item_count = 2 * seg_count
    out_shapes = [
        (6, item_count),
        (2 * x_cells, 2 * x_cells),
        (2 * x_cells, 2 * x_cells),
        (2 * y_cells, 2 * y_cells),
        (2 * y_cells, 2 * y_cells),
        (2 * padded_rows, 2 * y_cells),
        (y_cells, 4 * padded_rows),
        shape,
        z_fwd.shape[1:],
        z_inv.shape[1:],
    ]
    types = [bf16] * 6 + [f32] + [bf16] * 2
    vmem = pl.BlockSpec(memory_space=pltpu.VMEM)
    out = pl.pallas_call(
        functools.partial(tables_kernel, seg_count),
        in_specs=[smem] * 4 + [vmem] * 2 + [anywhere] * len(after),
        out_specs=[smem] + [vmem] * 9,
        out_shape=[jax.ShapeDtypeStruct(out_shapes[0], jnp.int32)]
        + [array_of(s, t) for s, t in zip(out_shapes[1:], types)],
        compiler_params=params,
        cost_estimate=cost(costs["tables"]),
        name="tables",
    )(ids, box_sizes, holder, partner.reshape(part_count, item_count), z_fwd, z_inv, *after)
    names = ("x", "x_back", "y", "y_back", "face", "place", "squares", "z", "z_back")
    return out[0], dict(zip(names, out[1:]))


def factors(squares, plane, z_total):
    ratio_z = jnp.full(squares.shape, plane).astype(f32) * (1.0 / z_total)
    halved = squares + ratio_z * ratio_z * half_phase
    ratio = sine_ratio(halved, 6)
    source = (time_step**2 * ratio) * ratio
    return 2.0 - (4.0 / time_step**2) * (halved * source), source


def parcel_shapes(whole_shape, part_shape, count, parts, paired):
    near = array_of((2,) + whole_shape if paired else whole_shape)
    return [array_of(whole_shape), near] + [array_of(part_shape)] * (
        (count - 2) * parts
    )


def near_spec(shape, which, index):
    if which is None:
        return pl.BlockSpec(shape, index)
    return pl.BlockSpec((None,) + shape, lambda *a: (which,) + index(*a))


def parcel_of(out, parts):
    return [out[0], out[1]] + [out[i : i + parts] for i in range(2, len(out), parts)]


def array_in(block):
    return block[0] if isinstance(block, tuple) else block


def block_spec(block, shape, index):
    if isinstance(block, tuple):
        return pl.BlockSpec((None,) + shape, lambda *a: (block[1],) + index(*a))
    return pl.BlockSpec(shape, index)


def z_modes(field_ref, table):
    block, y_cells, z_cells = field_ref.shape
    modes = times(field_ref[...].reshape(block * y_cells, z_cells), table)
    return [modes[x * y_cells : (x + 1) * y_cells].T for x in range(block)]


def z_lead_kernel(count, me_ref, field_ref, table_ref, *refs):
    out_refs, modes_ref = refs[:-1], refs[-1]
    width = field_ref.shape[2] // count
    for x, turned in enumerate(z_modes(field_ref, table_ref[0])):
        modes_ref[x] = turned
    for k, ref in enumerate(out_refs, 2):
        start = pl.multiple_of((me_ref[0] ^ k) * width, width)
        ref[...] = modes_ref[:, pl.ds(start, width), :]


def z_forward_kernel(count, parts, after, me_ref, field_ref, table_ref, *refs):
    out_refs = refs[after:]
    width = field_ref.shape[2] // count
    part = width // parts
    for x, turned in enumerate(z_modes(field_ref, table_ref[0])):
        out_refs[0][x] = turned[:width]
        out_refs[1][x] = turned[width : 2 * width]
        for i, ref in enumerate(out_refs[2:]):
            start = 2 * width + i * part
            ref[x] = turned[start : start + part]


def z_in_specs(field, tables):
    _, y_cells, z_cells = field.shape
    return [
        pl.BlockSpec((x_block, y_cells, z_cells), lambda i, me: (i, 0, 0)),
        pl.BlockSpec((1,) + tables.shape[1:], lambda i, me: (me[0], 0, 0)),
    ]


def z_lead(field, me, tables, count):
    _, y_cells, z_cells = field.shape
    shape = (x_block, z_cells // count, y_cells)
    block = (lead_block,) + shape[1:]
    return pl.pallas_call(
        functools.partial(z_lead_kernel, count),
        grid=(x_block // lead_block,),
        in_specs=[
            smem,
            pl.BlockSpec((lead_block, y_cells, z_cells), lambda i: (i, 0, 0)),
            pl.BlockSpec((1,) + tables.shape[1:], lambda i: (0, 0, 0)),
        ],
        out_specs=[pl.BlockSpec(block, lambda i: (i, 0, 0))] * (count - 2),
        out_shape=[array_of(shape)] * (count - 2),
        scratch_shapes=[pltpu.VMEM((lead_block, z_cells, y_cells), f32)],
        compiler_params=params,
        cost_estimate=cost(costs["lead"]),
        name="z_lead",
    )(me, field, tables)


def z_forward(field, me, tables, count, parts, after, key, which=None, lead=0):
    size, y_cells, z_cells = field.shape
    width = z_cells // count
    part = width // parts
    rest = (count - 2) * parts
    far = size - lead * x_block
    out = pl.pallas_call(
        functools.partial(z_forward_kernel, count, parts, len(after)),
        grid_spec=pltpu.PrefetchScalarGridSpec(
            num_scalar_prefetch=1,
            grid=(size // x_block,),
            in_specs=z_in_specs(field, tables) + [anywhere] * len(after),
            out_specs=[
                pl.BlockSpec((x_block, width, y_cells), lambda i, me: (i, 0, 0)),
                near_spec((x_block, width, y_cells), which, lambda i, me: (i, 0, 0)),
            ]
            + [
                pl.BlockSpec(
                    (x_block, part, y_cells), lambda i, me: (jnp.maximum(i - lead, 0), 0, 0)
                )
            ]
            * rest,
        ),
        out_shape=parcel_shapes(
            (size, width, y_cells), (far, part, y_cells), count, parts, which is not None
        ),
        compiler_params=params,
        cost_estimate=cost(costs[key]),
        name="z_forward",
    )(me, field, tables, *after)
    return parcel_of(out, parts)


def plane_forward(block_refs, y_table, x_table):
    planes = block_refs[0].shape[1]
    value = jnp.concatenate([ref[...] for ref in block_refs], axis=0)
    x_cells, _, y_cells = value.shape
    value = jnp.swapaxes(value, 0, 1).reshape(planes * x_cells, y_cells)
    value = flip(times(value, y_table), planes)
    return times(value, x_table)


def store_faces(step, total, forced, face_table, rows_ref):
    planes = len(forced)
    for j, value in enumerate(forced):
        both = jnp.dot(
            face_table, jnp.concatenate(split(value), axis=0), preferred_element_type=f32
        )
        rows = both[:padded_rows] + both[padded_rows:]
        rows_ref[pl.ds(step * planes + j, padded_rows, stride=total), :] = rows


def send_faces(rows, x_table, face_refs):
    value = times(rows, x_table).T
    x_local = value.shape[0] // len(face_refs)
    for k, ref in enumerate(face_refs):
        ref[...] = packed(value[k * x_local : (k + 1) * x_local])


def first_kernel(count, held, last, offset, z_total, me_ref, *refs):
    blocks, refs = refs[:held], refs[held:]
    squares_ref, y_ref, x_ref, face_ref = refs[:4]
    spectral = plane_forward(blocks, y_ref[...], x_ref[...])
    if not last:
        out_ref, rows_ref = refs[-2:]
    else:
        x_back_ref, before_ref = refs[4:6]
        out_ref, face_refs, rows_ref = refs[-2 - count], refs[-1 - count : -1], refs[-1]
    planes, y_modes, x_modes = out_ref.shape
    total = rows_ref.shape[0] // padded_rows
    first = me_ref[0] * (z_total // count) + offset + pl.program_id(0) * planes
    forced = []
    for j in range(planes):
        mine = spectral[j * y_modes : (j + 1) * y_modes]
        wave, source = factors(squares_ref[...], first + j, z_total)
        out_ref[j] = wave * mine
        forced.append(source * mine)
    store_faces(pl.program_id(0), total, forced, face_ref[...], rows_ref)
    if last:

        @pl.when(pl.program_id(0) == pl.num_programs(0) - 1)
        def _():
            rows = []
            for r in range(padded_rows):
                rows += [ref[r * total : (r + 1) * total] for ref in (before_ref, rows_ref)]
            send_faces(jnp.concatenate(rows, axis=0), x_back_ref[...], face_refs)


def difference_kernel(count, *refs):
    blocks = refs[:count]
    waved_ref, y_ref, x_ref, out_ref = refs[count : count + 3] + refs[-1:]
    spectral = plane_forward(blocks, y_ref[...], x_ref[...])
    out_ref[...] = waved_ref[...] - spectral.reshape(waved_ref.shape)


def second_kernel(count, skip, z_total, me_ref, *refs):
    sums, refs = refs[:count], refs[count:]
    partial_ref, squares_ref, x_ref, x_back_ref, y_back_ref, face_ref, place_ref = refs[:7]
    refs = refs[7 + skip :]
    out_refs, face_refs = refs[: count + 1], refs[count + 1 : 2 * count + 1]
    rows_ref, terms_ref = refs[2 * count + 1 :]
    step = pl.program_id(0)
    planes = partial_ref.shape[0]
    total = rows_ref.shape[0] // padded_rows

    @pl.when(step == 0)
    def _():
        rows = [lanes_of(sums, r) for r in range(face_rows)]
        rows += [jnp.zeros_like(rows[0])] * (padded_rows - face_rows)
        terms_ref[...] = times(jnp.concatenate(rows, axis=0), x_ref[...])

    waved, forced = [], []
    for j in range(planes):
        rows = terms_ref[pl.ds(step * planes + j, padded_rows, stride=total), :]
        high = rows.astype(bf16).astype(f32)
        low = rows - high
        stack = jnp.concatenate([high, low, high, jnp.zeros_like(rows)], axis=0).astype(bf16)
        added = jnp.dot(place_ref[...], stack, preferred_element_type=f32)
        mine = partial_ref[j] + added
        wave, source = factors(squares_ref[...], me_ref[0] * total + step * planes + j, z_total)
        waved.append(wave * mine)
        forced.append(source * mine)
    store_faces(step, total, forced, face_ref[...], rows_ref)
    store_cells(waved, x_back_ref[...], y_back_ref[...], out_refs)

    @pl.when(step == pl.num_programs(0) - 1)
    def _():
        send_faces(rows_ref[...], x_back_ref[...], face_refs)


def store_cells(waved, x_table, y_table, out_refs):
    planes = len(waved)
    value = times(jnp.concatenate(waved, axis=0), x_table)
    value = times(flip(value, planes), y_table)
    value = value.reshape(planes, value.shape[0] // planes, value.shape[1])
    value = jnp.swapaxes(value, 0, 1)
    first = 0
    for ref in out_refs:
        ref[...] = value[first : first + ref.shape[0]]
        first += ref.shape[0]


def inverse_kernel(count, waved_ref, x_ref, y_ref, pair_ref, *out_refs):
    waved = [waved_ref[j] for j in range(waved_ref.shape[0])]
    store_cells(waved, x_ref[...], y_ref[...], out_refs)


def whole(shape):
    zeros = (0,) * len(shape)
    return pl.BlockSpec(shape, lambda i, *s: zeros)


def plane_specs(blocks, planes=None, first=0):
    specs = []
    for b in blocks:
        x_cells, held, y_cells = array_in(b).shape[-3:]
        start = first if held == planes else 0
        specs.append(
            block_spec(
                b, (x_cells, plane_block, y_cells), lambda i, *s, start=start: (0, start + i, 0)
            )
        )
    return specs


def mode_spec(shape, first=0):
    return pl.BlockSpec((plane_block,) + shape[1:], lambda i, *s: (first + i, 0, 0))


def first_part(blocks, place, tabs, before, after, key):
    own = blocks[-1].shape[1]
    x_local, planes, _ = blocks[0].shape
    y_modes, x_modes = tabs["squares"].shape
    small = [tabs["squares"], tabs["y"], tabs["x"], tabs["face"]]
    count = x_modes // x_local
    last = before is not None
    offset = planes - own if last else 0
    shape = (planes, y_modes, x_modes)
    operands = [place, *map(array_in, blocks), *small]
    in_specs = plane_specs(blocks, planes, offset // plane_block) + [whole(t.shape) for t in small]
    rows_shape = (padded_rows * own, x_modes)
    out_specs = [mode_spec(shape, offset // plane_block)]
    out_shape = [array_of(shape)]
    scratch, aliases = [], {}
    if last:
        waved, rows = before
        operands += [tabs["x_back"], rows, waved]
        in_specs += [whole(tabs["x_back"].shape), whole(rows.shape), anywhere]
        aliases = {len(operands) - 1: 0}
        face_shape = packed_shape(x_local, planes)
        out_specs += [whole(face_shape)] * count
        out_shape += [array_of(face_shape)] * count
        scratch = [pltpu.VMEM(rows_shape, f32)]
    else:
        out_specs += [whole(rows_shape)]
        out_shape += [array_of(rows_shape)]
    operands += after
    in_specs += [anywhere] * len(after)
    out = pl.pallas_call(
        functools.partial(first_kernel, count, len(blocks), last, offset, planes * count),
        grid_spec=pltpu.PrefetchScalarGridSpec(
            num_scalar_prefetch=0,
            grid=(own // plane_block,),
            in_specs=[smem]
            + in_specs,
            out_specs=out_specs,
            scratch_shapes=scratch,
        ),
        out_shape=out_shape,
        input_output_aliases=aliases,
        compiler_params=params,
        cost_estimate=cost(costs[key]),
        name="first_modes",
    )(*operands)
    return out[0], out[1:] if last else out[1]


def difference_part(blocks, waved, tabs, after):
    count = len(blocks)
    small = [tabs["y"], tabs["x"]]
    return pl.pallas_call(
        functools.partial(difference_kernel, count),
        grid=(waved.shape[0] // plane_block,),
        in_specs=plane_specs(blocks)
        + [mode_spec(waved.shape)]
        + [whole(t.shape) for t in small]
        + [anywhere] * len(after),
        out_specs=mode_spec(waved.shape),
        out_shape=array_of(waved.shape),
        compiler_params=params,
        cost_estimate=cost(costs["later"]),
        name="later_modes",
    )(*map(array_in, blocks), waved, *small, *after)


def second_part(sums, partial, place, tabs, after):
    count = len(sums)
    planes, y_modes, x_modes = partial.shape
    y_cells = tabs["y_back"].shape[1] // 2
    x_local = x_modes // count
    face_shape = packed_shape(x_local, planes)
    sizes = [x_local] * (count - 1) + [x_local // 2] * 2
    small = [tabs[n] for n in ("squares", "x", "x_back", "y_back", "face", "place")]
    out = pl.pallas_call(
        functools.partial(second_kernel, count, len(after), planes * count),
        grid_spec=pltpu.PrefetchScalarGridSpec(
            num_scalar_prefetch=0,
            grid=(planes // plane_block,),
            in_specs=[smem]
            + [whole(s.shape) for s in sums]
            + [mode_spec(partial.shape)]
            + [whole(t.shape) for t in small]
            + [anywhere] * len(after),
            out_specs=[
                pl.BlockSpec((n, plane_block, y_cells), lambda i, *s: (0, i, 0)) for n in sizes
            ]
            + [whole(face_shape)] * count,
            scratch_shapes=[
                pltpu.VMEM((padded_rows * planes, x_modes), f32),
                pltpu.VMEM((padded_rows * planes, x_modes), f32),
            ],
        ),
        out_shape=[array_of((n, planes, y_cells)) for n in sizes]
        + [array_of(face_shape)] * count,
        compiler_params=params,
        cost_estimate=cost(costs["second"]),
        name="second_modes",
    )(place, *sums, partial, *small, *after)
    return list(out[: count + 1]), out[count + 1 :]


def inverse_part(waved, tabs, count, key, pair):
    planes, y_modes, x_modes = waved.shape
    y_cells = tabs["y_back"].shape[1] // 2
    x_local = x_modes // count
    small = [tabs["x_back"], tabs["y_back"]]
    shape = (x_local, plane_block, y_cells)
    out = pl.pallas_call(
        functools.partial(inverse_kernel, count),
        grid=(planes // plane_block,),
        in_specs=[mode_spec(waved.shape)] + [whole(t.shape) for t in small] + [anywhere],
        out_specs=[pl.BlockSpec(shape, lambda i: (0, i, 0))]
        + [near_spec(shape, 1, lambda i: (0, i, 0))]
        + [pl.BlockSpec(shape, lambda i: (0, i, 0))] * (count - 2),
        out_shape=parcel_shapes(
            (x_local, planes, y_cells), (x_local, planes, y_cells), count, 1, True
        ),
        input_output_aliases={3: 1},
        compiler_params=params,
        cost_estimate=cost(costs[key]),
        name="modes_to_cells",
    )(waved, *small, pair)
    return list(out)


def strips_kernel(count, seg_count, scalars_ref, *refs):
    faces, table_ref, (own_ref, send_ref) = refs[:count], refs[count], refs[-2:]
    rows, x_local, z_cells = own_ref.shape
    value = jnp.concatenate([lanes_of(faces, r) for r in range(rows)], axis=0)
    value = times(value, table_ref[...]).reshape(rows, x_local, z_cells)
    own_ref[...] = value
    seg_cells = z_cells // seg_count
    groups = z_cells // seg_cells
    lane = lax.broadcasted_iota(jnp.int32, (8, z_cells), 1) // seg_cells
    for item in range(2 * seg_count):
        face, seg = item // seg_count, item % seg_count
        dest, slot, wall = scalars_ref[1, item], scalars_ref[2, item], scalars_ref[5, item]

        @pl.when(wall == 0)
        def _():
            for j in range(3):
                packed = jnp.zeros((8, z_cells), f32)
                for c in range(groups):
                    piece = value[face * 3 + j, 8 * c : 8 * (c + 1)]
                    shift = (c - seg) * seg_cells % z_cells
                    if shift:
                        piece = pltpu.roll(piece, shift, 1)
                    packed = jnp.where(lane == c, piece, packed)
                send_ref[dest, slot, j] = packed


def strips_part(faces, scalars, tables, seg_count, part_count, x_local, after, key):
    count = len(faces)
    z_cells = tables.shape[1] // 2
    own_shape = (face_rows, x_local, z_cells)
    send_shape = (part_count, pair_limit, 3, 8, z_cells)
    return pl.pallas_call(
        functools.partial(strips_kernel, count, seg_count),
        grid_spec=pltpu.PrefetchScalarGridSpec(
            num_scalar_prefetch=0,
            grid=(1,),
            in_specs=[smem]
            + [pl.BlockSpec(f.shape, lambda i: (0, 0)) for f in faces]
            + [pl.BlockSpec(tables.shape, lambda i: (0, 0))]
            + [anywhere] * len(after),
            out_specs=[
                pl.BlockSpec(own_shape, lambda i: (0, 0, 0)),
                pl.BlockSpec(send_shape, lambda i: (0, 0, 0, 0, 0)),
            ],
        ),
        out_shape=[array_of(own_shape), array_of(send_shape)],
        compiler_params=params,
        cost_estimate=cost(costs[key]),
        name="strips",
    )(scalars, *faces, tables, *after)


def coupled_terms(seg_count, scalars_ref, own_ref, got_ref):
    _, x_local, z_cells = own_ref.shape
    seg_cells = z_cells // seg_count
    groups = z_cells // seg_cells
    lane = lax.broadcasted_iota(jnp.int32, (8, z_cells), 1) // seg_cells
    row_x = scalars_ref[0, 3] + lax.broadcasted_iota(jnp.int32, (x_local, z_cells), 0)
    lane_all = lax.broadcasted_iota(jnp.int32, (x_local, z_cells), 1) // seg_cells
    terms = []
    for face in range(2):
        limit = jnp.zeros((x_local, z_cells), jnp.int32)
        other = [[jnp.zeros((8, z_cells), f32)] * groups for _ in range(3)]
        for seg in range(seg_count):
            item = face * seg_count + seg
            source, slot = scalars_ref[1, item], scalars_ref[3, item]
            limit = jnp.where(lane_all == seg, scalars_ref[4, item], limit)
            for j in range(3):
                packed = got_ref[source, slot, j]
                for c in range(groups):
                    shift = (seg - c) * seg_cells % z_cells
                    piece = pltpu.roll(packed, shift, 1) if shift else packed
                    other[j][c] = jnp.where(lane == seg, piece, other[j][c])
        other = [jnp.concatenate(o, axis=0) for o in other]
        own = [own_ref[face * 3 + j] for j in range(3)]
        low, high = (other, own) if face == 0 else (own, other)
        keep = row_x < limit
        for i in range(3):
            row = weights[3 + i] if face == 0 else weights[i]
            total = jnp.zeros((x_local, z_cells), f32)
            for j in range(6):
                if row[j] != 0:
                    total = total + float(row[j]) * (low + high)[j]
            terms.append(jnp.where(keep, total, 0.0))
    return terms


def couple_kernel(count, seg_count, skip, scalars_ref, own_ref, got_ref, table_ref, *out_refs):
    out_refs = out_refs[skip:]
    terms = coupled_terms(seg_count, scalars_ref, own_ref, got_ref)
    for r, term in enumerate(terms):
        out_refs[0][r] = term
    _, x_local, z_cells = own_ref.shape
    blank = [jnp.zeros((x_local, z_cells), f32)] * (padded_rows - len(terms))
    value = times(jnp.concatenate(terms + blank, axis=0), table_ref[...]).T
    width = z_cells // count
    for k in range(count):
        out_refs[1 + k][...] = packed(value[k * width : (k + 1) * width])


def couple_part(own, got, scalars, tables, seg_count, count, after, key):
    rows, x_local, z_cells = own.shape
    sum_shape = packed_shape(z_cells // count, x_local)
    out = pl.pallas_call(
        functools.partial(couple_kernel, count, seg_count, len(after)),
        grid_spec=pltpu.PrefetchScalarGridSpec(
            num_scalar_prefetch=0,
            grid=(1,),
            in_specs=[smem]
            + [
                pl.BlockSpec(own.shape, lambda i: (0, 0, 0)),
                pl.BlockSpec(got.shape, lambda i: (0, 0, 0, 0, 0)),
                pl.BlockSpec(tables.shape, lambda i: (0, 0)),
            ]
            + [anywhere] * len(after),
            out_specs=[pl.BlockSpec(own.shape, lambda i: (0, 0, 0))]
            + [pl.BlockSpec(sum_shape, lambda i: (0, 0))] * count,
        ),
        out_shape=[array_of(own.shape)] + [array_of(sum_shape)] * count,
        compiler_params=params,
        cost_estimate=cost(costs[key]),
        name="couple",
    )(scalars, own, got, tables, *after)
    return out[0], out[1:]


def z_inverse_kernel(count, seg_count, offset, scalars_ref, *refs):
    blocks, (earlier_ref, table_ref) = refs[:count], refs[count : count + 2]
    block, y_cells, z_cells = earlier_ref.shape
    len_x, len_y = scalars_ref[0, 1], scalars_ref[0, 2]
    step = offset + pl.program_id(0)
    if seg_count:
        own_ref, got_ref = refs[count + 2 : count + 4]
        out_ref, terms_ref = refs[-2:]

        @pl.when(pl.program_id(0) == 0)
        def _():
            for r, term in enumerate(coupled_terms(seg_count, scalars_ref, own_ref, got_ref)):
                terms_ref[r] = term

    else:
        terms_ref, out_ref = refs[count + 2], refs[-1]
    first = scalars_ref[0, 3] + step * block
    row = lax.broadcasted_iota(jnp.int32, (y_cells, z_cells), 0)
    pieces = []
    for x in range(block):
        modes = jnp.concatenate([ref[x] for ref in blocks], axis=0)
        pieces.append(modes.T)
    value = times(jnp.concatenate(pieces, axis=0), table_ref[...])
    for x in range(block):
        limit = jnp.where(first + x < len_x, len_y, 0)
        out_ref[x] = value[x * y_cells : (x + 1) * y_cells] - jnp.where(
            row < limit, earlier_ref[x], 0.0
        )
    start = pl.multiple_of(jnp.minimum((len_y - 3) // 8 * 8, y_cells - 16), 8)
    mine = pl.ds(pl.multiple_of(step * block, block), block)
    terms = [terms_ref[r, mine][:, None, :] for r in range(face_rows)]
    low_row = lax.broadcasted_iota(jnp.int32, (block, 8, z_cells), 1)
    high_row = start + lax.broadcasted_iota(jnp.int32, (block, 16, z_cells), 1)
    low = out_ref[:, 0:8, :]
    for r in range(3):
        low = low + jnp.where(low_row == r, terms[r], 0.0)
    out_ref[:, 0:8, :] = low
    high = out_ref[:, pl.ds(start, 16), :]
    for r in range(3):
        high = high + jnp.where(high_row == len_y - 3 + r, terms[3 + r], 0.0)
    out_ref[:, pl.ds(start, 16), :] = high


def z_inverse(
    blocks, earlier, terms, scalars, tables, seg_count, key, after=(), first=0, filled=None
):
    count = len(blocks)
    x_local, y_cells, z_cells = earlier.shape
    width = z_cells // count
    start = first // x_block
    given = len(terms) == 1
    operands = [scalars, *map(array_in, blocks), earlier, tables, *terms, *after]
    aliases = {}
    if filled is not None:
        aliases = {len(operands): 0}
        operands.append(filled)
    terms_shape = (face_rows, x_local, z_cells)

    def rows_from(begin):
        return lambda i: (begin + i, 0, 0)

    out = pl.pallas_call(
        functools.partial(z_inverse_kernel, count, 0 if given else seg_count, start),
        grid_spec=pl.GridSpec(
            grid=(array_in(blocks[-1]).shape[-3] // x_block,),
            in_specs=[smem]
            + [
                block_spec(
                    b,
                    (x_block, width, y_cells),
                    rows_from(start if array_in(b).shape[-3] == x_local else 0),
                )
                for b in blocks
            ]
            + [pl.BlockSpec((x_block, y_cells, z_cells), rows_from(start))]
            + [whole(t.shape) for t in (tables, *terms)]
            + [anywhere] * (len(after) + len(aliases)),
            out_specs=[pl.BlockSpec((x_block, y_cells, z_cells), rows_from(start))]
            + ([] if given else [whole(terms_shape)]),
        ),
        out_shape=[array_of(earlier.shape)] + ([] if given else [array_of(terms_shape)]),
        input_output_aliases=aliases,
        compiler_params=params,
        cost_estimate=cost(costs[key]),
        name="z_inverse",
    )(*operands)
    return out[0] if given else out


def gate_kernel(*refs):
    pass


def gated(array, after):
    return pl.pallas_call(
        gate_kernel,
        in_specs=[anywhere] * (1 + len(after)),
        out_specs=anywhere,
        out_shape=array_of(array.shape),
        input_output_aliases={0: 0},
        compiler_params=params,
        cost_estimate=cost(costs["gate"]),
        name="gate",
    )(array, *after)


def pairs_at(count, distance):
    return [(i, i ^ distance) for i in range(count)]


def send(block, distance):
    count = lax.axis_size("sub")
    return lax.ppermute(block, "sub", pairs_at(count, distance))


def exchange(blocks):
    return [blocks[0]] + [send(blocks[k], k) for k in range(1, len(blocks))]


def local(adj_next, adj_later, box_sizes, holder, partner):
    part_count = holder.shape[0]
    seg_count = partner.shape[2]
    my_group = lax.axis_index("grp").astype(jnp.int32)
    me = lax.axis_index("sub").astype(jnp.int32)
    count = lax.axis_size("sub")
    _, x_local, y_cells, z_cells = adj_next.shape
    x_total = x_local * count
    z_local = z_cells // count
    z_fwd, z_inv = (jnp.asarray(t) for t in z_tables(z_cells, count))
    place = me.reshape(1)

    middle = count // 2
    lead = z_lead(adj_next[0], place, z_fwd, count)
    parcel = z_forward(adj_next[0], place, z_fwd, count, 2, [lead[0]], "forward_next", lead=1)
    lead = [send(b, k) for k, b in enumerate(lead, 2)]
    first_a, first_b = [parcel[0], send(parcel[1], 1)], [parcel[0]]
    first_b.append(first_a[1])
    for c, blocks in enumerate((first_a, first_b)):
        for k in range(2, count):
            blocks += [lead[k - 2], send(parcel[k][c], k)]

    ids = jnp.stack([me, my_group, jnp.int32(x_local)])
    scalars, tabs = make_tables(
        ids,
        box_sizes,
        holder,
        partner,
        (y_cells, x_total),
        z_fwd,
        z_inv,
        [parcel[0]],
    )
    later = z_forward(
        adj_later[0], place, z_fwd, count, 1, [tabs["squares"]], "forward_later", 0
    )
    pair = later[1]
    later = [later[0], None] + [b[0] for b in later[2:]]
    for k in range(2, middle + 1):
        later[k] = send(later[k], k)

    before = first_part(first_a, place, tabs, None, [later[0]], "first_a")
    waved, faces = first_part(first_b, place, tabs, before, [], "first_b")
    faces = exchange(faces)
    for k in range(middle + 1, count):
        later[k] = send(gated(later[k], [faces[1]]), k)
    back = inverse_part(waved, tabs, count, "back", pair)
    near = send(back[1], 1)
    later[1] = (near, 0)
    back[1] = (near, 1)
    own, outgoing = strips_part(
        faces,
        scalars,
        tabs["z_back"],
        seg_count,
        part_count,
        x_local,
        [back[0], *later[2 : middle + 1]],
        "strips_now",
    )
    for k in range(2, count):
        back[k] = send(gated(back[k], [outgoing]), k)
    got = lax.all_to_all(outgoing, "grp", 0, 0, tiled=True)
    partial = difference_part(later, waved, tabs, [outgoing])
    terms_now, sums = couple_part(
        own,
        got,
        scalars,
        tabs["z"],
        seg_count,
        count,
        [partial],
        "couple_now",
    )
    last, faces = second_part(
        exchange(sums), partial, place, tabs, back[2 : middle + 1]
    )
    faces = exchange(faces)
    near = last[1]
    last[2:] = [send(b, min(k, count - 1)) for k, b in enumerate(last[2:], 2)]
    own, outgoing = strips_part(
        faces,
        scalars,
        tabs["z_back"],
        seg_count,
        part_count,
        x_local,
        [last[0], back[-1]],
        "strips_earlier",
    )
    last[1] = send(gated(near, [outgoing]), 1)
    got = lax.all_to_all(outgoing, "grp", 0, 0, tiled=True)
    adj_now = z_inverse(
        back,
        adj_later[0],
        [terms_now],
        scalars,
        tabs["z_back"],
        seg_count,
        "now",
        last[2 : middle + 1],
    )
    common = (scalars, tabs["z_back"], seg_count)
    adj_earlier, terms = z_inverse(
        last[:-1], adj_next[0], [own, got], *common, "end_a", [adj_now]
    )
    adj_earlier = z_inverse(
        last[:-2] + last[-1:],
        adj_next[0],
        [terms],
        *common,
        "end_b",
        [],
        x_local // 2,
        adj_earlier,
    )
    return (adj_now[None], adj_earlier[None])


def solution(mesh):
    return jax.shard_map(
        local,
        mesh=mesh,
        in_specs=(P("grp", "sub", None, None), P("grp", "sub", None, None), P(), P(), P()),
        out_specs=(P("grp", "sub", None, None), P("grp", "sub", None, None)),
        check_vma=False,
    )
```
